32 devices in a mesh: dp: 16 (over z, y, core), tensor: 2 (over x).
Axes of the slice: x: 2, y: 2, z: 4, core: 2. Of those that a mesh axis runs over, the one named last changes fastest.
Arguments:
- context: bfloat16 [16384, 4096], P(('dp', 'tensor')), may hold values from -6 to 6
- latents: bfloat16 [4096, 4096], P('dp'), may hold values from -6 to 6
- lengths: int32 [16, 4], P('dp'), may hold values from 1 to 768, 1024 in all within a row
- ctx_gain: float32 [4096], replicated, may hold values from 0.25 to 1.75
- lat_gain: float32 [4096], replicated, may hold values from 0.25 to 1.75
- q_weight: bfloat16 [4096, 4096], P('dp', 'tensor'), may hold values from -0.09375 to 0.09375
- key_value_weight: bfloat16 [4096, 1024], P('dp'), may hold values from -0.09375 to 0.09375
- out_weight: bfloat16 [4096, 4096], P('dp', 'tensor'), may hold values from -0.75 to 0.75
- out_grad: bfloat16 [4096, 4096], P(('dp', 'tensor')), may hold values from -6 to 6
Outputs:
- resampled: bfloat16 [4096, 4096], P(('dp', 'tensor'))
- context_grad: float32 [16384, 4096], P(('dp', 'tensor'))
- latents_grad: float32 [4096, 4096], P(('dp', 'tensor'))
- ctx_gain_grad: float32 [4096], P(('dp', 'tensor'))
- lat_gain_grad: float32 [4096], P(('dp', 'tensor'))
- q_weight_grad: float32 [4096, 4096], P('dp', 'tensor')
- kv_weight_grad: float32 [4096, 1024], P(('dp', 'tensor'))
- out_weight_grad: float32 [4096, 4096], P('dp', 'tensor')
The draws below stay inside these ranges and needn't reach their ends.
Inputs may be any that keep to these rules, and one draw needn't show every extreme that they name: Each row holds 4 positive lengths that sum to 1024; the longest of each row is exactly 768.
All inputs are finite; a program needn't handle non-finite values.
Results may differ from the reference program's by a relative error of at most 0.011.
Values may be sent and summed in bfloat16 or wider, within the bound.
No kernel may reach another device: no remote copies, remote signals or barrier semaphores. Data moves between devices by JAX's collectives and lax.ppermute only.
A program may use at most 320 MiB of HBM per device.

```python
import math
from functools import partial
import jax
import jax.numpy as jnp
import numpy as np
from jax import lax

MODEL_WIDTH = 4096
QUERY_HEADS = 32
KEY_VALUE_HEADS = 4
HEAD_SIZE = 128
LAT = 64
IMG_GRP = 4
GRP_TOK = 1024
MOST_LEN = 768
PATCHES = 16384
LAT_ROWS = 4096
N_DP = 16
N_TENSOR = 2


def with_spikes(values, rng, source, target, blocks, factor):
    owner, partner = [(jnp.arange(values.shape[dim]) // (values.shape[dim] // blocks)).reshape([-1 if axis == dim else 1 for axis in range(values.ndim)]) for dim in (source, target)]
    chosen = jax.random.permutation(rng, blocks)[partner]
    strong = (owner == chosen) | (owner == (partner + blocks // 2) % blocks)
    return jnp.where(strong, factor * values, values)


def level_of(key, shape, cuts, smallest, largest):
    def one(axis_at, shards_of):
        steps = jax.random.uniform(jax.random.fold_in(jax.random.fold_in(key, 6), axis_at), (shards_of,), jnp.float32, smallest / len(cuts), largest / len(cuts))
        return jnp.repeat(jnp.exp(steps), shape[axis_at] // shards_of).reshape((-1,) + (1,) * (len(shape) - axis_at - 1))

    loudness = one(*cuts[0])
    for cut in cuts[1:]:
        loudness = loudness * one(*cut)
    return loudness


def profile(number_of, total, most, skew):
    loads = [(1 << 20) // math.isqrt(grade ** skew) + 1 for grade in range(2, number_of + 1)]
    surplus, given = total - most - (number_of - 1), [1] * (number_of - 1)
    while surplus > 0:
        candidates = [i for i in range(number_of - 1) if given[i] < most]
        mass, remaining = sum([loads[i] for i in candidates]), surplus
        for i in candidates:
            addition = min(most - given[i], max(1, remaining * loads[i] // mass), surplus)
            given[i] = given[i] + addition
            surplus = surplus - addition
    return np.array([most] + given)


def ragged_sizes(own_key, count, total, bound, slope):
    if count == 2:
        one = jax.random.randint(own_key, (), max(1, total - bound), min(bound, total - 1) + 1)
        return jnp.stack([one, total - one])
    sizes = jnp.asarray(profile(count, total, bound, slope), jnp.int32)
    pairs = (count - 1) // 2
    donor, sink = sizes[1:1 + 2 * pairs:2], sizes[2:2 + 2 * pairs:2]
    margin = jnp.minimum(donor - 1, bound - sink)
    shifted = jax.random.randint(jax.random.fold_in(own_key, 1), (pairs,), 0, 1 << 20) % (margin + 1)
    sizes = sizes.at[1:1 + 2 * pairs:2].set(donor - shifted).at[2:2 + 2 * pairs:2].set(sink + shifted)
    return sizes[jax.random.permutation(jax.random.fold_in(own_key, 2), count)]


def normal_values(rng, shape, deviation, limit, cuts=(), held_as=jnp.bfloat16):
    array = jax.random.normal(rng, shape, jnp.float32) * deviation
    if len(cuts) > 0:
        array = level_of(rng, shape, cuts, -0.22, 0.18) * array
    return jnp.clip(array, min=-limit, max=limit).astype(held_as)


def bell_draw_with(own_key, shape, scale, most, cuts, heavy, held_as=jnp.bfloat16):
    array = scale * jax.random.normal(own_key, shape, jnp.float32)
    if cuts:
        array = array * level_of(own_key, shape, cuts, -0.22, 0.18)
    return jnp.clip(with_spikes(array, jax.random.fold_in(own_key, 3), *heavy), -most, most).astype(held_as)


def setup_inputs(seed: int = 0) -> dict:
    keys = jax.random.split(jax.random.key(seed), 10)
    return {
        "context": bell_draw_with(keys[0], (PATCHES, MODEL_WIDTH), 1.0, 6.0, ((0, 32),), (0, 1, 32, 2.75)),
        "latents": bell_draw_with(keys[1], (LAT_ROWS, MODEL_WIDTH), 1.0, 6.0, ((0, 16),), (0, 1, 16, 2.0)),
        "lengths": jax.vmap(lambda own: ragged_sizes(own, IMG_GRP, GRP_TOK, MOST_LEN, 2))(jax.random.split(keys[2], N_DP)).reshape((N_DP, IMG_GRP)).astype(jnp.int32),
        "ctx_gain": jnp.clip(1.0 + 0.15 * jax.random.normal(keys[3], (MODEL_WIDTH,), jnp.float32), 0.25, 1.75),
        "lat_gain": jnp.clip(1.0 + 0.15 * jax.random.normal(keys[4], (MODEL_WIDTH,), jnp.float32), 0.25, 1.75),
        "q_weight": normal_values(keys[5], (MODEL_WIDTH, QUERY_HEADS * HEAD_SIZE), MODEL_WIDTH ** -0.5, 0.09375, ((0, 16), (1, 2))),
        "key_value_weight": normal_values(keys[6], (MODEL_WIDTH, 2 * KEY_VALUE_HEADS * HEAD_SIZE), MODEL_WIDTH ** -0.5, 0.09375, ((0, 16),)),
        "out_weight": normal_values(keys[7], (MODEL_WIDTH, QUERY_HEADS * HEAD_SIZE), (max(QUERY_HEADS * HEAD_SIZE // 64, 1)) ** -0.5, 0.75, ((0, 16), (1, 2))),
        "out_grad": normal_values(keys[8], (LAT_ROWS, MODEL_WIDTH), 1.0, 6.0, ((0, 32),)),
    }


norm_eps = 1e-06
highest = lax.Precision.HIGHEST

@jax.custom_vjp
def low(v):
    return lax.optimization_barrier(v.astype(jnp.bfloat16)).astype(jnp.float32)

@jax.custom_vjp
def low_back(v):
    return v

def low_keep(v):
    return (low(v), None)

def low_pass(kept, grad):
    return (grad,)

def back_keep(v):
    return (v, None)

def back_low(kept, grad):
    return (low(grad),)
low.defvjp(low_keep, low_pass)
low_back.defvjp(back_keep, back_low)

def rms_norm(values, gain):
    scale_rows = lax.rsqrt(lax.optimization_barrier(jnp.mean(values * values, axis=-1, keepdims=True)) + norm_eps)
    return values * scale_rows * gain

def group_attention(pieces):
    query_rows, kv_patch, kv_latent, group_lengths = pieces
    count_of_rows = query_rows.shape[0]
    patch_count = kv_patch.shape[0]
    joined_heads = jnp.concatenate([kv_patch, kv_latent], axis=0)
    total_sum = joined_heads.shape[0]
    joined_heads = joined_heads.reshape(total_sum, N_TENSOR, 2, KEY_VALUE_HEADS // N_TENSOR, HEAD_SIZE)
    key_matrix_rows = joined_heads[:, :, 0].reshape(total_sum, KEY_VALUE_HEADS, HEAD_SIZE)
    value_matrix_rows = joined_heads[:, :, 1].reshape(total_sum, KEY_VALUE_HEADS, HEAD_SIZE)
    heads_of_query = query_rows.reshape(count_of_rows, KEY_VALUE_HEADS, QUERY_HEADS // KEY_VALUE_HEADS, HEAD_SIZE)
    scores = low_back(jnp.einsum('rkgd,nkd->kgrn', heads_of_query, key_matrix_rows, precision=highest))
    ends = jnp.cumsum(group_lengths).astype(jnp.int32)
    positions = jnp.arange(patch_count).astype(jnp.int32)
    patch_ids = lax.optimization_barrier(jnp.sum((positions[:, None] >= ends[None, :]).astype(jnp.int32), axis=1)).astype(jnp.int32)
    latent_ids = (jnp.arange(count_of_rows) // LAT).astype(jnp.int32)
    key_ids = jnp.concatenate([patch_ids, latent_ids])
    allowed = latent_ids[:, None] == key_ids[None, :]
    masked = jnp.where(allowed, scores * HEAD_SIZE ** (-0.5), -1e+30)
    soft = low(jax.nn.softmax(masked, axis=-1))
    mixed = jnp.einsum('kgrn,nkd->rkgd', soft, value_matrix_rows, precision=highest)
    return low_back(low(mixed.reshape(count_of_rows, QUERY_HEADS * HEAD_SIZE)))

def forward(context, latents, ctx_gain, lat_gain, q_weight, key_value_weight, out_weight, lengths):
    ctx_n = low(rms_norm(context, ctx_gain))
    lat_n = low(rms_norm(latents, lat_gain))
    query_rows = low_back(low(jnp.dot(lat_n, q_weight, precision=highest)))
    kv_patch = low_back(low(jnp.dot(ctx_n, key_value_weight, precision=highest)))
    kv_latent = low_back(low(jnp.dot(lat_n, key_value_weight, precision=highest)))
    groups = lengths.shape[0]
    width = key_value_weight.shape[1]
    mixed = lax.map(jax.checkpoint(group_attention), (query_rows.reshape(groups, -1, QUERY_HEADS * HEAD_SIZE), kv_patch.reshape(groups, -1, width), kv_latent.reshape(groups, -1, width), lengths))
    mixed = mixed.reshape(latents.shape[0], QUERY_HEADS * HEAD_SIZE)
    branch = low_back(jnp.dot(mixed, out_weight.T, precision=highest))
    return latents + branch

def reference(context, latents, lengths, ctx_gain, lat_gain, q_weight, key_value_weight, out_weight, out_grad):
    inputs = (context.astype(jnp.float32), latents.astype(jnp.float32), ctx_gain.astype(jnp.float32), lat_gain.astype(jnp.float32), q_weight.astype(jnp.float32), key_value_weight.astype(jnp.float32), out_weight.astype(jnp.float32))
    result, pullback = jax.vjp(partial(forward, lengths=lengths), *inputs)
    grads = pullback(out_grad.astype(jnp.float32))
    return (result.astype(jnp.bfloat16), grads[0], grads[1], grads[2], grads[3], grads[4], grads[5], grads[6])
```

```python
import math

import jax
import jax.numpy as jnp
from jax import lax
from jax.experimental import pallas as pl
from jax.experimental.pallas import tpu as pltpu
from jax.sharding import PartitionSpec as P

QUERY_HEADS = 32
KEY_VALUE_HEADS = 4
HEAD_SIZE = 128
LAT = 64
IMG_GRP = 4
GROUPED = QUERY_HEADS // KEY_VALUE_HEADS

norm_eps = 1e-06
scale = HEAD_SIZE ** (-0.5)
scale_log2 = scale * math.log2(math.e)
low = jnp.bfloat16
full = jnp.float32
CHUNK = 256
HINT = 1000
VMEM_BYTES = 48 * 1024 * 1024


def dot_nt(a, b):
    return lax.dot_general(a, b, (((1,), (1,)), ((), ())), preferred_element_type=full)


def dot_nn(a, b):
    return lax.dot_general(a, b, (((1,), (0,)), ((), ())), preferred_element_type=full)


def stack_heads(wide):
    return jnp.concatenate(
        [wide[:, h * HEAD_SIZE : (h + 1) * HEAD_SIZE] for h in range(GROUPED)], axis=0
    )


def spread_heads(tall):
    return jnp.concatenate([tall[h * LAT : (h + 1) * LAT] for h in range(GROUPED)], axis=1)


def fwd_kernel(bounds, q_ref, kvp_ref, kvl_ref, o_ref, lse_ref, s_scr, m_scr, l_scr, acc_scr):
    image = pl.program_id(0) * IMG_GRP + pl.program_id(1)
    lo = bounds[0, image]
    hi = bounds[1, image]
    chunks = kvp_ref.shape[1] // CHUNK
    qs = stack_heads(q_ref[...])
    s_lat = dot_nt(kvl_ref[:, :HEAD_SIZE], qs) * scale_log2
    m_scr[...] = jnp.max(s_lat, axis=0, keepdims=True)
    for j in range(chunks):

        @pl.when((lo < (j + 1) * CHUNK) & (hi > j * CHUNK))
        def _():
            keys = kvp_ref[0, j * CHUNK : (j + 1) * CHUNK, :HEAD_SIZE]
            s = dot_nt(keys, qs) * scale_log2
            at = lax.broadcasted_iota(jnp.int32, s.shape, 0) + j * CHUNK
            s = jnp.where((at >= lo) & (at < hi), s, -1e30)
            s_scr[j * CHUNK : (j + 1) * CHUNK, :] = s
            m_scr[...] = jnp.maximum(m_scr[...], jnp.max(s, axis=0, keepdims=True))

    top = m_scr[...]
    p = jnp.exp2(s_lat - top)
    l_scr[...] = jnp.sum(p, axis=0, keepdims=True)
    acc_scr[...] = dot_nn(kvl_ref[:, HEAD_SIZE:].T, p.astype(low))
    for j in range(chunks):

        @pl.when((lo < (j + 1) * CHUNK) & (hi > j * CHUNK))
        def _():
            values = kvp_ref[0, j * CHUNK : (j + 1) * CHUNK, HEAD_SIZE:]
            p = jnp.exp2(s_scr[j * CHUNK : (j + 1) * CHUNK, :] - top)
            l_scr[...] += jnp.sum(p, axis=0, keepdims=True)
            acc_scr[...] += dot_nn(values.T, p.astype(low))

    total = l_scr[...]
    lse_ref[0] = top + jnp.log2(total)
    o_ref[...] = spread_heads((acc_scr[...] / total).T).astype(low)


def bwd_kernel(
    bounds, q_ref, do_ref, kvp_ref, kvl_ref, lse_ref,
    dq_ref, dkvp_ref, dkvl_ref,
    p_scr, dp_scr, dkv_scr, dl_scr, dq_scr,
):
    i = pl.program_id(1)
    image = pl.program_id(0) * IMG_GRP + i
    lo = bounds[0, image]
    hi = bounds[1, image]
    chunks = kvp_ref.shape[1] // CHUNK
    qs = stack_heads(q_ref[...])
    dos = stack_heads(do_ref[...])
    lse = lse_ref[0]

    @pl.when(i == 0)
    def _():
        dkv_scr[...] = jnp.zeros_like(dkv_scr)

    k_lat = kvl_ref[:, :HEAD_SIZE]
    p_lat = jnp.exp2(dot_nt(k_lat, qs) * scale_log2 - lse)
    dp_lat = dot_nt(kvl_ref[:, HEAD_SIZE:], dos)
    dl_scr[...] = jnp.sum(p_lat * dp_lat, axis=0, keepdims=True)
    for j in range(chunks):

        @pl.when((lo < (j + 1) * CHUNK) & (hi > j * CHUNK))
        def _():
            rows = slice(j * CHUNK, (j + 1) * CHUNK)
            s = dot_nt(kvp_ref[0, rows, :HEAD_SIZE], qs) * scale_log2
            at = lax.broadcasted_iota(jnp.int32, s.shape, 0) + j * CHUNK
            s = jnp.where((at >= lo) & (at < hi), s - lse, -1e30)
            p = jnp.exp2(s)
            dp = dot_nt(kvp_ref[0, rows, HEAD_SIZE:], dos)
            dl_scr[...] += jnp.sum(p * dp, axis=0, keepdims=True)
            p_scr[rows, :] = p
            dp_scr[rows, :] = dp

    delta = dl_scr[...]
    ds_lat = (p_lat * (dp_lat - delta) * scale).astype(low)
    dq_scr[...] = dot_nn(k_lat.T, ds_lat)
    dkvl_ref[:, :HEAD_SIZE] = dot_nn(ds_lat, qs).astype(low)
    dkvl_ref[:, HEAD_SIZE:] = dot_nn(p_lat.astype(low), dos).astype(low)
    for j in range(chunks):

        @pl.when((lo < (j + 1) * CHUNK) & (hi > j * CHUNK))
        def _():
            rows = slice(j * CHUNK, (j + 1) * CHUNK)
            p = p_scr[rows, :]
            ds = (p * (dp_scr[rows, :] - delta) * scale).astype(low)
            dq_scr[...] += dot_nn(kvp_ref[0, rows, :HEAD_SIZE].T, ds)
            dkv_scr[rows, :HEAD_SIZE] += dot_nn(ds, qs)
            dkv_scr[rows, HEAD_SIZE:] += dot_nn(p.astype(low), dos)

    dq_ref[...] = spread_heads(dq_scr[...].T).astype(low)

    @pl.when(i == IMG_GRP - 1)
    def _():
        dkvp_ref[0] = dkv_scr[...].astype(low)


def attention_specs(groups, patches, heads_width):
    rows = pl.BlockSpec((LAT, heads_width), lambda g, i, b: (g * IMG_GRP + i, 0))
    kvp = pl.BlockSpec((1, patches, 2 * HEAD_SIZE), lambda g, i, b: (g, 0, 0))
    kvl = pl.BlockSpec((LAT, 2 * HEAD_SIZE), lambda g, i, b: (g * IMG_GRP + i, 0))
    lse = pl.BlockSpec((1, 1, GROUPED * LAT), lambda g, i, b: (g * IMG_GRP + i, 0, 0))
    return rows, kvp, kvl, lse


def attend(bounds, q, kvp, kvl):
    groups, patches, _ = kvp.shape
    rows, kvp_spec, kvl_spec, lse_spec = attention_specs(groups, patches, q.shape[1])
    wide = GROUPED * LAT
    return pl.pallas_call(
        fwd_kernel,
        grid_spec=pltpu.PrefetchScalarGridSpec(
            num_scalar_prefetch=1,
            grid=(groups, IMG_GRP),
            in_specs=[rows, kvp_spec, kvl_spec],
            out_specs=[rows, lse_spec],
            scratch_shapes=[
                pltpu.VMEM((patches, wide), full),
                pltpu.VMEM((1, wide), full),
                pltpu.VMEM((1, wide), full),
                pltpu.VMEM((HEAD_SIZE, wide), full),
            ],
        ),
        out_shape=[
            jax.ShapeDtypeStruct(q.shape, low),
            jax.ShapeDtypeStruct((groups * IMG_GRP, 1, wide), full),
        ],
        compiler_params=pltpu.CompilerParams(vmem_limit_bytes=VMEM_BYTES),
        cost_estimate=pl.CostEstimate(
            flops=2 * 2 * groups * IMG_GRP * wide * patches * HEAD_SIZE // HINT,
            bytes_accessed=(4 * q.size + 2 * kvp.size) // HINT,
            transcendentals=groups * IMG_GRP * wide * patches // HINT,
        ),
        name="attention_forward",
    )(bounds, q, kvp, kvl)


def attend_back(bounds, q, d_out, kvp, kvl, lse):
    groups, patches, _ = kvp.shape
    rows, kvp_spec, kvl_spec, lse_spec = attention_specs(groups, patches, q.shape[1])
    wide = GROUPED * LAT
    return pl.pallas_call(
        bwd_kernel,
        grid_spec=pltpu.PrefetchScalarGridSpec(
            num_scalar_prefetch=1,
            grid=(groups, IMG_GRP),
            in_specs=[rows, rows, kvp_spec, kvl_spec, lse_spec],
            out_specs=[rows, kvp_spec, kvl_spec],
            scratch_shapes=[
                pltpu.VMEM((patches, wide), full),
                pltpu.VMEM((patches, wide), full),
                pltpu.VMEM((patches, 2 * HEAD_SIZE), full),
                pltpu.VMEM((1, wide), full),
                pltpu.VMEM((HEAD_SIZE, wide), full),
            ],
        ),
        out_shape=[
            jax.ShapeDtypeStruct(q.shape, low),
            jax.ShapeDtypeStruct(kvp.shape, low),
            jax.ShapeDtypeStruct(kvl.shape, low),
        ],
        compiler_params=pltpu.CompilerParams(vmem_limit_bytes=VMEM_BYTES),
        cost_estimate=pl.CostEstimate(
            flops=2 * 5 * groups * IMG_GRP * wide * patches * HEAD_SIZE // HINT,
            bytes_accessed=(6 * q.size + 4 * kvp.size) // HINT,
            transcendentals=groups * IMG_GRP * wide * patches // HINT,
        ),
        name="attention_backward",
    )(bounds, q, d_out, kvp, kvl, lse)


def dot_tn(a, b):
    return lax.dot_general(a, b, (((0,), (0,)), ((), ())), preferred_element_type=full)


def call(kernel, name, scalars, arrays, in_specs, out_specs, out_shape, scratch, grid, flops):
    moved = sum(a.size * a.dtype.itemsize for a in arrays)
    moved += sum(o.size * o.dtype.itemsize for o in out_shape)
    return pl.pallas_call(
        kernel,
        grid_spec=pltpu.PrefetchScalarGridSpec(
            num_scalar_prefetch=len(scalars),
            grid=grid,
            in_specs=in_specs,
            out_specs=out_specs,
            scratch_shapes=scratch,
        ),
        out_shape=out_shape,
        compiler_params=pltpu.CompilerParams(vmem_limit_bytes=VMEM_BYTES),
        cost_estimate=pl.CostEstimate(flops=flops // HINT, bytes_accessed=moved // HINT, transcendentals=0),
        name=name,
    )(*scalars, *arrays)


def whole(shape):
    return pl.BlockSpec(shape, lambda *_: (0,) * len(shape))


def fetch(offsets, pieces, held, sems):
    total = sum(piece.shape[0] for piece in pieces)
    rows = held.shape[0] // offsets.shape[0]
    assert total == held.shape[0]
    copies = []
    for piece in pieces:
        for first in range(0, piece.shape[0], rows):
            n = len(copies)
            at = pl.multiple_of(offsets[n], rows)
            copies.append(
                pltpu.make_async_copy(
                    piece.at[pl.ds(first, rows)], held.at[pl.ds(at, rows)], sems.at[n]
                )
            )
    for copy in copies:
        copy.start()
    for copy in copies:
        copy.wait()


def rows_kernel(count, offsets, act, *refs):
    pieces, (out, held, sems) = refs[:count], refs[count:]
    fetch(offsets, pieces, held, sems)
    step = 256
    for n in range(0, out.shape[1], step):
        out[:, n : n + step] = dot_nn(act[...], held[:, n : n + step]).astype(out.dtype)


def rows_times_weight(act, weight):
    offsets, pieces = weight
    cols = pieces[0].shape[1]
    rows, features = act.shape
    return call(
        lambda *refs: rows_kernel(len(pieces), *refs),
        "rows_times_weight",
        [offsets],
        [act, *pieces],
        [whole(act.shape)] + [pl.BlockSpec(memory_space=pltpu.HBM)] * len(pieces),
        [whole((rows, cols))],
        [jax.ShapeDtypeStruct((rows, cols), low)],
        [pltpu.VMEM((features, cols), low), pltpu.SemaphoreType.DMA((offsets.shape[0],))],
        (1,),
        2 * rows * features * cols,
    )[0]


def rows_times_kv(act, weight):
    offsets, pieces = weight
    rows, features = act.shape
    cols = pieces[0].shape[1]
    count = len(pieces)

    def kernel(offsets_ref, act_ref, *refs):
        out, held, sems = refs[count:]
        fetch(offsets_ref, refs[:count], held, sems)
        step = 256
        for n in range(0, cols, step):
            out[:, n : n + step] = dot_nn(act_ref[...], held[:, n : n + step]).astype(low)

    return call(
        kernel,
        "rows_times_kv",
        [offsets],
        [act, *pieces],
        [whole(act.shape)] + [pl.BlockSpec(memory_space=pltpu.HBM)] * count,
        [whole((rows, cols)), whole((features, cols))],
        [jax.ShapeDtypeStruct((rows, cols), low), jax.ShapeDtypeStruct((features, cols), low)],
        [pltpu.SemaphoreType.DMA((offsets.shape[0],))],
        (1,),
        2 * rows * features * cols,
    )


def keep_and_send(x, outs, n, step, value):
    a_keep, a_sent, b_keep, b_sent = outs
    quarter = value.shape[0] // 4
    parts = [value[k * quarter : (k + 1) * quarter] for k in range(4)]
    half = a_keep.shape[2]
    if n < half:
        for k in range(2):
            a_keep[k, :, n : n + step] = parts[k]
            a_sent[k, :, n : n + step] = parts[2 + k]
    else:
        span = slice(n - half, n - half + step)
        for g in range(2):
            b_keep[g, :, span] = jnp.where(x == 0, parts[2 * g], parts[2 * g + 1])
            b_sent[g, :, span] = jnp.where(x == 0, parts[2 * g + 1], parts[2 * g])


def heads_kernel(count, offsets, place, act, *refs):
    pieces, outs, (held, sems) = refs[:count], refs[count:-2], refs[-2:]
    fetch(offsets, pieces, held, sems)
    step = 512
    for n in range(0, held.shape[0], step):
        value = dot_nt(act[...], held[n : n + step]).astype(low)
        keep_and_send(place[0], outs, n, step, value)


def heads_times_weight(place, act, weight):
    offsets, pieces = weight
    rows, cols = act.shape
    features = sum(piece.shape[0] for piece in pieces)
    half = (2, rows // 4, features // 2)
    return call(
        lambda *refs: heads_kernel(len(pieces), *refs),
        "heads_times_weight",
        [offsets, place],
        [act, *pieces],
        [whole(act.shape)] + [pl.BlockSpec(memory_space=pltpu.HBM)] * len(pieces),
        [whole(half)] * 4,
        [jax.ShapeDtypeStruct(half, low)] * 4,
        [pltpu.VMEM((features, cols), low), pltpu.SemaphoreType.DMA((offsets.shape[0],))],
        (1,),
        2 * rows * features * cols,
    )


def lat_back_kernel(count, offsets, place, act, kv_act, kv, lat_a, lat_b, scales, *refs):
    pieces, outs, (gain, held, sems) = refs[:count], refs[count:-3], refs[-3:]
    fetch(offsets, pieces, held, sems)
    step = 512
    scale_rows = scales[:, :1]
    for n in range(0, held.shape[0], step):
        value = dot_nt(act[...], held[n : n + step]) + dot_nt(kv_act[...], kv[n : n + step])
        lat = jnp.concatenate([lat_a[:, n : n + step], lat_b[:, n : n + step]], axis=0)
        unit = lat.astype(full) * scale_rows
        gain[:, n : n + step] = jnp.sum(value * unit, axis=0, keepdims=True)
        keep_and_send(place[0], outs, n, step, value.astype(low))


def lat_back(place, d_queries, weight, d_kv, kv, lat_a, lat_b, scales):
    offsets, pieces = weight
    rows, cols = d_queries.shape
    features = sum(piece.shape[0] for piece in pieces)
    half = (2, rows // 4, features // 2)
    arrays = [d_queries, d_kv, kv, lat_a, lat_b, scales]
    *parts, gain = call(
        lambda *refs: lat_back_kernel(len(pieces), *refs),
        "lat_back",
        [offsets, place],
        [*arrays, *pieces],
        [whole(a.shape) for a in arrays] + [pl.BlockSpec(memory_space=pltpu.HBM)] * len(pieces),
        [whole(half)] * 4 + [whole((1, features))],
        [jax.ShapeDtypeStruct(half, low)] * 4 + [jax.ShapeDtypeStruct((1, features), full)],
        [pltpu.VMEM((features, cols), low), pltpu.SemaphoreType.DMA((offsets.shape[0],))],
        (1,),
        2 * rows * features * (cols + kv.shape[1]),
    )
    return parts, gain


BLOCK = 256


def weight_grad(act, heads, blocks):
    rows, cols = heads.shape
    count = blocks.shape[0]

    def kernel(at, act_ref, heads_ref, out):
        out[0] = dot_tn(act_ref[...], heads_ref[...]).astype(low)

    return call(
        kernel,
        "weight_grad",
        [blocks],
        [act, heads],
        [pl.BlockSpec((rows, BLOCK), lambda i, at: (0, at[i])), whole(heads.shape)],
        [pl.BlockSpec((1, BLOCK, cols), lambda i, at: (i, 0, 0))],
        [jax.ShapeDtypeStruct((count, BLOCK, cols), low)],
        [],
        (count,),
        2 * rows * count * BLOCK * cols,
    )[0]


def kv_weight_grad_part(place, ctx_n, d_kv, lat_n, d_kv_lat, blocks):
    rows, cols = d_kv.shape
    count = blocks.shape[0]

    def kernel(at, here, ctx_ref, d_kv_ref, lat_ref, d_lat_ref, out, total):
        total[...] = dot_tn(ctx_ref[...], d_kv_ref[...])
        lat_part = dot_tn(lat_ref[...], d_lat_ref[...])
        first = here[0] * (cols // 2) + here[1] * HEAD_SIZE
        for k in range(2):
            at_k = pl.multiple_of(first + k * (cols // 4), HEAD_SIZE)
            span = pl.ds(at_k, HEAD_SIZE)
            total[:, span] += lat_part[:, k * HEAD_SIZE : (k + 1) * HEAD_SIZE]
        out[0] = total[...].astype(low)

    block = pl.BlockSpec((rows, BLOCK), lambda i, at, here: (0, at[i]))
    return call(
        kernel,
        "kv_weight_grad",
        [blocks, place],
        [ctx_n, d_kv, lat_n, d_kv_lat],
        [block, whole(d_kv.shape), block, whole(d_kv_lat.shape)],
        [pl.BlockSpec((1, BLOCK, cols), lambda i, at, here: (i, 0, 0))],
        [jax.ShapeDtypeStruct((count, BLOCK, cols), low)],
        [pltpu.VMEM((BLOCK, cols), full)],
        (count,),
        2 * rows * count * BLOCK * (cols + 2 * HEAD_SIZE),
    )[0]


NORM_ROWS = 64


def norm_rows(sources, gain):
    rows, features = sources[0].shape
    steps = rows // NORM_ROWS
    count = len(sources)

    def kernel(*refs):
        gain_ref, out, scale_out = refs[count:]
        for n in range(count):

            @pl.when(pl.program_id(0) == n)
            def _():
                values = refs[n][...].astype(full)
                scale_rows = lax.rsqrt(jnp.mean(values * values, axis=1, keepdims=True) + norm_eps)
                out[...] = (values * scale_rows * gain_ref[...]).astype(low)
                scale_out[...] = jnp.broadcast_to(scale_rows, scale_out.shape)

    def source_spec(n):
        return pl.BlockSpec(
            (NORM_ROWS, features), lambda s, i: (jnp.where(s == n, i, 0), 0)
        )

    return call(
        kernel,
        "norm_rows",
        [],
        [*sources, gain[None]],
        [source_spec(n) for n in range(count)] + [whole((1, features))],
        [
            pl.BlockSpec((NORM_ROWS, features), lambda s, i: (s * steps + i, 0)),
            pl.BlockSpec((NORM_ROWS, 128), lambda s, i: (s * steps + i, 0)),
        ],
        [
            jax.ShapeDtypeStruct((count * rows, features), low),
            jax.ShapeDtypeStruct((count * rows, 128), full),
        ],
        [],
        (count, steps),
        4 * count * rows * features,
    )


def ctx_back(d_kv, full_kv, context, scales, gain):
    rows, cols = d_kv.shape
    features = full_kv.shape[0]
    step = 128

    def kernel(d_ref, kv_ref, ctx_ref, scale_ref, gain_ref, out, gain_out):
        @pl.when(pl.program_id(0) == 0)
        def _():
            gain_out[...] = jnp.zeros_like(gain_out)

        d = dot_nt(d_ref[...], kv_ref[...])
        scale_rows = scale_ref[:, :1]
        unit = ctx_ref[...].astype(full) * scale_rows
        weighted = d * unit
        gain_out[...] += jnp.sum(weighted, axis=0, keepdims=True)
        inner = jnp.mean(weighted * gain_ref[...], axis=1, keepdims=True)
        out[...] = scale_rows * (d * gain_ref[...] - unit * inner)

    return call(
        kernel,
        "ctx_back",
        [],
        [d_kv, full_kv, context, scales, gain[None]],
        [
            pl.BlockSpec((step, cols), lambda i: (i, 0)),
            whole(full_kv.shape),
            pl.BlockSpec((step, features), lambda i: (i, 0)),
            pl.BlockSpec((step, 128), lambda i: (i, 0)),
            whole((1, features)),
        ],
        [pl.BlockSpec((step, features), lambda i: (i, 0)), whole((1, features))],
        [jax.ShapeDtypeStruct((rows, features), full), jax.ShapeDtypeStruct((1, features), full)],
        [],
        (rows // step,),
        2 * rows * cols * features,
    )


def after(value, *earlier):
    if not earlier:
        return value
    return lax.optimization_barrier((value, *earlier))[0]


class Place:
    def __init__(self):
        dp = lax.axis_size("dp")
        me = lax.axis_index("dp")
        self.dp = dp
        self.depth = dp // 4
        self.z = me // 4
        self.y = (me // 2) % 2
        self.c = me % 2
        self.x = lax.axis_index("tensor")
        self.scalars = jnp.stack([self.x, self.y]).astype(jnp.int32)
        self.perm_core = [(i, i ^ 1) for i in range(dp)]
        self.perm_y = [(i, i ^ 2) for i in range(dp)]
        self.perm_ring = [(i, (i + 4) % dp) for i in range(dp)]
        self.y_groups = [[i for i in range(dp) if (i // 2) % 2 == y] for y in range(2)]
        self.manual = self.depth == 4

    def over_core(self, v):
        return lax.ppermute(v, "dp", self.perm_core)

    def over_y(self, v):
        return lax.ppermute(v, "dp", self.perm_y)

    def over_x(self, v):
        return lax.ppermute(v, "tensor", [(0, 1), (1, 0)])

    def ring(self, v, *earlier):
        return lax.ppermute(after(v, *earlier), "dp", self.perm_ring)

    def row_block(self, z, y_other, c):
        return (z * 2 + (self.y ^ y_other)) * 2 + c

    def block(self, r, y_other, c_other):
        z = (self.z - r) % self.depth
        return (z * 2 + (self.y ^ y_other)) * 2 + (self.c ^ c_other)


def ordered(at, mine, other, axis):
    first = jnp.where(at == 0, mine, other)
    second = jnp.where(at == 0, other, mine)
    return jnp.concatenate([first, second], axis=axis)


def pick(v, at, axis):
    return lax.dynamic_index_in_dim(v, at, axis, keepdims=False)


def add(a, b):
    return a.astype(full) + b.astype(full)


def group_cols(v, x):
    half = v.shape[1] // 2
    return lax.dynamic_slice_in_dim(v, x * half, half, 1)


def head_cols(v, y):
    keys = lax.dynamic_slice_in_dim(v, y * HEAD_SIZE, HEAD_SIZE, 1)
    values = lax.dynamic_slice_in_dim(v, (2 + y) * HEAD_SIZE, HEAD_SIZE, 1)
    return jnp.concatenate([keys, values], axis=1)


def join_heads(y, mine, other):
    first = jnp.where(y == 0, mine, other)
    second = jnp.where(y == 0, other, mine)
    return jnp.concatenate(
        [
            first[:, :HEAD_SIZE],
            second[:, :HEAD_SIZE],
            first[:, HEAD_SIZE:],
            second[:, HEAD_SIZE:],
        ],
        axis=1,
    )


def gather_weight(here, weight, sent_after=(), wait=()):
    rows, cols = weight.shape
    half = cols // 2
    if not here.manual:
        held = lax.all_gather(weight, "dp", axis=0, tiled=True)
        held = lax.dynamic_slice_in_dim(held, here.y * half, half, 1)
        return (jnp.zeros((1,), jnp.int32), [held]), held
    mine = lax.dynamic_slice_in_dim(weight, here.y * half, half, 1)
    sent = lax.dynamic_slice_in_dim(weight, (1 - here.y) * half, half, 1)
    from_y = here.over_y(after(sent, *sent_after))
    both = jnp.concatenate([mine, from_y], axis=0)
    held = lax.all_gather(
        after(both, *wait), "dp", axis=0, tiled=True, axis_index_groups=here.y_groups
    )
    offsets = [
        here.row_block(z, y_other, c) * rows
        for z in range(here.depth)
        for c in range(2)
        for y_other in range(2)
    ]
    return (jnp.stack(offsets).astype(jnp.int32), [held]), from_y


class GatherKv:
    def __init__(self, here, weight):
        self.here = here
        self.rows = weight.shape[0] // 2
        if here.manual:
            self.held = [lax.dynamic_slice_in_dim(weight, here.x * self.rows, self.rows, 0)]
        else:
            self.held = [lax.all_gather(weight, "dp", axis=0, tiled=True)] * 4
        self.offsets, self.pieces = [], []

    def step(self, *wait):
        if self.here.manual:
            self.held.append(self.here.ring(self.held[-1], *wait))

    def __getitem__(self, r):
        return self.held[r]

    def spread(self, first, y_wait=(), x_wait=()):
        here = self.here
        if not here.manual:
            self.offsets, self.pieces = [0], [self.held[0]]
            return self.held[0], self.held[0]
        here_y = jnp.concatenate(self.held[first : first + 2], axis=0)
        from_y = here.over_y(after(here_y, *y_wait))
        here_x = jnp.concatenate([here_y, from_y], axis=0)
        from_x = here.over_x(after(here_x, *x_wait))
        here_c = jnp.concatenate([here_x, from_x], axis=0)
        from_c = here.over_core(here_c)
        self.pieces += [here_c, from_c]
        for c in range(2):
            for x in range(2):
                for y in range(2):
                    for r in (first, first + 1):
                        half = (here.x ^ x) * self.rows
                        self.offsets.append(here.block(r, y, c) * 2 * self.rows + half)
        return from_y, from_x

    def result(self):
        return jnp.stack(self.offsets).astype(jnp.int32), self.pieces


def scatter_weight(here, act, heads, wait=()):
    cols = heads.shape[1]
    features = act.shape[1]
    if here.manual:
        blocks = [
            here.row_block(z, y_other, c)
            for z in range(here.depth)
            for c in range(2)
            for y_other in range(2)
        ]
        part = weight_grad(act, heads, jnp.stack(blocks).astype(jnp.int32))
        part = part.reshape(features, cols)
    else:
        part = weight_grad(act, heads, jnp.arange(features // BLOCK, dtype=jnp.int32))
        part = part.reshape(here.depth, 2, 2, -1, cols).swapaxes(1, 2)
        part = part.reshape(here.depth, 2, 2, -1)
        first, second = part[:, :, 0], part[:, :, 1]
        part = jnp.stack([jnp.where(here.y == 0, first, second), jnp.where(here.y == 0, second, first)], 2)
        part = part.reshape(features, cols)
    total = lax.psum_scatter(
        after(part, *wait), "dp", scatter_dimension=0, tiled=True, axis_index_groups=here.y_groups
    )
    own, other = jnp.split(total, 2, axis=0)
    return part, total, lambda *wait: ordered(
        here.y, own.astype(full), here.over_y(after(other, *wait)).astype(full), 1
    )


class ScatterKv:
    def __init__(self, here, ctx_n, d_kv, lat_n, d_kv_lat, own_after=()):
        self.here = here
        cols = d_kv.shape[1]
        features = ctx_n.shape[1]
        if not here.manual:
            every = jnp.arange(features // BLOCK, dtype=jnp.int32)
            part = kv_weight_grad_part(here.scalars, ctx_n, d_kv, lat_n, d_kv_lat, every)
            part = part.reshape(features, cols)
            self.sent = self.first = self.second = [part]
            total = lax.psum_scatter(part, ("dp", "tensor"), scatter_dimension=0, tiled=True)
            self.total = total.astype(full)
            return

        def part(d_kv, c_other):
            blocks = [here.block(r, y, c_other) for y in range(2) for r in range(here.depth)]
            blocks = jnp.stack(blocks).astype(jnp.int32)
            part = kv_weight_grad_part(here.scalars, ctx_n, d_kv, lat_n, d_kv_lat, blocks)
            return part.reshape(2, here.depth, 2, BLOCK // 2, cols)

        sent = part(d_kv, 1)
        received = here.over_core(sent)
        mine = part(after(d_kv, sent, *own_after), 0)
        half = cols // 2
        a = add(mine[..., :half], received[..., :half])
        b = add(mine[..., half:], received[..., half:])
        self.sent = [a[1].astype(low), pick(b, 1 - here.x, 2).astype(low)]
        self.first = [here.over_y(self.sent[0]), here.over_x(self.sent[1])]
        a = a[0] + self.first[0]
        b = pick(b, here.x, 2) + self.first[1]
        self.second = [
            here.over_x(pick(a, 1 - here.x, 1).astype(low)),
            here.over_y(b[1].astype(low)),
        ]
        a = pick(a, here.x, 1) + self.second[0]
        b = b[0] + self.second[1]
        self.total = jnp.concatenate([a, b], axis=-1)

    def result(self):
        if not self.here.manual:
            return self.total
        held = 0.0
        for r in (1, 2, 3):
            held = self.here.ring((self.total[r] + held).astype(low))
        return self.total[0] + held


def gather_rows(here, rows, y_wait=(), x_wait=(), y_late=(), x_late=()):
    half = rows.shape[1] // 2
    a, b = rows[:, :half], rows[:, half:]
    a = ordered(here.x, a[None], here.over_x(after(a, *x_wait))[None], 0)
    a = jnp.stack([a, here.over_y(after(a, *y_late))])
    b = jnp.stack([b, here.over_y(after(b, *y_wait))])
    b = ordered(here.x, b[:, None], here.over_x(after(b, *x_late))[:, None], 1)
    return jnp.concatenate([a, b], axis=-1)


def scatter_rows(here, a_keep, a_sent, b_keep, b_sent):
    a, b = here.over_y(a_sent), here.over_x(b_sent)
    a_sum, b_sum = add(a_keep, a), add(b_keep, b)
    a_last = here.over_x(pick(a_sum, 1 - here.x, 0).astype(low))
    b_last = here.over_y(b_sum[1].astype(low))
    return jnp.concatenate([pick(a_sum, here.x, 0) + a_last, b_sum[0] + b_last], axis=-1), [a, b]


def scatter_gains(here, part):
    if not here.manual:
        devices = here.dp * 2
        part = part.reshape(2, devices, -1).swapaxes(0, 1)
        return lax.psum_scatter(part, ("dp", "tensor"), scatter_dimension=0)
    part = part.reshape(2, here.depth, 2, 2, 2, -1)
    part = pick(part, here.c, 3) + here.over_core(pick(part, 1 - here.c, 3))
    part = pick(part, here.x, 3) + here.over_x(pick(part, 1 - here.x, 3))
    part = pick(part, here.y, 2) + here.over_y(pick(part, 1 - here.y, 2))
    held = 0.0
    for r in (1, 2, 3, 0):
        held = pick(part, (here.z - r) % here.depth, 1) + held
        if r:
            held = lax.ppermute(held, "dp", here.perm_ring)
    return held


def norm_back(grad_rows, values, gain):
    scale_rows = lax.rsqrt(jnp.mean(values * values, axis=-1, keepdims=True) + norm_eps)
    unit_rows = values * scale_rows
    grad_unit = grad_rows * gain
    inner = jnp.mean(grad_unit * unit_rows, axis=-1, keepdims=True)
    return scale_rows * (grad_unit - unit_rows * inner)


def per_device(
    context, latents, lengths, ctx_gain, lat_gain, q_weight, key_value_weight, out_weight, out_grad
):
    here = Place()
    group_rows = latents.shape[0]
    my_rows = group_rows // 2
    features = context.shape[1]
    patch_rows = context.shape[0]

    kv = GatherKv(here, key_value_weight)
    full_q, q_sent = gather_weight(here, q_weight)
    kv.step()
    kv.step()
    first_y, first_x = kv.spread(0, [q_sent], [kv[2]])
    kv.step()
    second_y, second_x = kv.spread(2, [first_y], [first_x])
    lat_half = lax.dynamic_slice_in_dim(latents, here.x * my_rows, my_rows, 0)
    lat_half = here.over_y(after(lat_half, second_y, first_x))
    lat_x = here.over_x(after(lat_half, second_x))
    ctx_n, ctx_scales = norm_rows([after(context, first_x)], ctx_gain)
    full_out, out_sent = gather_weight(
        here, out_weight, [lat_half, second_x, ctx_n], [full_q[1][0]]
    )
    full_kv = kv.result()
    both_lengths = jnp.concatenate([lengths, here.over_y(lengths)], axis=0)
    ends = jnp.cumsum(both_lengths, axis=1)
    bounds = jnp.stack([(ends - both_lengths).reshape(-1), ends.reshape(-1)])

    kv_mine, kv_weight = rows_times_kv(ctx_n, full_kv)
    own_kv = head_cols(group_cols(kv_weight, here.x), here.y)
    kv_x = here.over_x(group_cols(kv_mine, 1 - here.x))
    lat_other = ordered(here.x, lat_half, after(lat_x, kv_mine), 0)
    lat_n, lat_scales = norm_rows([latents, lat_other], lat_gain)
    by_x = ordered(here.x, group_cols(kv_mine, here.x), kv_x, 0)
    kv_y = here.over_y(after(head_cols(by_x, 1 - here.y), lat_n, out_sent))
    kv_patch = jnp.stack([head_cols(by_x, here.y), kv_y])
    grad_all = gather_rows(here, out_grad, [out_sent], [kv_x], [kv_y], [kv_y])
    grad_all = grad_all.reshape(2 * group_rows, features)

    kv_latent = jnp.dot(lat_n, own_kv, preferred_element_type=full).astype(low)
    queries = rows_times_weight(lat_n, full_q)

    mixed, lse = attend(bounds, queries, kv_patch, kv_latent)
    out_part, out_total, out_result = scatter_weight(here, grad_all, mixed)
    d_mixed = rows_times_weight(after(grad_all, out_part), full_out)
    branch_parts = heads_times_weight(here.scalars, after(mixed, d_mixed), full_out)
    branch, branch_steps = scatter_rows(here, *branch_parts)
    lat_mine = lax.dynamic_slice_in_dim(latents, here.x * my_rows, my_rows, 0).astype(full)
    resampled = (lat_mine + branch).astype(low)

    d_queries, d_kv_patch, d_kv_latent = attend_back(
        bounds, queries, after(d_mixed, branch_parts[0]), kv_patch, kv_latent, lse
    )
    d_group_y = here.over_y(d_kv_patch[1])
    d_group = join_heads(here.y, d_kv_patch[0], d_group_y).reshape(2, patch_rows, -1)
    d_kv_mine = ordered(
        here.x, pick(d_group, here.x, 0), here.over_x(pick(d_group, 1 - here.x, 0)), 1
    )
    q_part, q_total, q_result = scatter_weight(here, lat_n, d_queries)
    lat_parts, lat_gain_part = lat_back(
        here.scalars,
        after(d_queries, q_part, d_group_y),
        full_q, d_kv_latent, own_kv, latents, lat_other, lat_scales,
    )
    kv_sum = ScatterKv(here, ctx_n, after(d_kv_mine, lat_parts[0]), lat_n, d_kv_latent)
    d_lat_n, lat_steps = scatter_rows(here, *lat_parts)
    latents_grad = out_grad.astype(full) + norm_back(d_lat_n, lat_mine, lat_gain)

    context_grad, ctx_gain_part = ctx_back(
        after(d_kv_mine, *kv_sum.sent), kv_weight, context, ctx_scales, ctx_gain
    )
    out_weight_grad = out_result()
    q_weight_grad = q_result()
    kv_weight_grad = kv_sum.result()
    gains = scatter_gains(here, jnp.concatenate([ctx_gain_part, lat_gain_part], axis=0))
    return (
        resampled,
        context_grad,
        latents_grad,
        gains[0],
        gains[1],
        q_weight_grad,
        kv_weight_grad,
        out_weight_grad,
    )


def solution(mesh):
    in_specs = (
        P(("dp", "tensor"), None),
        P("dp", None),
        P("dp", None),
        P(),
        P(),
        P("dp", "tensor"),
        P("dp", None),
        P("dp", "tensor"),
        P(("dp", "tensor"), None),
    )
    out_specs = (
        P(("dp", "tensor"), None),
        P(("dp", "tensor"), None),
        P(("dp", "tensor"), None),
        P(("dp", "tensor")),
        P(("dp", "tensor")),
        P("dp", "tensor"),
        P(("dp", "tensor"), None),
        P("dp", "tensor"),
    )
    return jax.shard_map(
        per_device, mesh=mesh, in_specs=in_specs, out_specs=out_specs, check_vma=False
    )
```

```python
import math

import jax
import jax.numpy as jnp
from jax import lax
from jax.experimental import pallas as pl
from jax.experimental.pallas import tpu as pltpu
from jax.sharding import PartitionSpec as P

QUERY_HEADS = 32
KEY_VALUE_HEADS = 4
HEAD_SIZE = 128
LAT = 64
IMG_GRP = 4
GROUPED = QUERY_HEADS // KEY_VALUE_HEADS

norm_eps = 1e-06
scale = HEAD_SIZE ** (-0.5)
scale_log2 = scale * math.log2(math.e)
low = jnp.bfloat16
full = jnp.float32
CHUNK = 256
HINT = 1
VMEM_BYTES = 48 * 1024 * 1024


def dot_nt(a, b):
    return lax.dot_general(a, b, (((1,), (1,)), ((), ())), preferred_element_type=full)


def dot_nn(a, b):
    return lax.dot_general(a, b, (((1,), (0,)), ((), ())), preferred_element_type=full)


def stack_heads(wide):
    return jnp.concatenate(
        [wide[:, h * HEAD_SIZE : (h + 1) * HEAD_SIZE] for h in range(GROUPED)], axis=0
    )


def spread_heads(tall):
    return jnp.concatenate([tall[h * LAT : (h + 1) * LAT] for h in range(GROUPED)], axis=1)


def fwd_kernel(bounds, q_ref, kvp_ref, kvl_ref, o_ref, lse_ref, s_scr, m_scr, l_scr, acc_scr):
    image = pl.program_id(0) * IMG_GRP + pl.program_id(1)
    lo = bounds[0, image]
    hi = bounds[1, image]
    chunks = kvp_ref.shape[1] // CHUNK
    qs = stack_heads(q_ref[...])
    s_lat = dot_nt(kvl_ref[:, :HEAD_SIZE], qs) * scale_log2
    m_scr[...] = jnp.max(s_lat, axis=0, keepdims=True)
    for j in range(chunks):

        @pl.when((lo < (j + 1) * CHUNK) & (hi > j * CHUNK))
        def _():
            keys = kvp_ref[0, j * CHUNK : (j + 1) * CHUNK, :HEAD_SIZE]
            s = dot_nt(keys, qs) * scale_log2
            at = lax.broadcasted_iota(jnp.int32, s.shape, 0) + j * CHUNK
            s = jnp.where((at >= lo) & (at < hi), s, -1e30)
            s_scr[j * CHUNK : (j + 1) * CHUNK, :] = s
            m_scr[...] = jnp.maximum(m_scr[...], jnp.max(s, axis=0, keepdims=True))

    top = m_scr[...]
    p = jnp.exp2(s_lat - top)
    l_scr[...] = jnp.sum(p, axis=0, keepdims=True)
    acc_scr[...] = dot_nn(kvl_ref[:, HEAD_SIZE:].T, p.astype(low))
    for j in range(chunks):

        @pl.when((lo < (j + 1) * CHUNK) & (hi > j * CHUNK))
        def _():
            values = kvp_ref[0, j * CHUNK : (j + 1) * CHUNK, HEAD_SIZE:]
            p = jnp.exp2(s_scr[j * CHUNK : (j + 1) * CHUNK, :] - top)
            l_scr[...] += jnp.sum(p, axis=0, keepdims=True)
            acc_scr[...] += dot_nn(values.T, p.astype(low))

    total = l_scr[...]
    lse_ref[0] = top + jnp.log2(total)
    o_ref[...] = spread_heads((acc_scr[...] / total).T).astype(low)


def bwd_kernel(
    bounds, q_ref, do_ref, kvp_ref, kvl_ref, lse_ref,
    dq_ref, dkvp_ref, dkvl_ref,
    p_scr, dp_scr, dkv_scr, dl_scr, dq_scr,
):
    i = pl.program_id(1)
    image = pl.program_id(0) * IMG_GRP + i
    lo = bounds[0, image]
    hi = bounds[1, image]
    chunks = kvp_ref.shape[1] // CHUNK
    qs = stack_heads(q_ref[...])
    dos = stack_heads(do_ref[...])
    lse = lse_ref[0]

    @pl.when(i == 0)
    def _():
        dkv_scr[...] = jnp.zeros_like(dkv_scr)

    k_lat = kvl_ref[:, :HEAD_SIZE]
    p_lat = jnp.exp2(dot_nt(k_lat, qs) * scale_log2 - lse)
    dp_lat = dot_nt(kvl_ref[:, HEAD_SIZE:], dos)
    dl_scr[...] = jnp.sum(p_lat * dp_lat, axis=0, keepdims=True)
    for j in range(chunks):

        @pl.when((lo < (j + 1) * CHUNK) & (hi > j * CHUNK))
        def _():
            rows = slice(j * CHUNK, (j + 1) * CHUNK)
            s = dot_nt(kvp_ref[0, rows, :HEAD_SIZE], qs) * scale_log2
            at = lax.broadcasted_iota(jnp.int32, s.shape, 0) + j * CHUNK
            s = jnp.where((at >= lo) & (at < hi), s - lse, -1e30)
            p = jnp.exp2(s)
            dp = dot_nt(kvp_ref[0, rows, HEAD_SIZE:], dos)
            dl_scr[...] += jnp.sum(p * dp, axis=0, keepdims=True)
            p_scr[rows, :] = p
            dp_scr[rows, :] = dp

    delta = dl_scr[...]
    ds_lat = (p_lat * (dp_lat - delta) * scale).astype(low)
    dq_scr[...] = dot_nn(k_lat.T, ds_lat)
    dkvl_ref[:, :HEAD_SIZE] = dot_nn(ds_lat, qs).astype(low)
    dkvl_ref[:, HEAD_SIZE:] = dot_nn(p_lat.astype(low), dos).astype(low)
    for j in range(chunks):

        @pl.when((lo < (j + 1) * CHUNK) & (hi > j * CHUNK))
        def _():
            rows = slice(j * CHUNK, (j + 1) * CHUNK)
            p = p_scr[rows, :]
            ds = (p * (dp_scr[rows, :] - delta) * scale).astype(low)
            dq_scr[...] += dot_nn(kvp_ref[0, rows, :HEAD_SIZE].T, ds)
            dkv_scr[rows, :HEAD_SIZE] += dot_nn(ds, qs)
            dkv_scr[rows, HEAD_SIZE:] += dot_nn(p.astype(low), dos)

    dq_ref[...] = spread_heads(dq_scr[...].T).astype(low)

    @pl.when(i == IMG_GRP - 1)
    def _():
        dkvp_ref[0] = dkv_scr[...].astype(low)


def attention_specs(groups, patches, heads_width):
    rows = pl.BlockSpec((LAT, heads_width), lambda g, i, b: (g * IMG_GRP + i, 0))
    kvp = pl.BlockSpec((1, patches, 2 * HEAD_SIZE), lambda g, i, b: (g, 0, 0))
    kvl = pl.BlockSpec((LAT, 2 * HEAD_SIZE), lambda g, i, b: (g * IMG_GRP + i, 0))
    lse = pl.BlockSpec((1, 1, GROUPED * LAT), lambda g, i, b: (g * IMG_GRP + i, 0, 0))
    return rows, kvp, kvl, lse


def attend(bounds, q, kvp, kvl):
    groups, patches, _ = kvp.shape
    rows, kvp_spec, kvl_spec, lse_spec = attention_specs(groups, patches, q.shape[1])
    wide = GROUPED * LAT
    return pl.pallas_call(
        fwd_kernel,
        grid_spec=pltpu.PrefetchScalarGridSpec(
            num_scalar_prefetch=1,
            grid=(groups, IMG_GRP),
            in_specs=[rows, kvp_spec, kvl_spec],
            out_specs=[rows, lse_spec],
            scratch_shapes=[
                pltpu.VMEM((patches, wide), full),
                pltpu.VMEM((1, wide), full),
                pltpu.VMEM((1, wide), full),
                pltpu.VMEM((HEAD_SIZE, wide), full),
            ],
        ),
        out_shape=[
            jax.ShapeDtypeStruct(q.shape, low),
            jax.ShapeDtypeStruct((groups * IMG_GRP, 1, wide), full),
        ],
        compiler_params=pltpu.CompilerParams(vmem_limit_bytes=VMEM_BYTES),
        cost_estimate=pl.CostEstimate(
            flops=2 * 2 * groups * IMG_GRP * wide * patches * HEAD_SIZE // HINT,
            bytes_accessed=(4 * q.size + 2 * kvp.size) // HINT,
            transcendentals=groups * IMG_GRP * wide * patches // HINT,
        ),
        name="attention_forward",
    )(bounds, q, kvp, kvl)


def attend_back(bounds, q, d_out, kvp, kvl, lse):
    groups, patches, _ = kvp.shape
    rows, kvp_spec, kvl_spec, lse_spec = attention_specs(groups, patches, q.shape[1])
    wide = GROUPED * LAT
    return pl.pallas_call(
        bwd_kernel,
        grid_spec=pltpu.PrefetchScalarGridSpec(
            num_scalar_prefetch=1,
            grid=(groups, IMG_GRP),
            in_specs=[rows, rows, kvp_spec, kvl_spec, lse_spec],
            out_specs=[rows, kvp_spec, kvl_spec],
            scratch_shapes=[
                pltpu.VMEM((patches, wide), full),
                pltpu.VMEM((patches, wide), full),
                pltpu.VMEM((patches, 2 * HEAD_SIZE), full),
                pltpu.VMEM((1, wide), full),
                pltpu.VMEM((HEAD_SIZE, wide), full),
            ],
        ),
        out_shape=[
            jax.ShapeDtypeStruct(q.shape, low),
            jax.ShapeDtypeStruct(kvp.shape, low),
            jax.ShapeDtypeStruct(kvl.shape, low),
        ],
        compiler_params=pltpu.CompilerParams(vmem_limit_bytes=VMEM_BYTES),
        cost_estimate=pl.CostEstimate(
            flops=2 * 5 * groups * IMG_GRP * wide * patches * HEAD_SIZE // 1000,
            bytes_accessed=(6 * q.size + 4 * kvp.size) // 1000,
            transcendentals=groups * IMG_GRP * wide * patches // 1000,
        ),
        name="attention_backward",
    )(bounds, q, d_out, kvp, kvl, lse)


def dot_tn(a, b):
    return lax.dot_general(a, b, (((0,), (0,)), ((), ())), preferred_element_type=full)


def call(kernel, name, scalars, arrays, in_specs, out_specs, out_shape, scratch, grid, flops, hint=1):
    moved = sum(a.size * a.dtype.itemsize for a in arrays)
    moved += sum(o.size * o.dtype.itemsize for o in out_shape)
    return pl.pallas_call(
        kernel,
        grid_spec=pltpu.PrefetchScalarGridSpec(
            num_scalar_prefetch=len(scalars),
            grid=grid,
            in_specs=in_specs,
            out_specs=out_specs,
            scratch_shapes=scratch,
        ),
        out_shape=out_shape,
        compiler_params=pltpu.CompilerParams(vmem_limit_bytes=VMEM_BYTES),
        cost_estimate=pl.CostEstimate(flops=flops // hint, bytes_accessed=moved // hint, transcendentals=0),
        name=name,
    )(*scalars, *arrays)


def whole(shape):
    return pl.BlockSpec(shape, lambda *_: (0,) * len(shape))


def fetch(offsets, pieces, held, sems):
    total = sum(piece.shape[0] for piece in pieces)
    rows = held.shape[0] // offsets.shape[0]
    assert total == held.shape[0]
    copies = []
    for piece in pieces:
        for first in range(0, piece.shape[0], rows):
            n = len(copies)
            at = pl.multiple_of(offsets[n], rows)
            copies.append(
                pltpu.make_async_copy(
                    piece.at[pl.ds(first, rows)], held.at[pl.ds(at, rows)], sems.at[n]
                )
            )
    for copy in copies:
        copy.start()
    for copy in copies:
        copy.wait()


def rows_kernel(count, offsets, act, *refs):
    pieces, (out, held, sems) = refs[:count], refs[count:]
    fetch(offsets, pieces, held, sems)
    step = 256
    for n in range(0, out.shape[1], step):
        out[:, n : n + step] = dot_nn(act[...], held[:, n : n + step]).astype(out.dtype)


def rows_times_weight(act, weight):
    offsets, pieces = weight
    cols = pieces[0].shape[1]
    rows, features = act.shape
    return call(
        lambda *refs: rows_kernel(len(pieces), *refs),
        "rows_times_weight",
        [offsets],
        [act, *pieces],
        [whole(act.shape)] + [pl.BlockSpec(memory_space=pltpu.HBM)] * len(pieces),
        [whole((rows, cols))],
        [jax.ShapeDtypeStruct((rows, cols), low)],
        [pltpu.VMEM((features, cols), low), pltpu.SemaphoreType.DMA((offsets.shape[0],))],
        (1,),
        2 * rows * features * cols,
    )[0]


def rows_times_kv(act, weight):
    offsets, pieces = weight
    rows, features = act.shape
    cols = pieces[0].shape[1]
    count = len(pieces)

    def kernel(offsets_ref, act_ref, *refs):
        out, held, sems = refs[count:]
        fetch(offsets_ref, refs[:count], held, sems)
        step = 256
        for n in range(0, cols, step):
            out[:, n : n + step] = dot_nn(act_ref[...], held[:, n : n + step]).astype(low)

    return call(
        kernel,
        "rows_times_kv",
        [offsets],
        [act, *pieces],
        [whole(act.shape)] + [pl.BlockSpec(memory_space=pltpu.HBM)] * count,
        [whole((rows, cols)), whole((features, cols))],
        [jax.ShapeDtypeStruct((rows, cols), low), jax.ShapeDtypeStruct((features, cols), low)],
        [pltpu.SemaphoreType.DMA((offsets.shape[0],))],
        (1,),
        2 * rows * features * cols,
    )


def split_features(features, part):
    first = features * part // 8
    return [first, first, features - first, features - first]


def keep_and_send(x, outs, n, step, value):
    a_keep, a_sent, b_keep, b_sent = outs
    quarter = value.shape[0] // 4
    parts = [value[k * quarter : (k + 1) * quarter] for k in range(4)]
    half = a_keep.shape[2]
    if n < half:
        for k in range(2):
            a_keep[k, :, n : n + step] = parts[k]
            a_sent[k, :, n : n + step] = parts[2 + k]
    else:
        span = slice(n - half, n - half + step)
        for g in range(2):
            b_keep[g, :, span] = jnp.where(x == 0, parts[2 * g], parts[2 * g + 1])
            b_sent[g, :, span] = jnp.where(x == 0, parts[2 * g + 1], parts[2 * g])


def heads_kernel(count, offsets, place, act, *refs):
    pieces, outs, (held, sems) = refs[:count], refs[count:-2], refs[-2:]
    fetch(offsets, pieces, held, sems)
    step = 512
    for n in range(0, held.shape[0], step):
        value = dot_nt(act[...], held[n : n + step]).astype(low)
        keep_and_send(place[0], outs, n, step, value)


def heads_times_weight(place, act, weight):
    offsets, pieces = weight
    rows, cols = act.shape
    features = sum(piece.shape[0] for piece in pieces)
    halves = [(2, rows // 4, n) for n in split_features(features, 4)]
    return call(
        lambda *refs: heads_kernel(len(pieces), *refs),
        "heads_times_weight",
        [offsets, place],
        [act, *pieces],
        [whole(act.shape)] + [pl.BlockSpec(memory_space=pltpu.HBM)] * len(pieces),
        [whole(half) for half in halves],
        [jax.ShapeDtypeStruct(half, low) for half in halves],
        [pltpu.VMEM((features, cols), low), pltpu.SemaphoreType.DMA((offsets.shape[0],))],
        (1,),
        2 * rows * features * cols,
        hint=1000,
    )


def lat_back_kernel(count, offsets, place, act, kv_act, kv, lat_a, lat_b, scales, *refs):
    pieces, outs, (gain, held, sems) = refs[:count], refs[count:-3], refs[-3:]
    fetch(offsets, pieces, held, sems)
    step = 512
    scale_rows = scales[:, :1]
    for n in range(0, held.shape[0], step):
        value = dot_nt(act[...], held[n : n + step]) + dot_nt(kv_act[...], kv[n : n + step])
        lat = jnp.concatenate([lat_a[:, n : n + step], lat_b[:, n : n + step]], axis=0)
        unit = lat.astype(full) * scale_rows
        gain[:, n : n + step] = jnp.sum(value * unit, axis=0, keepdims=True)
        keep_and_send(place[0], outs, n, step, value.astype(low))


def lat_back(place, d_queries, weight, d_kv, kv, lat_a, lat_b, scales):
    offsets, pieces = weight
    rows, cols = d_queries.shape
    features = sum(piece.shape[0] for piece in pieces)
    halves = [(2, rows // 4, n) for n in split_features(features, 4)]
    arrays = [d_queries, d_kv, kv, lat_a, lat_b, scales]
    *parts, gain = call(
        lambda *refs: lat_back_kernel(len(pieces), *refs),
        "lat_back",
        [offsets, place],
        [*arrays, *pieces],
        [whole(a.shape) for a in arrays] + [pl.BlockSpec(memory_space=pltpu.HBM)] * len(pieces),
        [whole(half) for half in halves] + [whole((1, features))],
        [jax.ShapeDtypeStruct(half, low) for half in halves] + [jax.ShapeDtypeStruct((1, features), full)],
        [pltpu.VMEM((features, cols), low), pltpu.SemaphoreType.DMA((offsets.shape[0],))],
        (1,),
        2 * rows * features * (cols + kv.shape[1]),
    )
    return parts, gain


BLOCK = 256


def weight_grad(act, heads, blocks):
    rows, cols = heads.shape
    count = blocks.shape[0]

    def kernel(at, act_ref, heads_ref, out):
        out[0] = dot_tn(act_ref[...], heads_ref[...]).astype(low)

    return call(
        kernel,
        "weight_grad",
        [blocks],
        [act, heads],
        [pl.BlockSpec((rows, BLOCK), lambda i, at: (0, at[i])), whole(heads.shape)],
        [pl.BlockSpec((1, BLOCK, cols), lambda i, at: (i, 0, 0))],
        [jax.ShapeDtypeStruct((count, BLOCK, cols), low)],
        [],
        (count,),
        2 * rows * count * BLOCK * cols,
    )[0]


def kv_weight_grad_part(place, ctx_n, d_kv, lat_n, d_kv_lat, blocks):
    rows, cols = d_kv.shape
    count = blocks.shape[0]

    def kernel(at, here, ctx_ref, d_kv_ref, lat_ref, d_lat_ref, out, total):
        total[...] = dot_tn(ctx_ref[...], d_kv_ref[...])
        lat_part = dot_tn(lat_ref[...], d_lat_ref[...])
        first = here[0] * (cols // 2) + here[1] * HEAD_SIZE
        for k in range(2):
            at_k = pl.multiple_of(first + k * (cols // 4), HEAD_SIZE)
            span = pl.ds(at_k, HEAD_SIZE)
            total[:, span] += lat_part[:, k * HEAD_SIZE : (k + 1) * HEAD_SIZE]
        out[0] = total[...].astype(low)

    block = pl.BlockSpec((rows, BLOCK), lambda i, at, here: (0, at[i]))
    return call(
        kernel,
        "kv_weight_grad",
        [blocks, place],
        [ctx_n, d_kv, lat_n, d_kv_lat],
        [block, whole(d_kv.shape), block, whole(d_kv_lat.shape)],
        [pl.BlockSpec((1, BLOCK, cols), lambda i, at, here: (i, 0, 0))],
        [jax.ShapeDtypeStruct((count, BLOCK, cols), low)],
        [pltpu.VMEM((BLOCK, cols), full)],
        (count,),
        2 * rows * count * BLOCK * (cols + 2 * HEAD_SIZE),
    )[0]


NORM_ROWS = 64


def norm_rows(sources, gain):
    rows, features = sources[0].shape
    steps = rows // NORM_ROWS
    count = len(sources)

    def kernel(*refs):
        gain_ref, out, scale_out = refs[count:]
        for n in range(count):

            @pl.when(pl.program_id(0) == n)
            def _():
                values = refs[n][...].astype(full)
                scale_rows = lax.rsqrt(jnp.mean(values * values, axis=1, keepdims=True) + norm_eps)
                out[...] = (values * scale_rows * gain_ref[...]).astype(low)
                scale_out[...] = jnp.broadcast_to(scale_rows, scale_out.shape)

    def source_spec(n):
        return pl.BlockSpec(
            (NORM_ROWS, features), lambda s, i: (jnp.where(s == n, i, 0), 0)
        )

    return call(
        kernel,
        "norm_rows",
        [],
        [*sources, gain[None]],
        [source_spec(n) for n in range(count)] + [whole((1, features))],
        [
            pl.BlockSpec((NORM_ROWS, features), lambda s, i: (s * steps + i, 0)),
            pl.BlockSpec((NORM_ROWS, 128), lambda s, i: (s * steps + i, 0)),
        ],
        [
            jax.ShapeDtypeStruct((count * rows, features), low),
            jax.ShapeDtypeStruct((count * rows, 128), full),
        ],
        [],
        (count, steps),
        4 * count * rows * features,
        hint=1,
    )


def ctx_back(d_kv, full_kv, context, scales, gain):
    rows, cols = d_kv.shape
    features = full_kv.shape[0]
    step = 128

    def kernel(d_ref, kv_ref, ctx_ref, scale_ref, gain_ref, out, gain_out):
        @pl.when(pl.program_id(0) == 0)
        def _():
            gain_out[...] = jnp.zeros_like(gain_out)

        d = dot_nt(d_ref[...], kv_ref[...])
        scale_rows = scale_ref[:, :1]
        unit = ctx_ref[...].astype(full) * scale_rows
        weighted = d * unit
        gain_out[...] += jnp.sum(weighted, axis=0, keepdims=True)
        inner = jnp.mean(weighted * gain_ref[...], axis=1, keepdims=True)
        out[...] = scale_rows * (d * gain_ref[...] - unit * inner)

    return call(
        kernel,
        "ctx_back",
        [],
        [d_kv, full_kv, context, scales, gain[None]],
        [
            pl.BlockSpec((step, cols), lambda i: (i, 0)),
            whole(full_kv.shape),
            pl.BlockSpec((step, features), lambda i: (i, 0)),
            pl.BlockSpec((step, 128), lambda i: (i, 0)),
            whole((1, features)),
        ],
        [pl.BlockSpec((step, features), lambda i: (i, 0)), whole((1, features))],
        [jax.ShapeDtypeStruct((rows, features), full), jax.ShapeDtypeStruct((1, features), full)],
        [],
        (rows // step,),
        2 * rows * cols * features,
        hint=1,
    )


def after(value, *earlier):
    if not earlier:
        return value
    return lax.optimization_barrier((value, *earlier))[0]


class Place:
    def __init__(self):
        dp = lax.axis_size("dp")
        me = lax.axis_index("dp")
        self.dp = dp
        self.depth = dp // 4
        self.z = me // 4
        self.y = (me // 2) % 2
        self.c = me % 2
        self.x = lax.axis_index("tensor")
        self.scalars = jnp.stack([self.x, self.y]).astype(jnp.int32)
        self.perm_core = [(i, i ^ 1) for i in range(dp)]
        self.perm_y = [(i, i ^ 2) for i in range(dp)]
        self.perm_ring = [(i, (i + 4) % dp) for i in range(dp)]
        self.y_groups = [[i for i in range(dp) if (i // 2) % 2 == y] for y in range(2)]
        self.z_groups = [list(range(k, dp, 4)) for k in range(4)]
        self.manual = self.depth == 4

    def over_core(self, v):
        return lax.ppermute(v, "dp", self.perm_core)

    def over_y(self, v):
        return lax.ppermute(v, "dp", self.perm_y)

    def over_x(self, v):
        return lax.ppermute(v, "tensor", [(0, 1), (1, 0)])

    def ring(self, v, *earlier):
        return lax.ppermute(after(v, *earlier), "dp", self.perm_ring)

    def shift(self, v, r):
        return lax.ppermute(v, "dp", [(i, (i + 4 * r) % self.dp) for i in range(self.dp)])

    def row_blocks(self):
        return [
            (z * 2 + (self.y ^ y_other)) * 2 + c
            for z in range(self.depth)
            for c in range(2)
            for y_other in range(2)
        ]

    def block(self, r, y_other, c_other):
        z = (self.z - r) % self.depth
        return (z * 2 + (self.y ^ y_other)) * 2 + (self.c ^ c_other)


def ordered(at, mine, other, axis):
    first = jnp.where(at == 0, mine, other)
    second = jnp.where(at == 0, other, mine)
    return jnp.concatenate([first, second], axis=axis)


def pick(v, at, axis):
    return lax.dynamic_index_in_dim(v, at, axis, keepdims=False)


def add(a, b):
    return a.astype(full) + b.astype(full)


def group_cols(v, x):
    half = v.shape[1] // 2
    return lax.dynamic_slice_in_dim(v, x * half, half, 1)


def head_cols(v, y):
    keys = lax.dynamic_slice_in_dim(v, y * HEAD_SIZE, HEAD_SIZE, 1)
    values = lax.dynamic_slice_in_dim(v, (2 + y) * HEAD_SIZE, HEAD_SIZE, 1)
    return jnp.concatenate([keys, values], axis=1)


def join_heads(y, mine, other):
    first = jnp.where(y == 0, mine, other)
    second = jnp.where(y == 0, other, mine)
    return jnp.concatenate(
        [
            first[:, :HEAD_SIZE],
            second[:, :HEAD_SIZE],
            first[:, HEAD_SIZE:],
            second[:, HEAD_SIZE:],
        ],
        axis=1,
    )


class WeightBlock:
    def __init__(self, here, weight):
        self.here = here
        self.rows, cols = weight.shape
        half = cols // 2
        if not here.manual:
            held = lax.all_gather(weight, "dp", axis=0, tiled=True)
            self.from_y = lax.dynamic_slice_in_dim(held, here.y * half, half, 1)
            return
        mine = lax.dynamic_slice_in_dim(weight, here.y * half, half, 1)
        sent = lax.dynamic_slice_in_dim(weight, (1 - here.y) * half, half, 1)
        self.from_y = here.over_y(sent)
        self.block = jnp.concatenate([mine, self.from_y], axis=0)

    def result(self, *wait):
        here = self.here
        if not here.manual:
            return jnp.zeros((1,), jnp.int32), [self.from_y]
        held = lax.all_gather(
            after(self.block, *wait), "dp", axis=0, tiled=True, axis_index_groups=here.y_groups
        )
        offsets = [row * self.rows for row in here.row_blocks()]
        return jnp.stack(offsets).astype(jnp.int32), [held]


class GatherKv:
    def __init__(self, here, weight):
        self.here = here
        self.rows = weight.shape[0] // 2
        if here.manual:
            mine = lax.dynamic_slice_in_dim(weight, here.x * self.rows, self.rows, 0)
            self.first = [here.shift(mine, r) for r in (1, 3, 2)]
            self.held = jnp.concatenate([mine] + [self.first[k] for k in (0, 2, 1)], axis=0)
        else:
            self.held = lax.all_gather(weight, "dp", axis=0, tiled=True)
            self.first = [self.held]

    def over_y(self, *wait):
        if self.here.manual:
            from_y = self.here.over_y(after(self.held, *wait))
            self.near = jnp.concatenate([self.held, from_y], axis=0)
            return from_y
        return self.held

    def over_x(self, *wait):
        if self.here.manual:
            self.far = self.here.over_x(after(self.near, *wait))
            return self.far
        return self.held

    def result(self, *wait):
        here = self.here
        if not here.manual:
            return jnp.zeros((1,), jnp.int32), [self.held]
        pieces = [self.near, self.far]
        pieces += [here.over_core(self.near), here.over_core(after(self.far, *wait))]
        offsets = [
            here.block(r, y, c) * 2 * self.rows + (here.x ^ x) * self.rows
            for c in range(2)
            for x in range(2)
            for y in range(2)
            for r in range(4)
        ]
        return jnp.stack(offsets).astype(jnp.int32), pieces


def scatter_rows_of_y(here, act, heads):
    cols = heads.shape[1]
    features = act.shape[1]
    if here.manual:
        blocks = here.row_blocks()[::2]
        part = weight_grad(act, heads, jnp.stack(blocks).astype(jnp.int32))
    else:
        part = weight_grad(act, heads, jnp.arange(features // BLOCK, dtype=jnp.int32))
        part = pick(part.reshape(here.depth, 2, 2, -1, cols), here.y, 1)
    part = part.reshape(features // 2, cols)
    total = lax.psum_scatter(
        part, "dp", scatter_dimension=0, tiled=True, axis_index_groups=here.y_groups
    )
    return part, total.astype(full)


def scatter_weight(here, act, heads):
    cols = heads.shape[1]
    features = act.shape[1]
    if here.manual:
        part = weight_grad(act, heads, jnp.stack(here.row_blocks()).astype(jnp.int32))
    else:
        part = weight_grad(act, heads, jnp.arange(features // BLOCK, dtype=jnp.int32))
        part = part.reshape(here.depth, 2, 2, -1, cols)
        part = jnp.stack([pick(part, here.y, 1), pick(part, 1 - here.y, 1)], axis=2)
    part = part.reshape(features, cols)
    total = lax.psum_scatter(
        part, "dp", scatter_dimension=0, tiled=True, axis_index_groups=here.y_groups
    )

    def result(*wait):
        own, other = jnp.split(after(total, *wait), 2, axis=0)
        from_y = here.over_y(other)
        return ordered(here.y, own.astype(full), from_y.astype(full), 1), from_y

    return part, result


class ScatterKv:
    def __init__(self, here, ctx_n, d_kv, lat_n, d_kv_lat):
        self.here = here
        self.cols = d_kv.shape[1]
        self.args = (ctx_n, d_kv, lat_n, d_kv_lat)
        if not here.manual:
            every = jnp.arange(ctx_n.shape[1] // BLOCK, dtype=jnp.int32)
            part = kv_weight_grad_part(here.scalars, *self.args, every)
            self.other_part = part.reshape(-1, self.cols)
            return
        self.other_part = self.part(d_kv, 1)
        self.received = here.over_core(self.other_part)

    def part(self, d_kv, c_other):
        here = self.here
        ctx_n, _, lat_n, d_kv_lat = self.args
        blocks = [here.block(r, y, c_other) for y in range(2) for r in range(here.depth)]
        blocks = jnp.stack(blocks).astype(jnp.int32)
        part = kv_weight_grad_part(here.scalars, ctx_n, d_kv, lat_n, d_kv_lat, blocks)
        return part.reshape(2, here.depth, 2, BLOCK // 2, self.cols)

    def own(self, *wait):
        self.own_part = self.other_part
        if self.here.manual:
            self.own_part = self.part(after(self.args[1], self.other_part, *wait), 0)

    def start(self, *wait):
        here = self.here
        if not here.manual:
            self.sent = self.first = self.last = [self.other_part]
            total = lax.psum_scatter(
                self.other_part, ("dp", "tensor"), scatter_dimension=0, tiled=True
            )
            self.total = total.astype(full)
            return
        mine, received = self.own_part, self.received
        half = self.cols // 2
        a = add(mine[..., :half], received[..., :half])
        b = add(mine[..., half:], received[..., half:])
        self.sent = [a[1].astype(low), pick(b, 1 - here.x, 2).astype(low)]
        self.first = [
            here.over_y(after(self.sent[0], *wait)),
            here.over_x(after(self.sent[1], *wait)),
        ]
        self.halves = [a[0] + self.first[0], pick(b, here.x, 2) + self.first[1]]

    def go_on(self, *wait):
        here = self.here
        if not here.manual:
            return
        a, b = self.halves
        self.last = [
            here.over_x(after(pick(a, 1 - here.x, 1).astype(low), *wait)),
            here.over_y(after(b[1].astype(low), *wait)),
        ]
        a, b = pick(a, here.x, 1) + self.last[0], b[0] + self.last[1]
        self.total = jnp.concatenate([a, b], axis=-1)

    def result(self, *wait):
        here, total = self.here, self.total
        if not here.manual:
            self.over_z = [total]
            return total
        held = [here.shift(after(total[r].astype(low), *wait), -r) for r in (1, 2, 3)]
        self.over_z = held
        return total[0] + held[0] + held[1] + held[2]


class ScatterRows:
    def __init__(self, here, a_keep, a_sent, b_keep, b_sent, y_wait=(), x_wait=()):
        self.here = here
        self.keep = [a_keep, b_keep]
        self.first = [here.over_y(after(a_sent, *y_wait)), here.over_x(after(b_sent, *x_wait))]

    def prepare(self, *wait):
        here = self.here
        (a_keep, b_keep), (a, b) = self.keep, [after(v, *wait) for v in self.first]
        self.sent = [
            add(pick(a_keep, 1 - here.x, 0), pick(a, 1 - here.x, 0)).astype(low),
            add(b_keep[1], b[1]).astype(low),
        ]

    def finish(self, x_wait=(), y_wait=()):
        here = self.here
        self.last = [
            here.over_x(after(self.sent[0], *x_wait)),
            here.over_y(after(self.sent[1], *y_wait)),
        ]

    def result(self, *wait):
        here = self.here
        (a_keep, b_keep), (a, b) = self.keep, self.first
        a_last, b_last = [after(v, *wait) for v in self.last]
        a = add(pick(a_keep, here.x, 0), pick(a, here.x, 0)) + a_last
        b = add(b_keep[0], b[0]) + b_last
        return jnp.concatenate([a, b], axis=-1)


def gather_gains(here, part):
    if not here.manual:
        return part
    part = part.reshape(2, here.depth, 2, 2, 2, -1)
    part = pick(part, here.c, 3) + here.over_core(pick(part, 1 - here.c, 3))
    part = pick(part, here.x, 3) + here.over_x(pick(part, 1 - here.x, 3))
    return pick(part, here.y, 2) + here.over_y(pick(part, 1 - here.y, 2))


def scatter_gains(here, part):
    if not here.manual:
        devices = here.dp * 2
        part = part.reshape(2, devices, -1).swapaxes(0, 1)
        return lax.psum_scatter(part, ("dp", "tensor"), scatter_dimension=0)
    mine = [pick(part, (here.z - r) % here.depth, 1) for r in range(4)]
    return mine[0] + here.shift(mine[1], -1) + here.shift(mine[2], -2) + here.shift(mine[3], -3)


def norm_back(grad_rows, values, gain):
    scale_rows = lax.rsqrt(jnp.mean(values * values, axis=-1, keepdims=True) + norm_eps)
    unit_rows = values * scale_rows
    grad_unit = grad_rows * gain
    inner = jnp.mean(grad_unit * unit_rows, axis=-1, keepdims=True)
    return scale_rows * (grad_unit - unit_rows * inner)


def per_device(
    context, latents, lengths, ctx_gain, lat_gain, q_weight, key_value_weight, out_weight, out_grad
):
    here = Place()
    group_rows = latents.shape[0]
    my_rows = group_rows // 2
    features = context.shape[1]
    patch_rows = context.shape[0]

    kv = GatherKv(here, key_value_weight)
    lengths_y = here.over_y(lengths)
    q_block = WeightBlock(here, q_weight)
    out_block = WeightBlock(here, out_weight)
    full_q = q_block.result(*kv.first, lengths_y, out_block.from_y)
    first = [q_block.from_y, out_block.from_y, *kv.first]
    kv_from_y = kv.over_y(*first)
    grad_x = here.over_x(after(out_grad, *first))
    ctx_n, ctx_scales = norm_rows([after(context, *first)], ctx_gain)
    second = [kv_from_y, grad_x, ctx_n]
    kv_from_x = kv.over_x(*second)
    lat_other = here.over_y(after(latents, *second))
    full_kv = kv.result(lat_other)
    full_out = out_block.result(full_q[1][0], full_kv[1][-1], lat_other)
    both_lengths = jnp.concatenate([lengths, lengths_y], axis=0)
    ends = jnp.cumsum(both_lengths, axis=1)
    bounds = jnp.stack([(ends - both_lengths).reshape(-1), ends.reshape(-1)])

    kv_mine, kv_weight = rows_times_kv(ctx_n, full_kv)
    own_kv = head_cols(group_cols(kv_weight, here.x), here.y)
    kv_x = here.over_x(group_cols(kv_mine, 1 - here.x))
    grad_y_a = here.over_y(after(grad_x, lat_other, kv_from_x))
    lat_n, lat_scales = norm_rows([latents, after(lat_other, kv_mine, grad_y_a)], lat_gain)
    by_x = ordered(here.x, group_cols(kv_mine, here.x), kv_x, 0)
    kv_y = here.over_y(after(head_cols(by_x, 1 - here.y), lat_n, full_q[1][0]))
    kv_patch = jnp.stack([head_cols(by_x, here.y), kv_y])
    grad_y_b = here.over_y(after(out_grad, kv_y))

    kv_latent = jnp.dot(lat_n, own_kv, preferred_element_type=full).astype(low)
    queries = rows_times_weight(lat_n, full_q)

    mixed, lse = attend(bounds, queries, kv_patch, kv_latent)
    grad_all = jnp.stack([out_grad, grad_x, after(grad_y_b, mixed), after(grad_y_a, mixed)])
    grad_all = grad_all.reshape(2, 2, my_rows, features)
    grad_all = ordered(here.x, grad_all[:, :1], grad_all[:, 1:], 1)
    grad_all = grad_all.reshape(2 * group_rows, features)
    out_part, out_result = scatter_weight(here, grad_all, mixed)
    d_mixed = rows_times_weight(after(grad_all, out_part), full_out)
    d_queries, d_kv_patch, d_kv_latent = attend_back(
        bounds, queries, d_mixed, kv_patch, kv_latent, lse
    )
    d_group_y = here.over_y(d_kv_patch[1])
    branch_parts = heads_times_weight(here.scalars, after(mixed, d_queries), full_out)
    d_group = join_heads(here.y, d_kv_patch[0], d_group_y).reshape(2, patch_rows, -1)

    d_group_x = here.over_x(after(pick(d_group, 1 - here.x, 0), branch_parts[0]))
    d_kv_mine = ordered(here.x, pick(d_group, here.x, 0), d_group_x, 1)
    d_queries_y = here.over_y(after(d_queries, d_group_y, branch_parts[0]))
    lat_parts, lat_gain_part = lat_back(
        here.scalars, after(d_queries, d_group_y), full_q, d_kv_latent, own_kv,
        latents, lat_other, lat_scales,
    )
    kv_sum = ScatterKv(here, ctx_n, after(d_kv_mine, lat_parts[0]), lat_n, d_kv_latent)
    d_queries_y = jnp.concatenate([d_queries_y[group_rows:], d_queries_y[:group_rows]], axis=0)
    d_queries_all = ordered(here.y, d_queries, d_queries_y, 1)
    branch = ScatterRows(here, *branch_parts, [d_queries_y], [d_group_y])
    q_part, q_weight_grad = scatter_rows_of_y(
        here, after(lat_n, kv_sum.other_part, branch.first[1]), d_queries_all
    )
    kv_sum.own(q_part)
    kv_sum.start(branch.first[0])
    branch.prepare()
    branch.finish(kv_sum.sent, kv_sum.sent)
    context_grad, ctx_gain_part = ctx_back(
        after(d_kv_mine, *kv_sum.sent), kv_weight, context, ctx_scales, ctx_gain
    )
    gains = jnp.concatenate([after(ctx_gain_part, *kv_sum.first), lat_gain_part], axis=0)
    gains = gather_gains(here, gains)

    second = [*kv_sum.first, *branch.last, ctx_gain_part, gains]
    lat_sum = ScatterRows(here, *lat_parts, second, second)
    kv_sum.go_on(*second)
    kv_weight_grad = kv_sum.result(*kv_sum.last)
    third = [*kv_sum.over_z, *lat_sum.first]
    lat_sum.prepare()
    lat_sum.finish(third, third)
    out_weight_grad, _ = out_result(*third)
    gains = scatter_gains(here, after(gains, *kv_sum.last))
    lat_mine = lax.dynamic_slice_in_dim(latents, here.x * my_rows, my_rows, 0).astype(full)
    resampled = (lat_mine + branch.result()).astype(low)
    latents_grad = out_grad.astype(full) + norm_back(lat_sum.result(), lat_mine, lat_gain)
    return (
        resampled,
        context_grad,
        latents_grad,
        gains[0],
        gains[1],
        q_weight_grad,
        kv_weight_grad,
        out_weight_grad,
    )


def solution(mesh):
    in_specs = (
        P(("dp", "tensor"), None),
        P("dp", None),
        P("dp", None),
        P(),
        P(),
        P("dp", "tensor"),
        P("dp", None),
        P("dp", "tensor"),
        P(("dp", "tensor"), None),
    )
    out_specs = (
        P(("dp", "tensor"), None),
        P(("dp", "tensor"), None),
        P(("dp", "tensor"), None),
        P(("dp", "tensor")),
        P(("dp", "tensor")),
        P("dp", "tensor"),
        P(("dp", "tensor"), None),
        P("dp", "tensor"),
    )
    return jax.shard_map(
        per_device, mesh=mesh, in_specs=in_specs, out_specs=out_specs, check_vma=False
    )
```

```python
import math

import jax
import jax.numpy as jnp
from jax import lax
from jax.experimental import pallas as pl
from jax.experimental.pallas import tpu as pltpu
from jax.sharding import PartitionSpec as P

QUERY_HEADS = 32
KEY_VALUE_HEADS = 4
HEAD_SIZE = 128
LAT = 64
IMG_GRP = 4
GROUPED = QUERY_HEADS // KEY_VALUE_HEADS

norm_eps = 1e-06
scale = HEAD_SIZE ** (-0.5)
scale_log2 = scale * math.log2(math.e)
low = jnp.bfloat16
full = jnp.float32
CHUNK = 256
HINT = 1
VMEM_BYTES = 48 * 1024 * 1024


def dot_nt(a, b):
    return lax.dot_general(a, b, (((1,), (1,)), ((), ())), preferred_element_type=full)


def dot_nn(a, b):
    return lax.dot_general(a, b, (((1,), (0,)), ((), ())), preferred_element_type=full)


def stack_heads(wide):
    return jnp.concatenate(
        [wide[:, h * HEAD_SIZE : (h + 1) * HEAD_SIZE] for h in range(GROUPED)], axis=0
    )


def spread_heads(tall):
    return jnp.concatenate([tall[h * LAT : (h + 1) * LAT] for h in range(GROUPED)], axis=1)


def fwd_kernel(bounds, q_ref, kvp_ref, kvl_ref, o_ref, lse_ref, s_scr, m_scr, l_scr, acc_scr):
    image = pl.program_id(0) * IMG_GRP + pl.program_id(1)
    lo = bounds[0, image]
    hi = bounds[1, image]
    chunks = kvp_ref.shape[1] // CHUNK
    qs = stack_heads(q_ref[...])
    s_lat = dot_nt(kvl_ref[:, :HEAD_SIZE], qs) * scale_log2
    m_scr[...] = jnp.max(s_lat, axis=0, keepdims=True)
    for j in range(chunks):

        @pl.when((lo < (j + 1) * CHUNK) & (hi > j * CHUNK))
        def _():
            keys = kvp_ref[0, j * CHUNK : (j + 1) * CHUNK, :HEAD_SIZE]
            s = dot_nt(keys, qs) * scale_log2
            at = lax.broadcasted_iota(jnp.int32, s.shape, 0) + j * CHUNK
            s = jnp.where((at >= lo) & (at < hi), s, -1e30)
            s_scr[j * CHUNK : (j + 1) * CHUNK, :] = s
            m_scr[...] = jnp.maximum(m_scr[...], jnp.max(s, axis=0, keepdims=True))

    top = m_scr[...]
    p = jnp.exp2(s_lat - top)
    l_scr[...] = jnp.sum(p, axis=0, keepdims=True)
    acc_scr[...] = dot_nn(kvl_ref[:, HEAD_SIZE:].T, p.astype(low))
    for j in range(chunks):

        @pl.when((lo < (j + 1) * CHUNK) & (hi > j * CHUNK))
        def _():
            values = kvp_ref[0, j * CHUNK : (j + 1) * CHUNK, HEAD_SIZE:]
            p = jnp.exp2(s_scr[j * CHUNK : (j + 1) * CHUNK, :] - top)
            l_scr[...] += jnp.sum(p, axis=0, keepdims=True)
            acc_scr[...] += dot_nn(values.T, p.astype(low))

    total = l_scr[...]
    lse_ref[0] = top + jnp.log2(total)
    o_ref[...] = spread_heads((acc_scr[...] / total).T).astype(low)


def bwd_kernel(
    bounds, q_ref, do_ref, kvp_ref, kvl_ref, lse_ref,
    dq_ref, dkvp_ref, dkvl_ref,
    p_scr, dp_scr, dkv_scr, dl_scr, dq_scr,
):
    i = pl.program_id(1)
    image = pl.program_id(0) * IMG_GRP + i
    lo = bounds[0, image]
    hi = bounds[1, image]
    chunks = kvp_ref.shape[1] // CHUNK
    qs = stack_heads(q_ref[...])
    dos = stack_heads(do_ref[...])
    lse = lse_ref[0]

    @pl.when(i == 0)
    def _():
        dkv_scr[...] = jnp.zeros_like(dkv_scr)

    k_lat = kvl_ref[:, :HEAD_SIZE]
    p_lat = jnp.exp2(dot_nt(k_lat, qs) * scale_log2 - lse)
    dp_lat = dot_nt(kvl_ref[:, HEAD_SIZE:], dos)
    dl_scr[...] = jnp.sum(p_lat * dp_lat, axis=0, keepdims=True)
    for j in range(chunks):

        @pl.when((lo < (j + 1) * CHUNK) & (hi > j * CHUNK))
        def _():
            rows = slice(j * CHUNK, (j + 1) * CHUNK)
            s = dot_nt(kvp_ref[0, rows, :HEAD_SIZE], qs) * scale_log2
            at = lax.broadcasted_iota(jnp.int32, s.shape, 0) + j * CHUNK
            s = jnp.where((at >= lo) & (at < hi), s - lse, -1e30)
            p = jnp.exp2(s)
            dp = dot_nt(kvp_ref[0, rows, HEAD_SIZE:], dos)
            dl_scr[...] += jnp.sum(p * dp, axis=0, keepdims=True)
            p_scr[rows, :] = p
            dp_scr[rows, :] = dp

    delta = dl_scr[...]
    ds_lat = (p_lat * (dp_lat - delta) * scale).astype(low)
    dq_scr[...] = dot_nn(k_lat.T, ds_lat)
    dkvl_ref[:, :HEAD_SIZE] = dot_nn(ds_lat, qs).astype(low)
    dkvl_ref[:, HEAD_SIZE:] = dot_nn(p_lat.astype(low), dos).astype(low)
    for j in range(chunks):

        @pl.when((lo < (j + 1) * CHUNK) & (hi > j * CHUNK))
        def _():
            rows = slice(j * CHUNK, (j + 1) * CHUNK)
            p = p_scr[rows, :]
            ds = (p * (dp_scr[rows, :] - delta) * scale).astype(low)
            dq_scr[...] += dot_nn(kvp_ref[0, rows, :HEAD_SIZE].T, ds)
            dkv_scr[rows, :HEAD_SIZE] += dot_nn(ds, qs)
            dkv_scr[rows, HEAD_SIZE:] += dot_nn(p.astype(low), dos)

    dq_ref[...] = spread_heads(dq_scr[...].T).astype(low)

    @pl.when(i == IMG_GRP - 1)
    def _():
        dkvp_ref[0] = dkv_scr[...].astype(low)


def attention_specs(groups, patches, heads_width):
    rows = pl.BlockSpec((LAT, heads_width), lambda g, i, b: (g * IMG_GRP + i, 0))
    kvp = pl.BlockSpec((1, patches, 2 * HEAD_SIZE), lambda g, i, b: (g, 0, 0))
    kvl = pl.BlockSpec((LAT, 2 * HEAD_SIZE), lambda g, i, b: (g * IMG_GRP + i, 0))
    lse = pl.BlockSpec((1, 1, GROUPED * LAT), lambda g, i, b: (g * IMG_GRP + i, 0, 0))
    return rows, kvp, kvl, lse


def attend(bounds, q, kvp, kvl):
    groups, patches, _ = kvp.shape
    rows, kvp_spec, kvl_spec, lse_spec = attention_specs(groups, patches, q.shape[1])
    wide = GROUPED * LAT
    return pl.pallas_call(
        fwd_kernel,
        grid_spec=pltpu.PrefetchScalarGridSpec(
            num_scalar_prefetch=1,
            grid=(groups, IMG_GRP),
            in_specs=[rows, kvp_spec, kvl_spec],
            out_specs=[rows, lse_spec],
            scratch_shapes=[
                pltpu.VMEM((patches, wide), full),
                pltpu.VMEM((1, wide), full),
                pltpu.VMEM((1, wide), full),
                pltpu.VMEM((HEAD_SIZE, wide), full),
            ],
        ),
        out_shape=[
            jax.ShapeDtypeStruct(q.shape, low),
            jax.ShapeDtypeStruct((groups * IMG_GRP, 1, wide), full),
        ],
        compiler_params=pltpu.CompilerParams(vmem_limit_bytes=VMEM_BYTES),
        cost_estimate=pl.CostEstimate(
            flops=2 * 2 * groups * IMG_GRP * wide * patches * HEAD_SIZE // HINT,
            bytes_accessed=(4 * q.size + 2 * kvp.size) // HINT,
            transcendentals=groups * IMG_GRP * wide * patches // HINT,
        ),
        name="attention_forward",
    )(bounds, q, kvp, kvl)


def attend_back(bounds, q, d_out, kvp, kvl, lse):
    groups, patches, _ = kvp.shape
    rows, kvp_spec, kvl_spec, lse_spec = attention_specs(groups, patches, q.shape[1])
    wide = GROUPED * LAT
    return pl.pallas_call(
        bwd_kernel,
        grid_spec=pltpu.PrefetchScalarGridSpec(
            num_scalar_prefetch=1,
            grid=(groups, IMG_GRP),
            in_specs=[rows, rows, kvp_spec, kvl_spec, lse_spec],
            out_specs=[rows, kvp_spec, kvl_spec],
            scratch_shapes=[
                pltpu.VMEM((patches, wide), full),
                pltpu.VMEM((patches, wide), full),
                pltpu.VMEM((patches, 2 * HEAD_SIZE), full),
                pltpu.VMEM((1, wide), full),
                pltpu.VMEM((HEAD_SIZE, wide), full),
            ],
        ),
        out_shape=[
            jax.ShapeDtypeStruct(q.shape, low),
            jax.ShapeDtypeStruct(kvp.shape, low),
            jax.ShapeDtypeStruct(kvl.shape, low),
        ],
        compiler_params=pltpu.CompilerParams(vmem_limit_bytes=VMEM_BYTES),
        cost_estimate=pl.CostEstimate(
            flops=2 * 5 * groups * IMG_GRP * wide * patches * HEAD_SIZE // 1000,
            bytes_accessed=(6 * q.size + 4 * kvp.size) // 1000,
            transcendentals=groups * IMG_GRP * wide * patches // 1000,
        ),
        name="attention_backward",
    )(bounds, q, d_out, kvp, kvl, lse)


def dot_tn(a, b):
    return lax.dot_general(a, b, (((0,), (0,)), ((), ())), preferred_element_type=full)


def call(kernel, name, scalars, arrays, in_specs, out_specs, out_shape, scratch, grid, flops, hint=1):
    moved = sum(a.size * a.dtype.itemsize for a in arrays)
    moved += sum(o.size * o.dtype.itemsize for o in out_shape)
    return pl.pallas_call(
        kernel,
        grid_spec=pltpu.PrefetchScalarGridSpec(
            num_scalar_prefetch=len(scalars),
            grid=grid,
            in_specs=in_specs,
            out_specs=out_specs,
            scratch_shapes=scratch,
        ),
        out_shape=out_shape,
        compiler_params=pltpu.CompilerParams(vmem_limit_bytes=VMEM_BYTES),
        cost_estimate=pl.CostEstimate(flops=flops // hint, bytes_accessed=moved // hint, transcendentals=0),
        name=name,
    )(*scalars, *arrays)


def whole(shape):
    return pl.BlockSpec(shape, lambda *_: (0,) * len(shape))


def fetch(offsets, pieces, held, sems):
    total = sum(piece.shape[0] for piece in pieces)
    rows = held.shape[0] // offsets.shape[0]
    assert total == held.shape[0]
    copies = []
    for piece in pieces:
        for first in range(0, piece.shape[0], rows):
            n = len(copies)
            at = pl.multiple_of(offsets[n], rows)
            copies.append(
                pltpu.make_async_copy(
                    piece.at[pl.ds(first, rows)], held.at[pl.ds(at, rows)], sems.at[n]
                )
            )
    for copy in copies:
        copy.start()
    for copy in copies:
        copy.wait()


def rows_kernel(count, offsets, act, *refs):
    pieces, (out, held, sems) = refs[:count], refs[count:]
    fetch(offsets, pieces, held, sems)
    step = 256
    for n in range(0, out.shape[1], step):
        out[:, n : n + step] = dot_nn(act[...], held[:, n : n + step]).astype(out.dtype)


def rows_times_weight(act, weight):
    offsets, pieces = weight
    cols = pieces[0].shape[1]
    rows, features = act.shape
    return call(
        lambda *refs: rows_kernel(len(pieces), *refs),
        "rows_times_weight",
        [offsets],
        [act, *pieces],
        [whole(act.shape)] + [pl.BlockSpec(memory_space=pltpu.HBM)] * len(pieces),
        [whole((rows, cols))],
        [jax.ShapeDtypeStruct((rows, cols), low)],
        [pltpu.VMEM((features, cols), low), pltpu.SemaphoreType.DMA((offsets.shape[0],))],
        (1,),
        2 * rows * features * cols,
    )[0]


def rows_times_kv(act, weight):
    offsets, pieces = weight
    rows, features = act.shape
    cols = pieces[0].shape[1]
    count = len(pieces)

    def kernel(offsets_ref, act_ref, *refs):
        out, held, sems = refs[count:]
        fetch(offsets_ref, refs[:count], held, sems)
        step = 256
        for n in range(0, cols, step):
            out[:, n : n + step] = dot_nn(act_ref[...], held[:, n : n + step]).astype(low)

    return call(
        kernel,
        "rows_times_kv",
        [offsets],
        [act, *pieces],
        [whole(act.shape)] + [pl.BlockSpec(memory_space=pltpu.HBM)] * count,
        [whole((rows, cols)), whole((features, cols))],
        [jax.ShapeDtypeStruct((rows, cols), low), jax.ShapeDtypeStruct((features, cols), low)],
        [pltpu.SemaphoreType.DMA((offsets.shape[0],))],
        (1,),
        2 * rows * features * cols,
    )


def split_features(features, part):
    first = features * part // 8
    return [first, first, features - first, features - first]


def keep_and_send(x, outs, n, step, value):
    a_keep, a_sent, b_keep, b_sent = outs
    quarter = value.shape[0] // 4
    parts = [value[k * quarter : (k + 1) * quarter] for k in range(4)]
    half = a_keep.shape[2]
    if n < half:
        for k in range(2):
            a_keep[k, :, n : n + step] = parts[k]
            a_sent[k, :, n : n + step] = parts[2 + k]
    else:
        span = slice(n - half, n - half + step)
        for g in range(2):
            b_keep[g, :, span] = jnp.where(x == 0, parts[2 * g], parts[2 * g + 1])
            b_sent[g, :, span] = jnp.where(x == 0, parts[2 * g + 1], parts[2 * g])


def heads_kernel(count, offsets, place, act, *refs):
    pieces, outs, (held, sems) = refs[:count], refs[count:-2], refs[-2:]
    fetch(offsets, pieces, held, sems)
    step = 512
    for n in range(0, held.shape[0], step):
        value = dot_nt(act[...], held[n : n + step]).astype(low)
        keep_and_send(place[0], outs, n, step, value)


def heads_times_weight(place, act, weight):
    offsets, pieces = weight
    rows, cols = act.shape
    features = sum(piece.shape[0] for piece in pieces)
    halves = [(2, rows // 4, n) for n in split_features(features, 3)]
    return call(
        lambda *refs: heads_kernel(len(pieces), *refs),
        "heads_times_weight",
        [offsets, place],
        [act, *pieces],
        [whole(act.shape)] + [pl.BlockSpec(memory_space=pltpu.HBM)] * len(pieces),
        [whole(half) for half in halves],
        [jax.ShapeDtypeStruct(half, low) for half in halves],
        [pltpu.VMEM((features, cols), low), pltpu.SemaphoreType.DMA((offsets.shape[0],))],
        (1,),
        2 * rows * features * cols,
        hint=1000,
    )


def lat_back_kernel(count, offsets, place, act, kv_act, kv, lat_a, lat_b, scales, *refs):
    pieces, outs, (gain, held, sems) = refs[:count], refs[count:-3], refs[-3:]
    fetch(offsets, pieces, held, sems)
    step = 512
    scale_rows = scales[:, :1]
    for n in range(0, held.shape[0], step):
        value = dot_nt(act[...], held[n : n + step]) + dot_nt(kv_act[...], kv[n : n + step])
        lat = jnp.concatenate([lat_a[:, n : n + step], lat_b[:, n : n + step]], axis=0)
        unit = lat.astype(full) * scale_rows
        gain[:, n : n + step] = jnp.sum(value * unit, axis=0, keepdims=True)
        keep_and_send(place[0], outs, n, step, value.astype(low))


def lat_back(place, d_queries, weight, d_kv, kv, lat_a, lat_b, scales):
    offsets, pieces = weight
    rows, cols = d_queries.shape
    features = sum(piece.shape[0] for piece in pieces)
    halves = [(2, rows // 4, n) for n in split_features(features, 4)]
    arrays = [d_queries, d_kv, kv, lat_a, lat_b, scales]
    *parts, gain = call(
        lambda *refs: lat_back_kernel(len(pieces), *refs),
        "lat_back",
        [offsets, place],
        [*arrays, *pieces],
        [whole(a.shape) for a in arrays] + [pl.BlockSpec(memory_space=pltpu.HBM)] * len(pieces),
        [whole(half) for half in halves] + [whole((1, features))],
        [jax.ShapeDtypeStruct(half, low) for half in halves] + [jax.ShapeDtypeStruct((1, features), full)],
        [pltpu.VMEM((features, cols), low), pltpu.SemaphoreType.DMA((offsets.shape[0],))],
        (1,),
        2 * rows * features * (cols + kv.shape[1]),
    )
    return parts, gain


BLOCK = 256


def weight_grad(act, heads, blocks):
    rows, cols = heads.shape
    count = blocks.shape[0]

    def kernel(at, act_ref, heads_ref, out):
        out[0] = dot_tn(act_ref[...], heads_ref[...]).astype(low)

    return call(
        kernel,
        "weight_grad",
        [blocks],
        [act, heads],
        [pl.BlockSpec((rows, BLOCK), lambda i, at: (0, at[i])), whole(heads.shape)],
        [pl.BlockSpec((1, BLOCK, cols), lambda i, at: (i, 0, 0))],
        [jax.ShapeDtypeStruct((count, BLOCK, cols), low)],
        [],
        (count,),
        2 * rows * count * BLOCK * cols,
    )[0]


def kv_weight_grad_part(place, ctx_n, d_kv, lat_n, d_kv_lat, blocks):
    rows, cols = d_kv.shape
    count = blocks.shape[0]

    def kernel(at, here, ctx_ref, d_kv_ref, lat_ref, d_lat_ref, out, total):
        total[...] = dot_tn(ctx_ref[...], d_kv_ref[...])
        lat_part = dot_tn(lat_ref[...], d_lat_ref[...])
        first = here[0] * (cols // 2) + here[1] * HEAD_SIZE
        for k in range(2):
            at_k = pl.multiple_of(first + k * (cols // 4), HEAD_SIZE)
            span = pl.ds(at_k, HEAD_SIZE)
            total[:, span] += lat_part[:, k * HEAD_SIZE : (k + 1) * HEAD_SIZE]
        half = total.shape[0] // 2
        for k in range(2):
            at_x = pl.multiple_of((here[0] ^ k) * half, half)
            out[k, 0] = total[pl.ds(at_x, half), :].astype(low)

    block = pl.BlockSpec((rows, BLOCK), lambda i, at, here: (0, at[i]))
    return call(
        kernel,
        "kv_weight_grad",
        [blocks, place],
        [ctx_n, d_kv, lat_n, d_kv_lat],
        [block, whole(d_kv.shape), block, whole(d_kv_lat.shape)],
        [pl.BlockSpec((2, 1, BLOCK // 2, cols), lambda i, at, here: (0, i, 0, 0))],
        [jax.ShapeDtypeStruct((2, count, BLOCK // 2, cols), low)],
        [pltpu.VMEM((BLOCK, cols), full)],
        (count,),
        2 * rows * count * BLOCK * (cols + 2 * HEAD_SIZE),
    )[0]


NORM_ROWS = 64


def norm_rows(sources, gain):
    rows, features = sources[0].shape
    steps = rows // NORM_ROWS
    count = len(sources)

    def kernel(*refs):
        gain_ref, out, scale_out = refs[count:]
        for n in range(count):

            @pl.when(pl.program_id(0) == n)
            def _():
                values = refs[n][...].astype(full)
                scale_rows = lax.rsqrt(jnp.mean(values * values, axis=1, keepdims=True) + norm_eps)
                out[...] = (values * scale_rows * gain_ref[...]).astype(low)
                scale_out[...] = jnp.broadcast_to(scale_rows, scale_out.shape)

    def source_spec(n):
        return pl.BlockSpec(
            (NORM_ROWS, features), lambda s, i: (jnp.where(s == n, i, 0), 0)
        )

    return call(
        kernel,
        "norm_rows",
        [],
        [*sources, gain[None]],
        [source_spec(n) for n in range(count)] + [whole((1, features))],
        [
            pl.BlockSpec((NORM_ROWS, features), lambda s, i: (s * steps + i, 0)),
            pl.BlockSpec((NORM_ROWS, 128), lambda s, i: (s * steps + i, 0)),
        ],
        [
            jax.ShapeDtypeStruct((count * rows, features), low),
            jax.ShapeDtypeStruct((count * rows, 128), full),
        ],
        [],
        (count, steps),
        4 * count * rows * features,
        hint=1,
    )


def ctx_back(d_kv, full_kv, context, scales, gain):
    rows, cols = d_kv.shape
    features = full_kv.shape[0]
    step = 128

    def kernel(d_ref, kv_ref, ctx_ref, scale_ref, gain_ref, out, gain_out):
        @pl.when(pl.program_id(0) == 0)
        def _():
            gain_out[...] = jnp.zeros_like(gain_out)

        d = dot_nt(d_ref[...], kv_ref[...])
        scale_rows = scale_ref[:, :1]
        unit = ctx_ref[...].astype(full) * scale_rows
        weighted = d * unit
        gain_out[...] += jnp.sum(weighted, axis=0, keepdims=True)
        inner = jnp.mean(weighted * gain_ref[...], axis=1, keepdims=True)
        out[...] = scale_rows * (d * gain_ref[...] - unit * inner)

    return call(
        kernel,
        "ctx_back",
        [],
        [d_kv, full_kv, context, scales, gain[None]],
        [
            pl.BlockSpec((step, cols), lambda i: (i, 0)),
            whole(full_kv.shape),
            pl.BlockSpec((step, features), lambda i: (i, 0)),
            pl.BlockSpec((step, 128), lambda i: (i, 0)),
            whole((1, features)),
        ],
        [pl.BlockSpec((step, features), lambda i: (i, 0)), whole((1, features))],
        [jax.ShapeDtypeStruct((rows, features), full), jax.ShapeDtypeStruct((1, features), full)],
        [],
        (rows // step,),
        2 * rows * cols * features,
        hint=1,
    )


def after(value, *earlier):
    if not earlier:
        return value
    return lax.optimization_barrier((value, *earlier))[0]


class Place:
    def __init__(self):
        dp = lax.axis_size("dp")
        me = lax.axis_index("dp")
        self.dp = dp
        self.depth = dp // 4
        self.z = me // 4
        self.y = (me // 2) % 2
        self.c = me % 2
        self.x = lax.axis_index("tensor")
        self.scalars = jnp.stack([self.x, self.y]).astype(jnp.int32)
        self.perm_core = [(i, i ^ 1) for i in range(dp)]
        self.perm_y = [(i, i ^ 2) for i in range(dp)]
        self.perm_ring = [(i, (i + 4) % dp) for i in range(dp)]
        self.y_groups = [[i for i in range(dp) if (i // 2) % 2 == y] for y in range(2)]
        self.z_groups = [list(range(k, dp, 4)) for k in range(4)]
        self.manual = self.depth == 4

    def over_core(self, v):
        return lax.ppermute(v, "dp", self.perm_core)

    def over_y(self, v):
        return lax.ppermute(v, "dp", self.perm_y)

    def over_x(self, v):
        return lax.ppermute(v, "tensor", [(0, 1), (1, 0)])

    def ring(self, v, *earlier):
        return lax.ppermute(after(v, *earlier), "dp", self.perm_ring)

    def shift(self, v, r):
        return lax.ppermute(v, "dp", [(i, (i + 4 * r) % self.dp) for i in range(self.dp)])

    def row_blocks(self):
        return [
            (z * 2 + (self.y ^ y_other)) * 2 + c
            for z in range(self.depth)
            for c in range(2)
            for y_other in range(2)
        ]

    def block(self, r, y_other, c_other):
        z = (self.z - r) % self.depth
        return (z * 2 + (self.y ^ y_other)) * 2 + (self.c ^ c_other)


def ordered(at, mine, other, axis):
    first = jnp.where(at == 0, mine, other)
    second = jnp.where(at == 0, other, mine)
    return jnp.concatenate([first, second], axis=axis)


def pick(v, at, axis):
    return lax.dynamic_index_in_dim(v, at, axis, keepdims=False)


def add(a, b):
    return a.astype(full) + b.astype(full)


def group_cols(v, x):
    half = v.shape[1] // 2
    return lax.dynamic_slice_in_dim(v, x * half, half, 1)


def head_cols(v, y):
    keys = lax.dynamic_slice_in_dim(v, y * HEAD_SIZE, HEAD_SIZE, 1)
    values = lax.dynamic_slice_in_dim(v, (2 + y) * HEAD_SIZE, HEAD_SIZE, 1)
    return jnp.concatenate([keys, values], axis=1)


def join_heads(y, mine, other):
    first = jnp.where(y == 0, mine, other)
    second = jnp.where(y == 0, other, mine)
    return jnp.concatenate(
        [
            first[:, :HEAD_SIZE],
            second[:, :HEAD_SIZE],
            first[:, HEAD_SIZE:],
            second[:, HEAD_SIZE:],
        ],
        axis=1,
    )


class WeightBlock:
    def __init__(self, here, weight):
        self.here = here
        self.rows, cols = weight.shape
        half = cols // 2
        if not here.manual:
            held = lax.all_gather(weight, "dp", axis=0, tiled=True)
            self.from_y = lax.dynamic_slice_in_dim(held, here.y * half, half, 1)
            return
        mine = lax.dynamic_slice_in_dim(weight, here.y * half, half, 1)
        sent = lax.dynamic_slice_in_dim(weight, (1 - here.y) * half, half, 1)
        self.from_y = here.over_y(sent)
        self.block = jnp.concatenate([mine, self.from_y], axis=0)

    def result(self, *wait):
        here = self.here
        if not here.manual:
            return jnp.zeros((1,), jnp.int32), [self.from_y]
        held = lax.all_gather(
            after(self.block, *wait), "dp", axis=0, tiled=True, axis_index_groups=here.y_groups
        )
        offsets = [row * self.rows for row in here.row_blocks()]
        return jnp.stack(offsets).astype(jnp.int32), [held]


class GatherKv:
    def __init__(self, here, weight):
        self.here = here
        self.rows = weight.shape[0] // 2
        if here.manual:
            mine = lax.dynamic_slice_in_dim(weight, here.x * self.rows, self.rows, 0)
            self.first = [here.shift(mine, r) for r in (1, 3, 2)]
            self.held = jnp.concatenate([mine] + [self.first[k] for k in (0, 2, 1)], axis=0)
        else:
            self.held = lax.all_gather(weight, "dp", axis=0, tiled=True)
            self.first = [self.held]

    def over_y(self, *wait):
        if self.here.manual:
            from_y = self.here.over_y(after(self.held, *wait))
            self.near = jnp.concatenate([self.held, from_y], axis=0)
            return from_y
        return self.held

    def over_x(self, *wait):
        if self.here.manual:
            self.far = self.here.over_x(after(self.near, *wait))
            return self.far
        return self.held

    def result(self, *wait):
        here = self.here
        if not here.manual:
            return jnp.zeros((1,), jnp.int32), [self.held]
        pieces = [self.near, self.far]
        pieces += [here.over_core(self.near), here.over_core(after(self.far, *wait))]
        offsets = [
            here.block(r, y, c) * 2 * self.rows + (here.x ^ x) * self.rows
            for c in range(2)
            for x in range(2)
            for y in range(2)
            for r in range(4)
        ]
        return jnp.stack(offsets).astype(jnp.int32), pieces


def scatter_rows_of_y(here, act, heads):
    cols = heads.shape[1]
    features = act.shape[1]
    if here.manual:
        blocks = here.row_blocks()[::2]
        part = weight_grad(act, heads, jnp.stack(blocks).astype(jnp.int32))
    else:
        part = weight_grad(act, heads, jnp.arange(features // BLOCK, dtype=jnp.int32))
        part = pick(part.reshape(here.depth, 2, 2, -1, cols), here.y, 1)
    part = part.reshape(features // 2, cols)
    total = lax.psum_scatter(
        part, "dp", scatter_dimension=0, tiled=True, axis_index_groups=here.y_groups
    )
    return part, total.astype(full)


def scatter_weight(here, act, heads):
    cols = heads.shape[1]
    features = act.shape[1]
    if here.manual:
        part = weight_grad(act, heads, jnp.stack(here.row_blocks()).astype(jnp.int32))
    else:
        part = weight_grad(act, heads, jnp.arange(features // BLOCK, dtype=jnp.int32))
        part = part.reshape(here.depth, 2, 2, -1, cols)
        part = jnp.stack([pick(part, here.y, 1), pick(part, 1 - here.y, 1)], axis=2)
    part = part.reshape(features, cols)
    total = lax.psum_scatter(
        part, "dp", scatter_dimension=0, tiled=True, axis_index_groups=here.y_groups
    )

    def result(*wait):
        own, other = jnp.split(after(total, *wait), 2, axis=0)
        from_y = here.over_y(other)
        return ordered(here.y, own.astype(full), from_y.astype(full), 1), from_y

    return part, result


class ScatterKv:
    def __init__(self, here, ctx_n, d_kv, lat_n, d_kv_lat):
        self.here = here
        self.cols = d_kv.shape[1]
        self.args = (ctx_n, d_kv, lat_n, d_kv_lat)
        if not here.manual:
            every = jnp.arange(ctx_n.shape[1] // BLOCK, dtype=jnp.int32)
            part = kv_weight_grad_part(here.scalars, *self.args, every)
            part = ordered(here.x, part[0][:, None], part[1][:, None], 1)
            self.other_part = part.reshape(-1, self.cols)
            return
        self.other_part = self.part(d_kv, 1)
        self.received = here.over_core(self.other_part)

    def part(self, d_kv, c_other):
        here = self.here
        ctx_n, _, lat_n, d_kv_lat = self.args
        blocks = [here.block(r, y, c_other) for y in range(2) for r in range(here.depth)]
        blocks = jnp.stack(blocks).astype(jnp.int32)
        part = kv_weight_grad_part(here.scalars, ctx_n, d_kv, lat_n, d_kv_lat, blocks)
        return part.reshape(2, 2, here.depth, BLOCK // 2, self.cols)

    def own(self, *wait):
        self.own_part = self.other_part
        if self.here.manual:
            self.own_part = self.part(after(self.args[1], self.other_part, *wait), 0)

    def start(self, *wait):
        here = self.here
        if not here.manual:
            self.sent = self.first = self.last = [self.other_part]
            total = lax.psum_scatter(
                self.other_part, ("dp", "tensor"), scatter_dimension=0, tiled=True
            )
            self.total = total.astype(full)
            return
        mine, received = self.own_part, self.received
        half = self.cols // 2
        self.sent = [
            add(mine[:, 1, ..., :half], received[:, 1, ..., :half]).astype(low),
            add(mine[1, ..., half:], received[1, ..., half:]).astype(low),
        ]
        self.first = [
            here.over_y(after(self.sent[0], *wait)),
            here.over_x(after(self.sent[1], *wait)),
        ]
        self.halves = [
            add(mine[:, 0, ..., :half], received[:, 0, ..., :half]) + self.first[0],
            add(mine[0, ..., half:], received[0, ..., half:]) + self.first[1],
        ]

    def go_on(self, *wait):
        here = self.here
        if not here.manual:
            return
        a, b = self.halves
        self.last = [
            here.over_x(after(a[1].astype(low), *wait)),
            here.over_y(after(b[1].astype(low), *wait)),
        ]
        a, b = a[0] + self.last[0], b[0] + self.last[1]
        self.total = jnp.concatenate([a, b], axis=-1)

    def result(self, wait, *late):
        here, total = self.here, self.total
        if not here.manual:
            self.over_z = [total]
            return total
        held = [here.shift(after(total[r].astype(low), *wait), -r) for r in (1, 2, 3)]
        self.over_z = held
        return after(total[0], *late) + held[0] + held[1] + held[2]


class ScatterRows:
    def __init__(self, here, a_keep, a_sent, b_keep, b_sent, y_wait=(), x_wait=()):
        self.here = here
        self.keep = [a_keep, b_keep]
        self.first = [here.over_y(after(a_sent, *y_wait)), here.over_x(after(b_sent, *x_wait))]

    def prepare(self, *wait):
        here = self.here
        (a_keep, b_keep), (a, b) = self.keep, [after(v, *wait) for v in self.first]
        self.sent = [
            add(pick(a_keep, 1 - here.x, 0), pick(a, 1 - here.x, 0)).astype(low),
            add(b_keep[1], b[1]).astype(low),
        ]

    def finish(self, x_wait=(), y_wait=()):
        here = self.here
        self.last = [
            here.over_x(after(self.sent[0], *x_wait)),
            here.over_y(after(self.sent[1], *y_wait)),
        ]

    def result(self, *wait):
        here = self.here
        (a_keep, b_keep), (a, b) = self.keep, self.first
        a_last, b_last = [after(v, *wait) for v in self.last]
        a = add(pick(a_keep, here.x, 0), pick(a, here.x, 0)) + a_last
        b = add(b_keep[0], b[0]) + b_last
        return jnp.concatenate([a, b], axis=-1)


def gather_gains(here, part):
    if not here.manual:
        return part
    part = part.reshape(2, here.depth, 2, 2, 2, -1)
    part = pick(part, here.c, 3) + here.over_core(pick(part, 1 - here.c, 3))
    mine = [pick(part, (here.z - r) % here.depth, 1) for r in range(4)]
    return mine[0] + here.shift(mine[1], -1) + here.shift(mine[2], -2) + here.shift(mine[3], -3)


def scatter_gains(here, part):
    if not here.manual:
        devices = here.dp * 2
        part = part.reshape(2, devices, -1).swapaxes(0, 1)
        return lax.psum_scatter(part, ("dp", "tensor"), scatter_dimension=0)
    part = pick(part, here.x, 2) + here.over_x(pick(part, 1 - here.x, 2))
    return pick(part, here.y, 1) + here.over_y(pick(part, 1 - here.y, 1))


def norm_back(grad_rows, values, gain):
    scale_rows = lax.rsqrt(jnp.mean(values * values, axis=-1, keepdims=True) + norm_eps)
    unit_rows = values * scale_rows
    grad_unit = grad_rows * gain
    inner = jnp.mean(grad_unit * unit_rows, axis=-1, keepdims=True)
    return scale_rows * (grad_unit - unit_rows * inner)


def per_device(
    context, latents, lengths, ctx_gain, lat_gain, q_weight, key_value_weight, out_weight, out_grad
):
    here = Place()
    group_rows = latents.shape[0]
    my_rows = group_rows // 2
    features = context.shape[1]
    patch_rows = context.shape[0]

    kv = GatherKv(here, key_value_weight)
    lengths_y = here.over_y(lengths)
    q_block = WeightBlock(here, q_weight)
    out_block = WeightBlock(here, out_weight)
    full_q = q_block.result(*kv.first, lengths_y, out_block.from_y)
    first = [q_block.from_y, out_block.from_y, *kv.first]
    kv_from_y = kv.over_y(*first)
    grad_x = here.over_x(after(out_grad, *first))
    ctx_n, ctx_scales = norm_rows([after(context, *first)], ctx_gain)
    second = [kv_from_y, grad_x, ctx_n]
    kv_from_x = kv.over_x(*second)
    lat_other = here.over_y(after(latents, *second))
    full_kv = kv.result(lat_other)
    full_out = out_block.result(full_q[1][0], *full_kv[1][-2:], lat_other)
    both_lengths = jnp.concatenate([lengths, lengths_y], axis=0)
    ends = jnp.cumsum(both_lengths, axis=1)
    bounds = jnp.stack([(ends - both_lengths).reshape(-1), ends.reshape(-1)])

    kv_mine, kv_weight = rows_times_kv(ctx_n, full_kv)
    own_kv = head_cols(group_cols(kv_weight, here.x), here.y)
    kv_x = here.over_x(group_cols(kv_mine, 1 - here.x))
    grad_y_a = here.over_y(after(grad_x, lat_other, kv_from_x))
    lat_n, lat_scales = norm_rows([latents, after(lat_other, kv_mine, grad_y_a)], lat_gain)
    by_x = ordered(here.x, group_cols(kv_mine, here.x), kv_x, 0)
    kv_y = here.over_y(after(head_cols(by_x, 1 - here.y), lat_n, full_q[1][0]))
    kv_patch = jnp.stack([head_cols(by_x, here.y), kv_y])
    grad_y_b = here.over_y(after(out_grad, kv_y))

    kv_latent = jnp.dot(lat_n, own_kv, preferred_element_type=full).astype(low)
    queries = rows_times_weight(lat_n, full_q)

    mixed, lse = attend(bounds, queries, kv_patch, kv_latent)
    grad_all = jnp.stack([out_grad, grad_x, after(grad_y_b, mixed), after(grad_y_a, mixed)])
    grad_all = grad_all.reshape(2, 2, my_rows, features)
    grad_all = ordered(here.x, grad_all[:, :1], grad_all[:, 1:], 1)
    grad_all = grad_all.reshape(2 * group_rows, features)
    out_part, out_result = scatter_weight(here, grad_all, mixed)
    d_mixed = rows_times_weight(after(grad_all, out_part), full_out)
    d_queries, d_kv_patch, d_kv_latent = attend_back(
        bounds, queries, d_mixed, kv_patch, kv_latent, lse
    )
    d_group_y = here.over_y(d_kv_patch[1])
    branch_parts = heads_times_weight(here.scalars, after(mixed, d_queries), full_out)
    d_group = join_heads(here.y, d_kv_patch[0], d_group_y).reshape(2, patch_rows, -1)

    d_group_x = here.over_x(after(pick(d_group, 1 - here.x, 0), branch_parts[0]))
    d_kv_mine = ordered(here.x, pick(d_group, here.x, 0), d_group_x, 1)
    d_queries_y = here.over_y(after(d_queries, d_group_y, branch_parts[0]))
    lat_parts, lat_gain_part = lat_back(
        here.scalars, after(d_queries, d_group_y), full_q, d_kv_latent, own_kv,
        latents, lat_other, lat_scales,
    )
    kv_sum = ScatterKv(here, ctx_n, after(d_kv_mine, lat_parts[0]), lat_n, d_kv_latent)
    d_queries_y = jnp.concatenate([d_queries_y[group_rows:], d_queries_y[:group_rows]], axis=0)
    d_queries_all = ordered(here.y, d_queries, d_queries_y, 1)
    kv_sum.own()
    branch = ScatterRows(here, *branch_parts, [d_group_y], [d_group_y])
    q_part, q_weight_grad = scatter_rows_of_y(
        here, after(lat_n, kv_sum.own_part, *branch.first), d_queries_all
    )
    kv_sum.start()
    branch.prepare(*kv_sum.sent)
    branch.finish()
    context_grad, ctx_gain_part = ctx_back(
        after(d_kv_mine, *kv_sum.sent), kv_weight, context, ctx_scales, ctx_gain
    )
    gains = jnp.concatenate([after(ctx_gain_part, *kv_sum.first), lat_gain_part], axis=0)
    gains = gather_gains(here, gains)

    second = [*kv_sum.first, *branch.last, ctx_gain_part]
    lat_sum = ScatterRows(here, *lat_parts, second, second)
    kv_sum.go_on(*second)
    third = [*kv_sum.last, *lat_sum.first]
    kv_weight_grad = kv_sum.result(third, q_weight_grad)
    lat_sum.prepare()
    lat_sum.finish(third, third)
    out_weight_grad, _ = out_result(*third)
    gains = scatter_gains(here, after(gains, *third))
    lat_mine = lax.dynamic_slice_in_dim(latents, here.x * my_rows, my_rows, 0).astype(full)
    resampled = (lat_mine + branch.result()).astype(low)
    latents_grad = out_grad.astype(full) + norm_back(lat_sum.result(), lat_mine, lat_gain)
    return (
        resampled,
        context_grad,
        latents_grad,
        gains[0],
        gains[1],
        q_weight_grad,
        kv_weight_grad,
        out_weight_grad,
    )


def solution(mesh):
    in_specs = (
        P(("dp", "tensor"), None),
        P("dp", None),
        P("dp", None),
        P(),
        P(),
        P("dp", "tensor"),
        P("dp", None),
        P("dp", "tensor"),
        P(("dp", "tensor"), None),
    )
    out_specs = (
        P(("dp", "tensor"), None),
        P(("dp", "tensor"), None),
        P(("dp", "tensor"), None),
        P(("dp", "tensor")),
        P(("dp", "tensor")),
        P("dp", "tensor"),
        P(("dp", "tensor"), None),
        P("dp", "tensor"),
    )
    return jax.shard_map(
        per_device, mesh=mesh, in_specs=in_specs, out_specs=out_specs, check_vma=False
    )
```

```python
import math

import jax
import jax.numpy as jnp
from jax import lax
from jax.experimental import pallas as pl
from jax.experimental.pallas import tpu as pltpu
from jax.sharding import PartitionSpec as P

QUERY_HEADS = 32
KEY_VALUE_HEADS = 4
HEAD_SIZE = 128
LAT = 64
IMG_GRP = 4
GROUPED = QUERY_HEADS // KEY_VALUE_HEADS

norm_eps = 1e-06
scale = HEAD_SIZE ** (-0.5)
scale_log2 = scale * math.log2(math.e)
low = jnp.bfloat16
full = jnp.float32
CHUNK = 256
HINT = 1
VMEM_BYTES = 48 * 1024 * 1024


def dot_nt(a, b):
    return lax.dot_general(a, b, (((1,), (1,)), ((), ())), preferred_element_type=full)


def dot_nn(a, b):
    return lax.dot_general(a, b, (((1,), (0,)), ((), ())), preferred_element_type=full)


def stack_heads(wide):
    return jnp.concatenate(
        [wide[:, h * HEAD_SIZE : (h + 1) * HEAD_SIZE] for h in range(GROUPED)], axis=0
    )


def spread_heads(tall):
    return jnp.concatenate([tall[h * LAT : (h + 1) * LAT] for h in range(GROUPED)], axis=1)


def fwd_kernel(bounds, q_ref, kvp_ref, kvl_ref, o_ref, lse_ref, s_scr, m_scr, l_scr, acc_scr):
    image = pl.program_id(0) * IMG_GRP + pl.program_id(1)
    lo = bounds[0, image]
    hi = bounds[1, image]
    chunks = kvp_ref.shape[1] // CHUNK
    qs = stack_heads(q_ref[...])
    s_lat = dot_nt(kvl_ref[:, :HEAD_SIZE], qs) * scale_log2
    m_scr[...] = jnp.max(s_lat, axis=0, keepdims=True)

    @pl.loop(0, chunks)
    def _(j):
        rows = pl.ds(pl.multiple_of(j * CHUNK, CHUNK), CHUNK)

        @pl.when((lo < (j + 1) * CHUNK) & (hi > j * CHUNK))
        def _():
            keys = kvp_ref[0, rows, :HEAD_SIZE]
            s = dot_nt(keys, qs) * scale_log2
            at = lax.broadcasted_iota(jnp.int32, s.shape, 0) + j * CHUNK
            s = jnp.where((at >= lo) & (at < hi), s, -1e30)
            s_scr[rows, :] = s
            m_scr[...] = jnp.maximum(m_scr[...], jnp.max(s, axis=0, keepdims=True))

    top = m_scr[...]
    p = jnp.exp2(s_lat - top)
    l_scr[...] = jnp.sum(p, axis=0, keepdims=True)
    acc_scr[...] = dot_nn(kvl_ref[:, HEAD_SIZE:].T, p.astype(low))

    @pl.loop(0, chunks)
    def _(j):
        rows = pl.ds(pl.multiple_of(j * CHUNK, CHUNK), CHUNK)

        @pl.when((lo < (j + 1) * CHUNK) & (hi > j * CHUNK))
        def _():
            values = kvp_ref[0, rows, HEAD_SIZE:]
            p = jnp.exp2(s_scr[rows, :] - top)
            l_scr[...] += jnp.sum(p, axis=0, keepdims=True)
            acc_scr[...] += dot_nn(values.T, p.astype(low))

    total = l_scr[...]
    lse_ref[0] = top + jnp.log2(total)
    o_ref[...] = spread_heads((acc_scr[...] / total).T).astype(low)


def bwd_kernel(
    bounds, q_ref, do_ref, kvp_ref, kvl_ref, lse_ref,
    dq_ref, dkvp_ref, dkvl_ref,
    p_scr, dp_scr, dkv_scr, dl_scr, dq_scr,
):
    i = pl.program_id(1)
    image = pl.program_id(0) * IMG_GRP + i
    lo = bounds[0, image]
    hi = bounds[1, image]
    chunks = kvp_ref.shape[1] // CHUNK
    qs = stack_heads(q_ref[...])
    dos = stack_heads(do_ref[...])
    lse = lse_ref[0]

    @pl.when(i == 0)
    def _():
        dkv_scr[...] = jnp.zeros_like(dkv_scr)

    k_lat = kvl_ref[:, :HEAD_SIZE]
    p_lat = jnp.exp2(dot_nt(k_lat, qs) * scale_log2 - lse)
    dp_lat = dot_nt(kvl_ref[:, HEAD_SIZE:], dos)
    dl_scr[...] = jnp.sum(p_lat * dp_lat, axis=0, keepdims=True)

    @pl.loop(0, chunks)
    def _(j):
        rows = pl.ds(pl.multiple_of(j * CHUNK, CHUNK), CHUNK)

        @pl.when((lo < (j + 1) * CHUNK) & (hi > j * CHUNK))
        def _():
            s = dot_nt(kvp_ref[0, rows, :HEAD_SIZE], qs) * scale_log2
            at = lax.broadcasted_iota(jnp.int32, s.shape, 0) + j * CHUNK
            s = jnp.where((at >= lo) & (at < hi), s - lse, -1e30)
            p = jnp.exp2(s)
            dp = dot_nt(kvp_ref[0, rows, HEAD_SIZE:], dos)
            dl_scr[...] += jnp.sum(p * dp, axis=0, keepdims=True)
            p_scr[rows, :] = p
            dp_scr[rows, :] = dp

    delta = dl_scr[...]
    ds_lat = (p_lat * (dp_lat - delta) * scale).astype(low)
    dq_scr[...] = dot_nn(k_lat.T, ds_lat)
    dkvl_ref[:, :HEAD_SIZE] = dot_nn(ds_lat, qs).astype(low)
    dkvl_ref[:, HEAD_SIZE:] = dot_nn(p_lat.astype(low), dos).astype(low)

    @pl.loop(0, chunks)
    def _(j):
        rows = pl.ds(pl.multiple_of(j * CHUNK, CHUNK), CHUNK)

        @pl.when((lo < (j + 1) * CHUNK) & (hi > j * CHUNK))
        def _():
            p = p_scr[rows, :]
            ds = (p * (dp_scr[rows, :] - delta) * scale).astype(low)
            dq_scr[...] += dot_nn(kvp_ref[0, rows, :HEAD_SIZE].T, ds)
            dkv_scr[rows, :HEAD_SIZE] += dot_nn(ds, qs)
            dkv_scr[rows, HEAD_SIZE:] += dot_nn(p.astype(low), dos)

    dq_ref[...] = spread_heads(dq_scr[...].T).astype(low)

    @pl.when(i == IMG_GRP - 1)
    def _():
        dkvp_ref[0] = dkv_scr[...].astype(low)


def attention_specs(groups, patches, heads_width):
    rows = pl.BlockSpec((LAT, heads_width), lambda g, i, b: (g * IMG_GRP + i, 0))
    kvp = pl.BlockSpec((1, patches, 2 * HEAD_SIZE), lambda g, i, b: (g, 0, 0))
    kvl = pl.BlockSpec((LAT, 2 * HEAD_SIZE), lambda g, i, b: (g * IMG_GRP + i, 0))
    lse = pl.BlockSpec((1, 1, GROUPED * LAT), lambda g, i, b: (g * IMG_GRP + i, 0, 0))
    return rows, kvp, kvl, lse


def attend(bounds, q, kvp, kvl):
    groups, patches, _ = kvp.shape
    rows, kvp_spec, kvl_spec, lse_spec = attention_specs(groups, patches, q.shape[1])
    wide = GROUPED * LAT
    return pl.pallas_call(
        fwd_kernel,
        grid_spec=pltpu.PrefetchScalarGridSpec(
            num_scalar_prefetch=1,
            grid=(groups, IMG_GRP),
            in_specs=[rows, kvp_spec, kvl_spec],
            out_specs=[rows, lse_spec],
            scratch_shapes=[
                pltpu.VMEM((patches, wide), full),
                pltpu.VMEM((1, wide), full),
                pltpu.VMEM((1, wide), full),
                pltpu.VMEM((HEAD_SIZE, wide), full),
            ],
        ),
        out_shape=[
            jax.ShapeDtypeStruct(q.shape, low),
            jax.ShapeDtypeStruct((groups * IMG_GRP, 1, wide), full),
        ],
        compiler_params=pltpu.CompilerParams(vmem_limit_bytes=VMEM_BYTES),
        cost_estimate=pl.CostEstimate(
            flops=2 * 2 * groups * IMG_GRP * wide * patches * HEAD_SIZE // HINT,
            bytes_accessed=(4 * q.size + 2 * kvp.size) // HINT,
            transcendentals=groups * IMG_GRP * wide * patches // HINT,
        ),
        name="attention_forward",
    )(bounds, q, kvp, kvl)


def attend_back(bounds, q, d_out, kvp, kvl, lse):
    groups, patches, _ = kvp.shape
    rows, kvp_spec, kvl_spec, lse_spec = attention_specs(groups, patches, q.shape[1])
    wide = GROUPED * LAT
    return pl.pallas_call(
        bwd_kernel,
        grid_spec=pltpu.PrefetchScalarGridSpec(
            num_scalar_prefetch=1,
            grid=(groups, IMG_GRP),
            in_specs=[rows, rows, kvp_spec, kvl_spec, lse_spec],
            out_specs=[rows, kvp_spec, kvl_spec],
            scratch_shapes=[
                pltpu.VMEM((patches, wide), full),
                pltpu.VMEM((patches, wide), full),
                pltpu.VMEM((patches, 2 * HEAD_SIZE), full),
                pltpu.VMEM((1, wide), full),
                pltpu.VMEM((HEAD_SIZE, wide), full),
            ],
        ),
        out_shape=[
            jax.ShapeDtypeStruct(q.shape, low),
            jax.ShapeDtypeStruct(kvp.shape, low),
            jax.ShapeDtypeStruct(kvl.shape, low),
        ],
        compiler_params=pltpu.CompilerParams(vmem_limit_bytes=VMEM_BYTES),
        cost_estimate=pl.CostEstimate(
            flops=2 * 5 * groups * IMG_GRP * wide * patches * HEAD_SIZE // 1000,
            bytes_accessed=(6 * q.size + 4 * kvp.size) // 1000,
            transcendentals=groups * IMG_GRP * wide * patches // 1000,
        ),
        name="attention_backward",
    )(bounds, q, d_out, kvp, kvl, lse)


def dot_tn(a, b):
    return lax.dot_general(a, b, (((0,), (0,)), ((), ())), preferred_element_type=full)


def call(kernel, name, scalars, arrays, in_specs, out_specs, out_shape, scratch, grid, flops, hint=1):
    moved = sum(a.size * a.dtype.itemsize for a in arrays)
    moved += sum(o.size * o.dtype.itemsize for o in out_shape)
    return pl.pallas_call(
        kernel,
        grid_spec=pltpu.PrefetchScalarGridSpec(
            num_scalar_prefetch=len(scalars),
            grid=grid,
            in_specs=in_specs,
            out_specs=out_specs,
            scratch_shapes=scratch,
        ),
        out_shape=out_shape,
        compiler_params=pltpu.CompilerParams(vmem_limit_bytes=VMEM_BYTES),
        cost_estimate=pl.CostEstimate(flops=flops // hint, bytes_accessed=moved // hint, transcendentals=0),
        name=name,
    )(*scalars, *arrays)


def whole(shape):
    return pl.BlockSpec(shape, lambda *_: (0,) * len(shape))


def fetch(offsets, pieces, held, sems):
    total = sum(piece.shape[0] for piece in pieces)
    rows = held.shape[0] // offsets.shape[0]
    assert total == held.shape[0]
    copies = []
    for piece in pieces:
        for first in range(0, piece.shape[0], rows):
            n = len(copies)
            at = pl.multiple_of(offsets[n], rows)
            copies.append(
                pltpu.make_async_copy(
                    piece.at[pl.ds(first, rows)], held.at[pl.ds(at, rows)], sems.at[n]
                )
            )
    for copy in copies:
        copy.start()
    for copy in copies:
        copy.wait()


def rows_kernel(count, offsets, act, *refs):
    pieces, (out, held, sems) = refs[:count], refs[count:]
    fetch(offsets, pieces, held, sems)
    step = 512

    @pl.loop(0, out.shape[1] // step)
    def _(n):
        span = pl.ds(pl.multiple_of(n * step, step), step)
        out[:, span] = dot_nn(act[...], held[:, span]).astype(out.dtype)


def rows_times_weight(act, weight):
    offsets, pieces = weight
    cols = pieces[0].shape[1]
    rows, features = act.shape
    return call(
        lambda *refs: rows_kernel(len(pieces), *refs),
        "rows_times_weight",
        [offsets],
        [act, *pieces],
        [whole(act.shape)] + [pl.BlockSpec(memory_space=pltpu.HBM)] * len(pieces),
        [whole((rows, cols))],
        [jax.ShapeDtypeStruct((rows, cols), low)],
        [pltpu.VMEM((features, cols), low), pltpu.SemaphoreType.DMA((offsets.shape[0],))],
        (1,),
        2 * rows * features * cols,
    )[0]


def rows_times_kv(act, weight):
    offsets, pieces = weight
    rows, features = act.shape
    cols = pieces[0].shape[1]
    count = len(pieces)

    def kernel(offsets_ref, act_ref, *refs):
        out, held, sems = refs[count:]
        fetch(offsets_ref, refs[:count], held, sems)
        step = 512

        @pl.loop(0, cols // step)
        def _(n):
            span = pl.ds(pl.multiple_of(n * step, step), step)
            out[:, span] = dot_nn(act_ref[...], held[:, span]).astype(low)

    return call(
        kernel,
        "rows_times_kv",
        [offsets],
        [act, *pieces],
        [whole(act.shape)] + [pl.BlockSpec(memory_space=pltpu.HBM)] * count,
        [whole((rows, cols)), whole((features, cols))],
        [jax.ShapeDtypeStruct((rows, cols), low), jax.ShapeDtypeStruct((features, cols), low)],
        [pltpu.SemaphoreType.DMA((offsets.shape[0],))],
        (1,),
        2 * rows * features * cols,
    )


def split_features(features, part):
    first = features * part // 8
    return [first, first, features - first, features - first]


def keep_and_send(x, outs, held, step, value_of):
    a_keep, a_sent, b_keep, b_sent = outs
    rows, first = a_keep.shape[1], a_keep.shape[2]

    def parts_of(n, start):
        value = value_of(pl.ds(pl.multiple_of(start + n * step, step), step))
        return [value[k * rows : (k + 1) * rows] for k in range(4)]

    @pl.loop(0, first // step)
    def _(n):
        parts = parts_of(n, 0)
        span = pl.ds(pl.multiple_of(n * step, step), step)
        for k in range(2):
            a_keep[k, :, span] = parts[k]
            a_sent[k, :, span] = parts[2 + k]

    @pl.loop(0, (held.shape[0] - first) // step)
    def _(n):
        parts = parts_of(n, first)
        span = pl.ds(pl.multiple_of(n * step, step), step)
        for g in range(2):
            b_keep[g, :, span] = jnp.where(x == 0, parts[2 * g], parts[2 * g + 1])
            b_sent[g, :, span] = jnp.where(x == 0, parts[2 * g + 1], parts[2 * g])


def heads_kernel(count, offsets, place, act, *refs):
    pieces, outs, (held, sems) = refs[:count], refs[count:-2], refs[-2:]
    fetch(offsets, pieces, held, sems)
    keep_and_send(
        place[0], outs, held, 512, lambda span: dot_nt(act[...], held[span, :]).astype(low)
    )


def heads_times_weight(place, act, weight):
    offsets, pieces = weight
    rows, cols = act.shape
    features = sum(piece.shape[0] for piece in pieces)
    halves = [(2, rows // 4, n) for n in split_features(features, 3)]
    return call(
        lambda *refs: heads_kernel(len(pieces), *refs),
        "heads_times_weight",
        [offsets, place],
        [act, *pieces],
        [whole(act.shape)] + [pl.BlockSpec(memory_space=pltpu.HBM)] * len(pieces),
        [whole(half) for half in halves],
        [jax.ShapeDtypeStruct(half, low) for half in halves],
        [pltpu.VMEM((features, cols), low), pltpu.SemaphoreType.DMA((offsets.shape[0],))],
        (1,),
        2 * rows * features * cols,
        hint=1000,
    )


def lat_back_kernel(count, offsets, place, act, kv_act, kv, lat_a, lat_b, scales, *refs):
    pieces, outs, (gain, held, sems) = refs[:count], refs[count:-3], refs[-3:]
    fetch(offsets, pieces, held, sems)

    def value_of(span):
        value = dot_nt(act[...], held[span, :]) + dot_nt(kv_act[...], kv[span, :])
        lat = jnp.concatenate([lat_a[:, span], lat_b[:, span]], axis=0)
        unit = lat.astype(full) * scales[:, :1]
        gain[:, span] = jnp.sum(value * unit, axis=0, keepdims=True)
        return value.astype(low)

    keep_and_send(place[0], outs, held, 512, value_of)


def lat_back(place, d_queries, weight, d_kv, kv, lat_a, lat_b, scales):
    offsets, pieces = weight
    rows, cols = d_queries.shape
    features = sum(piece.shape[0] for piece in pieces)
    halves = [(2, rows // 4, n) for n in split_features(features, 4)]
    arrays = [d_queries, d_kv, kv, lat_a, lat_b, scales]
    *parts, gain = call(
        lambda *refs: lat_back_kernel(len(pieces), *refs),
        "lat_back",
        [offsets, place],
        [*arrays, *pieces],
        [whole(a.shape) for a in arrays] + [pl.BlockSpec(memory_space=pltpu.HBM)] * len(pieces),
        [whole(half) for half in halves] + [whole((1, features))],
        [jax.ShapeDtypeStruct(half, low) for half in halves] + [jax.ShapeDtypeStruct((1, features), full)],
        [pltpu.VMEM((features, cols), low), pltpu.SemaphoreType.DMA((offsets.shape[0],))],
        (1,),
        2 * rows * features * (cols + kv.shape[1]),
    )
    return parts, gain


BLOCK = 256


def weight_grad(act, heads, blocks):
    rows, cols = heads.shape
    count = blocks.shape[0]

    def kernel(at, act_ref, heads_ref, out):
        out[0] = dot_tn(act_ref[...], heads_ref[...]).astype(low)

    return call(
        kernel,
        "weight_grad",
        [blocks],
        [act, heads],
        [pl.BlockSpec((rows, BLOCK), lambda i, at: (0, at[i])), whole(heads.shape)],
        [pl.BlockSpec((1, BLOCK, cols), lambda i, at: (i, 0, 0))],
        [jax.ShapeDtypeStruct((count, BLOCK, cols), low)],
        [],
        (count,),
        2 * rows * count * BLOCK * cols,
    )[0]


def kv_weight_grad_part(place, ctx_n, d_kv, lat_n, d_kv_lat, blocks):
    rows, cols = d_kv.shape
    count = blocks.shape[0]

    def kernel(at, here, ctx_ref, d_kv_ref, lat_ref, d_lat_ref, out, total):
        total[...] = dot_tn(ctx_ref[...], d_kv_ref[...])
        lat_part = dot_tn(lat_ref[...], d_lat_ref[...])
        first = here[0] * (cols // 2) + here[1] * HEAD_SIZE
        for k in range(2):
            at_k = pl.multiple_of(first + k * (cols // 4), HEAD_SIZE)
            span = pl.ds(at_k, HEAD_SIZE)
            total[:, span] += lat_part[:, k * HEAD_SIZE : (k + 1) * HEAD_SIZE]
        half = total.shape[0] // 2
        for k in range(2):
            at_x = pl.multiple_of((here[0] ^ k) * half, half)
            out[k, 0] = total[pl.ds(at_x, half), :].astype(low)

    block = pl.BlockSpec((rows, BLOCK), lambda i, at, here: (0, at[i]))
    return call(
        kernel,
        "kv_weight_grad",
        [blocks, place],
        [ctx_n, d_kv, lat_n, d_kv_lat],
        [block, whole(d_kv.shape), block, whole(d_kv_lat.shape)],
        [pl.BlockSpec((2, 1, BLOCK // 2, cols), lambda i, at, here: (0, i, 0, 0))],
        [jax.ShapeDtypeStruct((2, count, BLOCK // 2, cols), low)],
        [pltpu.VMEM((BLOCK, cols), full)],
        (count,),
        2 * rows * count * BLOCK * (cols + 2 * HEAD_SIZE),
    )[0]


NORM_ROWS = 64


def norm_rows(sources, gain):
    rows, features = sources[0].shape
    steps = rows // NORM_ROWS
    count = len(sources)

    def kernel(*refs):
        gain_ref, out, scale_out = refs[count:]
        for n in range(count):

            @pl.when(pl.program_id(0) == n)
            def _():
                values = refs[n][...].astype(full)
                scale_rows = lax.rsqrt(jnp.mean(values * values, axis=1, keepdims=True) + norm_eps)
                out[...] = (values * scale_rows * gain_ref[...]).astype(low)
                scale_out[...] = jnp.broadcast_to(scale_rows, scale_out.shape)

    def source_spec(n):
        return pl.BlockSpec(
            (NORM_ROWS, features), lambda s, i: (jnp.where(s == n, i, 0), 0)
        )

    return call(
        kernel,
        "norm_rows",
        [],
        [*sources, gain[None]],
        [source_spec(n) for n in range(count)] + [whole((1, features))],
        [
            pl.BlockSpec((NORM_ROWS, features), lambda s, i: (s * steps + i, 0)),
            pl.BlockSpec((NORM_ROWS, 128), lambda s, i: (s * steps + i, 0)),
        ],
        [
            jax.ShapeDtypeStruct((count * rows, features), low),
            jax.ShapeDtypeStruct((count * rows, 128), full),
        ],
        [],
        (count, steps),
        4 * count * rows * features,
        hint=1,
    )


def ctx_back(d_kv, full_kv, context, scales, gain):
    rows, cols = d_kv.shape
    features = full_kv.shape[0]
    step = 128

    def kernel(d_ref, kv_ref, ctx_ref, scale_ref, gain_ref, out, gain_out):
        @pl.when(pl.program_id(0) == 0)
        def _():
            gain_out[...] = jnp.zeros_like(gain_out)

        d = dot_nt(d_ref[...], kv_ref[...])
        scale_rows = scale_ref[:, :1]
        unit = ctx_ref[...].astype(full) * scale_rows
        weighted = d * unit
        gain_out[...] += jnp.sum(weighted, axis=0, keepdims=True)
        inner = jnp.mean(weighted * gain_ref[...], axis=1, keepdims=True)
        out[...] = scale_rows * (d * gain_ref[...] - unit * inner)

    return call(
        kernel,
        "ctx_back",
        [],
        [d_kv, full_kv, context, scales, gain[None]],
        [
            pl.BlockSpec((step, cols), lambda i: (i, 0)),
            whole(full_kv.shape),
            pl.BlockSpec((step, features), lambda i: (i, 0)),
            pl.BlockSpec((step, 128), lambda i: (i, 0)),
            whole((1, features)),
        ],
        [pl.BlockSpec((step, features), lambda i: (i, 0)), whole((1, features))],
        [jax.ShapeDtypeStruct((rows, features), full), jax.ShapeDtypeStruct((1, features), full)],
        [],
        (rows // step,),
        2 * rows * cols * features,
        hint=1,
    )


def after(value, *earlier):
    if not earlier:
        return value
    return lax.optimization_barrier((value, *earlier))[0]


class Place:
    def __init__(self):
        dp = lax.axis_size("dp")
        me = lax.axis_index("dp")
        self.dp = dp
        self.depth = dp // 4
        self.z = me // 4
        self.y = (me // 2) % 2
        self.c = me % 2
        self.x = lax.axis_index("tensor")
        self.scalars = jnp.stack([self.x, self.y]).astype(jnp.int32)
        self.perm_core = [(i, i ^ 1) for i in range(dp)]
        self.perm_y = [(i, i ^ 2) for i in range(dp)]
        self.perm_ring = [(i, (i + 4) % dp) for i in range(dp)]
        self.y_groups = [[i for i in range(dp) if (i // 2) % 2 == y] for y in range(2)]
        self.z_groups = [list(range(k, dp, 4)) for k in range(4)]
        self.manual = self.depth == 4

    def over_core(self, v):
        return lax.ppermute(v, "dp", self.perm_core)

    def over_y(self, v):
        return lax.ppermute(v, "dp", self.perm_y)

    def over_x(self, v):
        return lax.ppermute(v, "tensor", [(0, 1), (1, 0)])

    def ring(self, v, *earlier):
        return lax.ppermute(after(v, *earlier), "dp", self.perm_ring)

    def shift(self, v, r):
        return lax.ppermute(v, "dp", [(i, (i + 4 * r) % self.dp) for i in range(self.dp)])

    def row_blocks(self):
        return [
            (z * 2 + (self.y ^ y_other)) * 2 + c
            for z in range(self.depth)
            for c in range(2)
            for y_other in range(2)
        ]

    def block(self, r, y_other, c_other):
        z = (self.z - r) % self.depth
        return (z * 2 + (self.y ^ y_other)) * 2 + (self.c ^ c_other)


def ordered(at, mine, other, axis):
    first = jnp.where(at == 0, mine, other)
    second = jnp.where(at == 0, other, mine)
    return jnp.concatenate([first, second], axis=axis)


def pick(v, at, axis):
    return lax.dynamic_index_in_dim(v, at, axis, keepdims=False)


def add(a, b):
    return a.astype(full) + b.astype(full)


def group_cols(v, x):
    half = v.shape[1] // 2
    return lax.dynamic_slice_in_dim(v, x * half, half, 1)


def head_cols(v, y):
    keys = lax.dynamic_slice_in_dim(v, y * HEAD_SIZE, HEAD_SIZE, 1)
    values = lax.dynamic_slice_in_dim(v, (2 + y) * HEAD_SIZE, HEAD_SIZE, 1)
    return jnp.concatenate([keys, values], axis=1)


def join_heads(y, mine, other):
    first = jnp.where(y == 0, mine, other)
    second = jnp.where(y == 0, other, mine)
    return jnp.concatenate(
        [
            first[:, :HEAD_SIZE],
            second[:, :HEAD_SIZE],
            first[:, HEAD_SIZE:],
            second[:, HEAD_SIZE:],
        ],
        axis=1,
    )


class WeightBlock:
    def __init__(self, here, weight):
        self.here = here
        self.rows, cols = weight.shape
        half = cols // 2
        if not here.manual:
            held = lax.all_gather(weight, "dp", axis=0, tiled=True)
            self.from_y = lax.dynamic_slice_in_dim(held, here.y * half, half, 1)
            return
        mine = lax.dynamic_slice_in_dim(weight, here.y * half, half, 1)
        sent = lax.dynamic_slice_in_dim(weight, (1 - here.y) * half, half, 1)
        self.from_y = here.over_y(sent)
        self.block = jnp.concatenate([mine, self.from_y], axis=0)

    def result(self, *wait):
        here = self.here
        if not here.manual:
            return jnp.zeros((1,), jnp.int32), [self.from_y]
        held = lax.all_gather(
            after(self.block, *wait), "dp", axis=0, tiled=True, axis_index_groups=here.y_groups
        )
        offsets = [row * self.rows for row in here.row_blocks()]
        return jnp.stack(offsets).astype(jnp.int32), [held]


class GatherKv:
    def __init__(self, here, weight):
        self.here = here
        self.rows = weight.shape[0] // 2
        if here.manual:
            mine = lax.dynamic_slice_in_dim(weight, here.x * self.rows, self.rows, 0)
            self.first = [here.shift(mine, r) for r in (1, 3, 2)]
            self.held = jnp.concatenate([mine] + [self.first[k] for k in (0, 2, 1)], axis=0)
        else:
            self.held = lax.all_gather(weight, "dp", axis=0, tiled=True)
            self.first = [self.held]

    def over_y(self, *wait):
        if self.here.manual:
            from_y = self.here.over_y(after(self.held, *wait))
            self.near = jnp.concatenate([self.held, from_y], axis=0)
            return from_y
        return self.held

    def over_x(self, *wait):
        if self.here.manual:
            self.far = self.here.over_x(after(self.near, *wait))
            return self.far
        return self.held

    def result(self, *wait):
        here = self.here
        if not here.manual:
            return jnp.zeros((1,), jnp.int32), [self.held]
        pieces = [self.near, self.far]
        pieces += [here.over_core(self.near), here.over_core(after(self.far, *wait))]
        offsets = [
            here.block(r, y, c) * 2 * self.rows + (here.x ^ x) * self.rows
            for c in range(2)
            for x in range(2)
            for y in range(2)
            for r in range(4)
        ]
        return jnp.stack(offsets).astype(jnp.int32), pieces


def scatter_rows_of_y(here, act, heads):
    cols = heads.shape[1]
    features = act.shape[1]
    if here.manual:
        blocks = here.row_blocks()[::2]
        part = weight_grad(act, heads, jnp.stack(blocks).astype(jnp.int32))
    else:
        part = weight_grad(act, heads, jnp.arange(features // BLOCK, dtype=jnp.int32))
        part = pick(part.reshape(here.depth, 2, 2, -1, cols), here.y, 1)
    part = part.reshape(features // 2, cols)
    total = lax.psum_scatter(
        part, "dp", scatter_dimension=0, tiled=True, axis_index_groups=here.y_groups
    )
    return part, total.astype(full)


def scatter_weight(here, act, heads):
    cols = heads.shape[1]
    features = act.shape[1]
    if here.manual:
        part = weight_grad(act, heads, jnp.stack(here.row_blocks()).astype(jnp.int32))
    else:
        part = weight_grad(act, heads, jnp.arange(features // BLOCK, dtype=jnp.int32))
        part = part.reshape(here.depth, 2, 2, -1, cols)
        part = jnp.stack([pick(part, here.y, 1), pick(part, 1 - here.y, 1)], axis=2)
    part = part.reshape(features, cols)
    total = lax.psum_scatter(
        part, "dp", scatter_dimension=0, tiled=True, axis_index_groups=here.y_groups
    )

    def result(*wait):
        own, other = jnp.split(after(total, *wait), 2, axis=0)
        from_y = here.over_y(other)
        return ordered(here.y, own.astype(full), from_y.astype(full), 1), from_y

    return part, result


class ScatterKv:
    def __init__(self, here, ctx_n, d_kv, lat_n, d_kv_lat):
        self.here = here
        self.cols = d_kv.shape[1]
        self.args = (ctx_n, d_kv, lat_n, d_kv_lat)
        if not here.manual:
            every = jnp.arange(ctx_n.shape[1] // BLOCK, dtype=jnp.int32)
            part = kv_weight_grad_part(here.scalars, *self.args, every)
            part = ordered(here.x, part[0][:, None], part[1][:, None], 1)
            self.other_part = part.reshape(-1, self.cols)
            return
        self.other_part = self.part(d_kv, 1)
        self.received = here.over_core(self.other_part)

    def part(self, d_kv, c_other):
        here = self.here
        ctx_n, _, lat_n, d_kv_lat = self.args
        blocks = [here.block(r, y, c_other) for y in range(2) for r in range(here.depth)]
        blocks = jnp.stack(blocks).astype(jnp.int32)
        part = kv_weight_grad_part(here.scalars, ctx_n, d_kv, lat_n, d_kv_lat, blocks)
        return part.reshape(2, 2, here.depth, BLOCK // 2, self.cols)

    def own(self, *wait):
        self.own_part = self.other_part
        if self.here.manual:
            self.own_part = self.part(after(self.args[1], self.other_part, *wait), 0)

    def start(self, *wait):
        here = self.here
        if not here.manual:
            self.sent = self.first = self.last = [self.other_part]
            total = lax.psum_scatter(
                self.other_part, ("dp", "tensor"), scatter_dimension=0, tiled=True
            )
            self.total = total.astype(full)
            return
        mine, received = self.own_part, self.received
        half = self.cols // 2
        self.sent = [
            add(mine[:, 1, ..., :half], received[:, 1, ..., :half]).astype(low),
            add(mine[1, ..., half:], received[1, ..., half:]).astype(low),
        ]
        self.first = [
            here.over_y(after(self.sent[0], *wait)),
            here.over_x(after(self.sent[1], *wait)),
        ]
        self.halves = [
            add(mine[:, 0, ..., :half], received[:, 0, ..., :half]) + self.first[0],
            add(mine[0, ..., half:], received[0, ..., half:]) + self.first[1],
        ]

    def go_on(self, *wait):
        here = self.here
        if not here.manual:
            return
        a, b = self.halves
        self.last = [
            here.over_x(after(a[1].astype(low), *wait)),
            here.over_y(after(b[1].astype(low), *wait)),
        ]
        a, b = a[0] + self.last[0], b[0] + self.last[1]
        self.total = jnp.concatenate([a, b], axis=-1)

    def result(self, wait, *late):
        here, total = self.here, self.total
        if not here.manual:
            self.over_z = [total]
            return total
        held = [here.shift(after(total[r].astype(low), *wait), -r) for r in (1, 2, 3)]
        self.over_z = held
        return after(total[0], *late) + held[0] + held[1] + held[2]


class ScatterRows:
    def __init__(self, here, a_keep, a_sent, b_keep, b_sent, y_wait=(), x_wait=()):
        self.here = here
        self.keep = [a_keep, b_keep]
        self.first = [here.over_y(after(a_sent, *y_wait)), here.over_x(after(b_sent, *x_wait))]

    def prepare(self, *wait):
        here = self.here
        (a_keep, b_keep), (a, b) = self.keep, [after(v, *wait) for v in self.first]
        self.sent = [
            add(pick(a_keep, 1 - here.x, 0), pick(a, 1 - here.x, 0)).astype(low),
            add(b_keep[1], b[1]).astype(low),
        ]

    def finish(self, x_wait=(), y_wait=()):
        here = self.here
        self.last = [
            here.over_x(after(self.sent[0], *x_wait)),
            here.over_y(after(self.sent[1], *y_wait)),
        ]

    def result(self, *wait):
        here = self.here
        (a_keep, b_keep), (a, b) = self.keep, self.first
        a_last, b_last = [after(v, *wait) for v in self.last]
        a = add(pick(a_keep, here.x, 0), pick(a, here.x, 0)) + a_last
        b = add(b_keep[0], b[0]) + b_last
        return jnp.concatenate([a, b], axis=-1)


def gather_gains(here, part):
    if not here.manual:
        return part
    part = part.reshape(2, here.depth, 2, 2, 2, -1)
    part = pick(part, here.c, 3) + here.over_core(pick(part, 1 - here.c, 3))
    mine = [pick(part, (here.z - r) % here.depth, 1) for r in range(4)]
    return mine[0] + here.shift(mine[1], -1) + here.shift(mine[2], -2) + here.shift(mine[3], -3)


def scatter_gains(here, part):
    if not here.manual:
        devices = here.dp * 2
        part = part.reshape(2, devices, -1).swapaxes(0, 1)
        return lax.psum_scatter(part, ("dp", "tensor"), scatter_dimension=0)
    part = pick(part, here.x, 2) + here.over_x(pick(part, 1 - here.x, 2))
    return pick(part, here.y, 1) + here.over_y(pick(part, 1 - here.y, 1))


def norm_back(grad_rows, values, gain):
    scale_rows = lax.rsqrt(jnp.mean(values * values, axis=-1, keepdims=True) + norm_eps)
    unit_rows = values * scale_rows
    grad_unit = grad_rows * gain
    inner = jnp.mean(grad_unit * unit_rows, axis=-1, keepdims=True)
    return scale_rows * (grad_unit - unit_rows * inner)


def per_device(
    context, latents, lengths, ctx_gain, lat_gain, q_weight, key_value_weight, out_weight, out_grad
):
    here = Place()
    group_rows = latents.shape[0]
    my_rows = group_rows // 2
    features = context.shape[1]
    patch_rows = context.shape[0]

    kv = GatherKv(here, key_value_weight)
    lengths_y = here.over_y(lengths)
    q_block = WeightBlock(here, q_weight)
    out_block = WeightBlock(here, out_weight)
    full_q = q_block.result(*kv.first, lengths_y, out_block.from_y)
    first = [q_block.from_y, out_block.from_y, *kv.first]
    kv_from_y = kv.over_y(*first)
    grad_x = here.over_x(after(out_grad, *first))
    ctx_n, ctx_scales = norm_rows([after(context, *first)], ctx_gain)
    second = [kv_from_y, grad_x, ctx_n]
    kv_from_x = kv.over_x(*second)
    lat_other = here.over_y(after(latents, *second))
    full_kv = kv.result(lat_other)
    full_out = out_block.result(full_q[1][0], *full_kv[1][-2:], lat_other)
    both_lengths = jnp.concatenate([lengths, lengths_y], axis=0)
    ends = jnp.cumsum(both_lengths, axis=1)
    bounds = jnp.stack([(ends - both_lengths).reshape(-1), ends.reshape(-1)])

    kv_mine, kv_weight = rows_times_kv(ctx_n, full_kv)
    own_kv = head_cols(group_cols(kv_weight, here.x), here.y)
    kv_x = here.over_x(group_cols(kv_mine, 1 - here.x))
    grad_y_a = here.over_y(after(grad_x, lat_other, kv_from_x))
    lat_n, lat_scales = norm_rows([latents, after(lat_other, kv_mine, grad_y_a)], lat_gain)
    by_x = ordered(here.x, group_cols(kv_mine, here.x), kv_x, 0)
    kv_y = here.over_y(after(head_cols(by_x, 1 - here.y), lat_n, full_q[1][0]))
    kv_patch = jnp.stack([head_cols(by_x, here.y), kv_y])
    grad_y_b = here.over_y(after(out_grad, kv_y))

    kv_latent = jnp.dot(lat_n, own_kv, preferred_element_type=full).astype(low)
    queries = rows_times_weight(lat_n, full_q)

    mixed, lse = attend(bounds, queries, kv_patch, kv_latent)
    grad_all = jnp.stack([out_grad, grad_x, after(grad_y_b, mixed), after(grad_y_a, mixed)])
    grad_all = grad_all.reshape(2, 2, my_rows, features)
    grad_all = ordered(here.x, grad_all[:, :1], grad_all[:, 1:], 1)
    grad_all = grad_all.reshape(2 * group_rows, features)
    out_part, out_result = scatter_weight(here, grad_all, mixed)
    d_mixed = rows_times_weight(after(grad_all, out_part), full_out)
    d_queries, d_kv_patch, d_kv_latent = attend_back(
        bounds, queries, d_mixed, kv_patch, kv_latent, lse
    )
    d_group_y = here.over_y(d_kv_patch[1])
    branch_parts = heads_times_weight(here.scalars, after(mixed, d_queries), full_out)
    d_group = join_heads(here.y, d_kv_patch[0], d_group_y).reshape(2, patch_rows, -1)

    d_group_x = here.over_x(after(pick(d_group, 1 - here.x, 0), branch_parts[0]))
    d_kv_mine = ordered(here.x, pick(d_group, here.x, 0), d_group_x, 1)
    d_queries_y = here.over_y(after(d_queries, d_group_y, branch_parts[0]))
    lat_parts, lat_gain_part = lat_back(
        here.scalars, after(d_queries, d_group_y), full_q, d_kv_latent, own_kv,
        latents, lat_other, lat_scales,
    )
    kv_sum = ScatterKv(here, ctx_n, after(d_kv_mine, lat_parts[0]), lat_n, d_kv_latent)
    d_queries_y = jnp.concatenate([d_queries_y[group_rows:], d_queries_y[:group_rows]], axis=0)
    d_queries_all = ordered(here.y, d_queries, d_queries_y, 1)
    kv_sum.own()
    branch = ScatterRows(here, *branch_parts, [d_group_y], [d_group_y])
    q_part, q_weight_grad = scatter_rows_of_y(
        here, after(lat_n, kv_sum.own_part, *branch.first), d_queries_all
    )
    kv_sum.start()
    branch.prepare(*kv_sum.sent)
    branch.finish()
    context_grad, ctx_gain_part = ctx_back(
        after(d_kv_mine, *kv_sum.sent), kv_weight, context, ctx_scales, ctx_gain
    )
    gains = jnp.concatenate([after(ctx_gain_part, *kv_sum.first), lat_gain_part], axis=0)
    gains = gather_gains(here, gains)

    second = [*kv_sum.first, *branch.last, ctx_gain_part]
    lat_sum = ScatterRows(here, *lat_parts, second, second)
    kv_sum.go_on(*second)
    third = [*kv_sum.last, *lat_sum.first]
    kv_weight_grad = kv_sum.result(third, q_weight_grad)
    lat_sum.prepare()
    lat_sum.finish(third, third)
    out_weight_grad, _ = out_result(*third)
    gains = scatter_gains(here, after(gains, *third))
    lat_mine = lax.dynamic_slice_in_dim(latents, here.x * my_rows, my_rows, 0).astype(full)
    resampled = (lat_mine + branch.result()).astype(low)
    latents_grad = out_grad.astype(full) + norm_back(lat_sum.result(), lat_mine, lat_gain)
    return (
        resampled,
        context_grad,
        latents_grad,
        gains[0],
        gains[1],
        q_weight_grad,
        kv_weight_grad,
        out_weight_grad,
    )


def solution(mesh):
    in_specs = (
        P(("dp", "tensor"), None),
        P("dp", None),
        P("dp", None),
        P(),
        P(),
        P("dp", "tensor"),
        P("dp", None),
        P("dp", "tensor"),
        P(("dp", "tensor"), None),
    )
    out_specs = (
        P(("dp", "tensor"), None),
        P(("dp", "tensor"), None),
        P(("dp", "tensor"), None),
        P(("dp", "tensor")),
        P(("dp", "tensor")),
        P("dp", "tensor"),
        P(("dp", "tensor"), None),
        P("dp", "tensor"),
    )
    return jax.shard_map(
        per_device, mesh=mesh, in_specs=in_specs, out_specs=out_specs, check_vma=False
    )
```

```python
import math

import jax
import jax.numpy as jnp
from jax import lax
from jax.experimental import pallas as pl
from jax.experimental.pallas import tpu as pltpu
from jax.sharding import PartitionSpec as P

QUERY_HEADS = 32
KEY_VALUE_HEADS = 4
HEAD_SIZE = 128
LAT = 64
IMG_GRP = 4
GROUPED = QUERY_HEADS // KEY_VALUE_HEADS

norm_eps = 1e-06
scale = HEAD_SIZE ** (-0.5)
scale_log2 = scale * math.log2(math.e)
low = jnp.bfloat16
full = jnp.float32
CHUNK = 256
HINT = 1
VMEM_BYTES = 48 * 1024 * 1024


def dot_nt(a, b):
    return lax.dot_general(a, b, (((1,), (1,)), ((), ())), preferred_element_type=full)


def dot_nn(a, b):
    return lax.dot_general(a, b, (((1,), (0,)), ((), ())), preferred_element_type=full)


def stack_heads(wide):
    return jnp.concatenate(
        [wide[:, h * HEAD_SIZE : (h + 1) * HEAD_SIZE] for h in range(GROUPED)], axis=0
    )


def spread_heads(tall):
    return jnp.concatenate([tall[h * LAT : (h + 1) * LAT] for h in range(GROUPED)], axis=1)


def fwd_kernel(bounds, q_ref, kvp_ref, kvl_ref, o_ref, lse_ref, s_scr, m_scr, l_scr, acc_scr):
    image = pl.program_id(0) * IMG_GRP + pl.program_id(1)
    lo = bounds[0, image]
    hi = bounds[1, image]
    chunks = kvp_ref.shape[1] // CHUNK
    qs = stack_heads(q_ref[...])
    s_lat = dot_nt(kvl_ref[:, :HEAD_SIZE], qs) * scale_log2
    m_scr[...] = jnp.max(s_lat, axis=0, keepdims=True)

    @pl.loop(0, chunks)
    def _(j):
        rows = pl.ds(pl.multiple_of(j * CHUNK, CHUNK), CHUNK)

        @pl.when((lo < (j + 1) * CHUNK) & (hi > j * CHUNK))
        def _():
            keys = kvp_ref[0, rows, :HEAD_SIZE]
            s = dot_nt(keys, qs) * scale_log2
            at = lax.broadcasted_iota(jnp.int32, s.shape, 0) + j * CHUNK
            s = jnp.where((at >= lo) & (at < hi), s, -1e30)
            s_scr[rows, :] = s
            m_scr[...] = jnp.maximum(m_scr[...], jnp.max(s, axis=0, keepdims=True))

    top = m_scr[...]
    p = jnp.exp2(s_lat - top)
    l_scr[...] = jnp.sum(p, axis=0, keepdims=True)
    acc_scr[...] = dot_nn(kvl_ref[:, HEAD_SIZE:].T, p.astype(low))

    @pl.loop(0, chunks)
    def _(j):
        rows = pl.ds(pl.multiple_of(j * CHUNK, CHUNK), CHUNK)

        @pl.when((lo < (j + 1) * CHUNK) & (hi > j * CHUNK))
        def _():
            values = kvp_ref[0, rows, HEAD_SIZE:]
            p = jnp.exp2(s_scr[rows, :] - top)
            l_scr[...] += jnp.sum(p, axis=0, keepdims=True)
            acc_scr[...] += dot_nn(values.T, p.astype(low))

    total = l_scr[...]
    lse_ref[0] = top + jnp.log2(total)
    o_ref[...] = spread_heads((acc_scr[...] / total).T).astype(low)


def bwd_kernel(
    bounds, q_ref, do_ref, kvp_ref, kvl_ref, lse_ref,
    dq_ref, dkvp_ref, dkvl_ref,
    p_scr, dp_scr, dkv_scr, dl_scr, dq_scr,
):
    i = pl.program_id(1)
    image = pl.program_id(0) * IMG_GRP + i
    lo = bounds[0, image]
    hi = bounds[1, image]
    chunks = kvp_ref.shape[1] // CHUNK
    qs = stack_heads(q_ref[...])
    dos = stack_heads(do_ref[...])
    lse = lse_ref[0]

    @pl.when(i == 0)
    def _():
        dkv_scr[...] = jnp.zeros_like(dkv_scr)

    k_lat = kvl_ref[:, :HEAD_SIZE]
    p_lat = jnp.exp2(dot_nt(k_lat, qs) * scale_log2 - lse)
    dp_lat = dot_nt(kvl_ref[:, HEAD_SIZE:], dos)
    dl_scr[...] = jnp.sum(p_lat * dp_lat, axis=0, keepdims=True)

    @pl.loop(0, chunks)
    def _(j):
        rows = pl.ds(pl.multiple_of(j * CHUNK, CHUNK), CHUNK)

        @pl.when((lo < (j + 1) * CHUNK) & (hi > j * CHUNK))
        def _():
            s = dot_nt(kvp_ref[0, rows, :HEAD_SIZE], qs) * scale_log2
            at = lax.broadcasted_iota(jnp.int32, s.shape, 0) + j * CHUNK
            s = jnp.where((at >= lo) & (at < hi), s - lse, -1e30)
            p = jnp.exp2(s)
            dp = dot_nt(kvp_ref[0, rows, HEAD_SIZE:], dos)
            dl_scr[...] += jnp.sum(p * dp, axis=0, keepdims=True)
            p_scr[rows, :] = p
            dp_scr[rows, :] = dp

    delta = dl_scr[...]
    ds_lat = (p_lat * (dp_lat - delta) * scale).astype(low)
    dq_scr[...] = dot_nn(k_lat.T, ds_lat)
    dkvl_ref[:, :HEAD_SIZE] = dot_nn(ds_lat, qs).astype(low)
    dkvl_ref[:, HEAD_SIZE:] = dot_nn(p_lat.astype(low), dos).astype(low)

    @pl.loop(0, chunks)
    def _(j):
        rows = pl.ds(pl.multiple_of(j * CHUNK, CHUNK), CHUNK)

        @pl.when((lo < (j + 1) * CHUNK) & (hi > j * CHUNK))
        def _():
            p = p_scr[rows, :]
            ds = (p * (dp_scr[rows, :] - delta) * scale).astype(low)
            dq_scr[...] += dot_nn(kvp_ref[0, rows, :HEAD_SIZE].T, ds)
            dkv_scr[rows, :HEAD_SIZE] += dot_nn(ds, qs)
            dkv_scr[rows, HEAD_SIZE:] += dot_nn(p.astype(low), dos)

    dq_ref[...] = spread_heads(dq_scr[...].T).astype(low)

    @pl.when(i == IMG_GRP - 1)
    def _():
        dkvp_ref[0] = dkv_scr[...].astype(low)


def attention_specs(groups, patches, heads_width):
    rows = pl.BlockSpec((LAT, heads_width), lambda g, i, b: (g * IMG_GRP + i, 0))
    kvp = pl.BlockSpec((1, patches, 2 * HEAD_SIZE), lambda g, i, b: (g, 0, 0))
    kvl = pl.BlockSpec((LAT, 2 * HEAD_SIZE), lambda g, i, b: (g * IMG_GRP + i, 0))
    lse = pl.BlockSpec((1, 1, GROUPED * LAT), lambda g, i, b: (g * IMG_GRP + i, 0, 0))
    return rows, kvp, kvl, lse


def attend(bounds, q, kvp, kvl):
    groups, patches, _ = kvp.shape
    rows, kvp_spec, kvl_spec, lse_spec = attention_specs(groups, patches, q.shape[1])
    wide = GROUPED * LAT
    return pl.pallas_call(
        fwd_kernel,
        grid_spec=pltpu.PrefetchScalarGridSpec(
            num_scalar_prefetch=1,
            grid=(groups, IMG_GRP),
            in_specs=[rows, kvp_spec, kvl_spec],
            out_specs=[rows, lse_spec],
            scratch_shapes=[
                pltpu.VMEM((patches, wide), full),
                pltpu.VMEM((1, wide), full),
                pltpu.VMEM((1, wide), full),
                pltpu.VMEM((HEAD_SIZE, wide), full),
            ],
        ),
        out_shape=[
            jax.ShapeDtypeStruct(q.shape, low),
            jax.ShapeDtypeStruct((groups * IMG_GRP, 1, wide), full),
        ],
        compiler_params=pltpu.CompilerParams(vmem_limit_bytes=VMEM_BYTES),
        cost_estimate=pl.CostEstimate(
            flops=2 * 2 * groups * IMG_GRP * wide * patches * HEAD_SIZE // HINT,
            bytes_accessed=(4 * q.size + 2 * kvp.size) // HINT,
            transcendentals=groups * IMG_GRP * wide * patches // HINT,
        ),
        name="attention_forward",
    )(bounds, q, kvp, kvl)


def attend_back(bounds, q, d_out, kvp, kvl, lse):
    groups, patches, _ = kvp.shape
    rows, kvp_spec, kvl_spec, lse_spec = attention_specs(groups, patches, q.shape[1])
    wide = GROUPED * LAT
    return pl.pallas_call(
        bwd_kernel,
        grid_spec=pltpu.PrefetchScalarGridSpec(
            num_scalar_prefetch=1,
            grid=(groups, IMG_GRP),
            in_specs=[rows, rows, kvp_spec, kvl_spec, lse_spec],
            out_specs=[rows, kvp_spec, kvl_spec],
            scratch_shapes=[
                pltpu.VMEM((patches, wide), full),
                pltpu.VMEM((patches, wide), full),
                pltpu.VMEM((patches, 2 * HEAD_SIZE), full),
                pltpu.VMEM((1, wide), full),
                pltpu.VMEM((HEAD_SIZE, wide), full),
            ],
        ),
        out_shape=[
            jax.ShapeDtypeStruct(q.shape, low),
            jax.ShapeDtypeStruct(kvp.shape, low),
            jax.ShapeDtypeStruct(kvl.shape, low),
        ],
        compiler_params=pltpu.CompilerParams(vmem_limit_bytes=VMEM_BYTES),
        cost_estimate=pl.CostEstimate(
            flops=2 * 5 * groups * IMG_GRP * wide * patches * HEAD_SIZE // 1000,
            bytes_accessed=(6 * q.size + 4 * kvp.size) // 1000,
            transcendentals=groups * IMG_GRP * wide * patches // 1000,
        ),
        name="attention_backward",
    )(bounds, q, d_out, kvp, kvl, lse)


def dot_tn(a, b):
    return lax.dot_general(a, b, (((0,), (0,)), ((), ())), preferred_element_type=full)


def call(kernel, name, scalars, arrays, in_specs, out_specs, out_shape, scratch, grid, flops, hint=1):
    moved = sum(a.size * a.dtype.itemsize for a in arrays)
    moved += sum(o.size * o.dtype.itemsize for o in out_shape)
    return pl.pallas_call(
        kernel,
        grid_spec=pltpu.PrefetchScalarGridSpec(
            num_scalar_prefetch=len(scalars),
            grid=grid,
            in_specs=in_specs,
            out_specs=out_specs,
            scratch_shapes=scratch,
        ),
        out_shape=out_shape,
        compiler_params=pltpu.CompilerParams(vmem_limit_bytes=VMEM_BYTES),
        cost_estimate=pl.CostEstimate(flops=flops // hint, bytes_accessed=moved // hint, transcendentals=0),
        name=name,
    )(*scalars, *arrays)


def whole(shape):
    return pl.BlockSpec(shape, lambda *_: (0,) * len(shape))


def fetch(offsets, pieces, held, sems):
    total = sum(piece.shape[0] for piece in pieces)
    rows = held.shape[0] // offsets.shape[0]
    assert total == held.shape[0]
    copies = []
    for piece in pieces:
        for first in range(0, piece.shape[0], rows):
            n = len(copies)
            at = pl.multiple_of(offsets[n], rows)
            copies.append(
                pltpu.make_async_copy(
                    piece.at[pl.ds(first, rows)], held.at[pl.ds(at, rows)], sems.at[n]
                )
            )
    for copy in copies:
        copy.start()
    for copy in copies:
        copy.wait()


def rows_kernel(count, offsets, act, *refs):
    pieces, (out, held, sems) = refs[:count], refs[count:]
    fetch(offsets, pieces, held, sems)
    step = 512

    @pl.loop(0, out.shape[1] // step)
    def _(n):
        span = pl.ds(pl.multiple_of(n * step, step), step)
        out[:, span] = dot_nn(act[...], held[:, span]).astype(out.dtype)


def rows_times_weight(act, weight):
    offsets, pieces = weight
    cols = pieces[0].shape[1]
    rows, features = act.shape
    return call(
        lambda *refs: rows_kernel(len(pieces), *refs),
        "rows_times_weight",
        [offsets],
        [act, *pieces],
        [whole(act.shape)] + [pl.BlockSpec(memory_space=pltpu.HBM)] * len(pieces),
        [whole((rows, cols))],
        [jax.ShapeDtypeStruct((rows, cols), low)],
        [pltpu.VMEM((features, cols), low), pltpu.SemaphoreType.DMA((offsets.shape[0],))],
        (1,),
        2 * rows * features * cols,
    )[0]


def rows_times_kv(act, weight):
    offsets, pieces = weight
    rows, features = act.shape
    cols = pieces[0].shape[1]
    count = len(pieces)

    def kernel(offsets_ref, act_ref, *refs):
        out, held, sems = refs[count:]
        fetch(offsets_ref, refs[:count], held, sems)
        step = 512

        @pl.loop(0, cols // step)
        def _(n):
            span = pl.ds(pl.multiple_of(n * step, step), step)
            out[:, span] = dot_nn(act_ref[...], held[:, span]).astype(low)

    return call(
        kernel,
        "rows_times_kv",
        [offsets],
        [act, *pieces],
        [whole(act.shape)] + [pl.BlockSpec(memory_space=pltpu.HBM)] * count,
        [whole((rows, cols)), whole((features, cols))],
        [jax.ShapeDtypeStruct((rows, cols), low), jax.ShapeDtypeStruct((features, cols), low)],
        [pltpu.SemaphoreType.DMA((offsets.shape[0],))],
        (1,),
        2 * rows * features * cols,
    )


def split_features(features, part):
    first = features * part // 8
    return [first, first, features - first, features - first]


def keep_and_send(x, outs, held, step, value_of):
    a_keep, a_sent, b_keep, b_sent = outs
    rows, first = a_keep.shape[1], a_keep.shape[2]

    def parts_of(n, start):
        value = value_of(pl.ds(pl.multiple_of(start + n * step, step), step))
        return [value[k * rows : (k + 1) * rows] for k in range(4)]

    @pl.loop(0, first // step)
    def _(n):
        parts = parts_of(n, 0)
        span = pl.ds(pl.multiple_of(n * step, step), step)
        for k in range(2):
            a_keep[k, :, span] = parts[k]
            a_sent[k, :, span] = parts[2 + k]

    @pl.loop(0, (held.shape[0] - first) // step)
    def _(n):
        parts = parts_of(n, first)
        span = pl.ds(pl.multiple_of(n * step, step), step)
        for g in range(2):
            b_keep[g, :, span] = jnp.where(x == 0, parts[2 * g], parts[2 * g + 1])
            b_sent[g, :, span] = jnp.where(x == 0, parts[2 * g + 1], parts[2 * g])


def heads_kernel(count, offsets, place, act, *refs):
    pieces, outs, (held, sems) = refs[:count], refs[count:-2], refs[-2:]
    fetch(offsets, pieces, held, sems)
    keep_and_send(
        place[0], outs, held, 512, lambda span: dot_nt(act[...], held[span, :]).astype(low)
    )


def heads_times_weight(place, act, weight):
    offsets, pieces = weight
    rows, cols = act.shape
    features = sum(piece.shape[0] for piece in pieces)
    halves = [(2, rows // 4, n) for n in split_features(features, 3)]
    return call(
        lambda *refs: heads_kernel(len(pieces), *refs),
        "heads_times_weight",
        [offsets, place],
        [act, *pieces],
        [whole(act.shape)] + [pl.BlockSpec(memory_space=pltpu.HBM)] * len(pieces),
        [whole(half) for half in halves],
        [jax.ShapeDtypeStruct(half, low) for half in halves],
        [pltpu.VMEM((features, cols), low), pltpu.SemaphoreType.DMA((offsets.shape[0],))],
        (1,),
        2 * rows * features * cols,
        hint=1000,
    )


def lat_back_kernel(count, offsets, place, act, kv_act, kv, lat_a, lat_b, scales, *refs):
    pieces, outs, (gain, held, sems) = refs[:count], refs[count:-3], refs[-3:]
    fetch(offsets, pieces, held, sems)

    def value_of(span):
        value = dot_nt(act[...], held[span, :]) + dot_nt(kv_act[...], kv[span, :])
        lat = jnp.concatenate([lat_a[:, span], lat_b[:, span]], axis=0)
        unit = lat.astype(full) * scales[:, :1]
        gain[:, span] = jnp.sum(value * unit, axis=0, keepdims=True)
        return value.astype(low)

    keep_and_send(place[0], outs, held, 512, value_of)


def lat_back(place, d_queries, weight, d_kv, kv, lat_a, lat_b, scales):
    offsets, pieces = weight
    rows, cols = d_queries.shape
    features = sum(piece.shape[0] for piece in pieces)
    halves = [(2, rows // 4, n) for n in split_features(features, 4)]
    arrays = [d_queries, d_kv, kv, lat_a, lat_b, scales]
    *parts, gain = call(
        lambda *refs: lat_back_kernel(len(pieces), *refs),
        "lat_back",
        [offsets, place],
        [*arrays, *pieces],
        [whole(a.shape) for a in arrays] + [pl.BlockSpec(memory_space=pltpu.HBM)] * len(pieces),
        [whole(half) for half in halves] + [whole((1, features))],
        [jax.ShapeDtypeStruct(half, low) for half in halves] + [jax.ShapeDtypeStruct((1, features), full)],
        [pltpu.VMEM((features, cols), low), pltpu.SemaphoreType.DMA((offsets.shape[0],))],
        (1,),
        2 * rows * features * (cols + kv.shape[1]),
    )
    return parts, gain


BLOCK = 256


def weight_grad(act, heads, blocks):
    rows, cols = heads.shape
    count = blocks.shape[0]

    def kernel(at, act_ref, heads_ref, out):
        out[0] = dot_tn(act_ref[...], heads_ref[...]).astype(low)

    return call(
        kernel,
        "weight_grad",
        [blocks],
        [act, heads],
        [pl.BlockSpec((rows, BLOCK), lambda i, at: (0, at[i])), whole(heads.shape)],
        [pl.BlockSpec((1, BLOCK, cols), lambda i, at: (i, 0, 0))],
        [jax.ShapeDtypeStruct((count, BLOCK, cols), low)],
        [],
        (count,),
        2 * rows * count * BLOCK * cols,
    )[0]


def kv_weight_grad_part(place, ctx_n, d_kv, lat_n, d_kv_lat, blocks):
    rows, cols = d_kv.shape
    count = blocks.shape[0]

    def kernel(at, here, ctx_ref, d_kv_ref, lat_ref, d_lat_ref, out, total):
        total[...] = dot_tn(ctx_ref[...], d_kv_ref[...])
        lat_part = dot_tn(lat_ref[...], d_lat_ref[...])
        first = here[0] * (cols // 2) + here[1] * HEAD_SIZE
        for k in range(2):
            at_k = pl.multiple_of(first + k * (cols // 4), HEAD_SIZE)
            span = pl.ds(at_k, HEAD_SIZE)
            total[:, span] += lat_part[:, k * HEAD_SIZE : (k + 1) * HEAD_SIZE]
        half = total.shape[0] // 2
        for k in range(2):
            at_x = pl.multiple_of((here[0] ^ k) * half, half)
            out[k, 0] = total[pl.ds(at_x, half), :].astype(low)

    block = pl.BlockSpec((rows, BLOCK), lambda i, at, here: (0, at[i]))
    return call(
        kernel,
        "kv_weight_grad",
        [blocks, place],
        [ctx_n, d_kv, lat_n, d_kv_lat],
        [block, whole(d_kv.shape), block, whole(d_kv_lat.shape)],
        [pl.BlockSpec((2, 1, BLOCK // 2, cols), lambda i, at, here: (0, i, 0, 0))],
        [jax.ShapeDtypeStruct((2, count, BLOCK // 2, cols), low)],
        [pltpu.VMEM((BLOCK, cols), full)],
        (count,),
        2 * rows * count * BLOCK * (cols + 2 * HEAD_SIZE),
    )[0]


NORM_ROWS = 64


def norm_rows(sources, gain):
    rows, features = sources[0].shape
    steps = rows // NORM_ROWS
    count = len(sources)

    def kernel(*refs):
        gain_ref, out, scale_out = refs[count:]
        for n in range(count):

            @pl.when(pl.program_id(0) == n)
            def _():
                values = refs[n][...].astype(full)
                scale_rows = lax.rsqrt(jnp.mean(values * values, axis=1, keepdims=True) + norm_eps)
                out[...] = (values * scale_rows * gain_ref[...]).astype(low)
                scale_out[...] = jnp.broadcast_to(scale_rows, scale_out.shape)

    def source_spec(n):
        return pl.BlockSpec(
            (NORM_ROWS, features), lambda s, i: (jnp.where(s == n, i, 0), 0)
        )

    return call(
        kernel,
        "norm_rows",
        [],
        [*sources, gain[None]],
        [source_spec(n) for n in range(count)] + [whole((1, features))],
        [
            pl.BlockSpec((NORM_ROWS, features), lambda s, i: (s * steps + i, 0)),
            pl.BlockSpec((NORM_ROWS, 128), lambda s, i: (s * steps + i, 0)),
        ],
        [
            jax.ShapeDtypeStruct((count * rows, features), low),
            jax.ShapeDtypeStruct((count * rows, 128), full),
        ],
        [],
        (count, steps),
        4 * count * rows * features,
        hint=1,
    )


def ctx_back(d_kv, full_kv, context, scales, gain):
    rows, cols = d_kv.shape
    features = full_kv.shape[0]
    step = 128

    def kernel(d_ref, kv_ref, ctx_ref, scale_ref, gain_ref, out, gain_out):
        @pl.when(pl.program_id(0) == 0)
        def _():
            gain_out[...] = jnp.zeros_like(gain_out)

        d = dot_nt(d_ref[...], kv_ref[...])
        scale_rows = scale_ref[:, :1]
        unit = ctx_ref[...].astype(full) * scale_rows
        weighted = d * unit
        gain_out[...] += jnp.sum(weighted, axis=0, keepdims=True)
        inner = jnp.mean(weighted * gain_ref[...], axis=1, keepdims=True)
        out[...] = scale_rows * (d * gain_ref[...] - unit * inner)

    return call(
        kernel,
        "ctx_back",
        [],
        [d_kv, full_kv, context, scales, gain[None]],
        [
            pl.BlockSpec((step, cols), lambda i: (i, 0)),
            whole(full_kv.shape),
            pl.BlockSpec((step, features), lambda i: (i, 0)),
            pl.BlockSpec((step, 128), lambda i: (i, 0)),
            whole((1, features)),
        ],
        [pl.BlockSpec((step, features), lambda i: (i, 0)), whole((1, features))],
        [jax.ShapeDtypeStruct((rows, features), full), jax.ShapeDtypeStruct((1, features), full)],
        [],
        (rows // step,),
        2 * rows * cols * features,
        hint=1,
    )


def after(value, *earlier):
    if not earlier:
        return value
    return lax.optimization_barrier((value, *earlier))[0]


class Place:
    def __init__(self):
        dp = lax.axis_size("dp")
        me = lax.axis_index("dp")
        self.dp = dp
        self.depth = dp // 4
        self.z = me // 4
        self.y = (me // 2) % 2
        self.c = me % 2
        self.x = lax.axis_index("tensor")
        self.scalars = jnp.stack([self.x, self.y]).astype(jnp.int32)
        self.perm_core = [(i, i ^ 1) for i in range(dp)]
        self.perm_y = [(i, i ^ 2) for i in range(dp)]
        self.perm_ring = [(i, (i + 4) % dp) for i in range(dp)]
        self.y_groups = [[i for i in range(dp) if (i // 2) % 2 == y] for y in range(2)]
        self.z_groups = [list(range(k, dp, 4)) for k in range(4)]
        self.manual = self.depth == 4

    def over_core(self, v):
        return lax.ppermute(v, "dp", self.perm_core)

    def over_y(self, v):
        return lax.ppermute(v, "dp", self.perm_y)

    def over_x(self, v):
        return lax.ppermute(v, "tensor", [(0, 1), (1, 0)])

    def ring(self, v, *earlier):
        return lax.ppermute(after(v, *earlier), "dp", self.perm_ring)

    def shift(self, v, r):
        return lax.ppermute(v, "dp", [(i, (i + 4 * r) % self.dp) for i in range(self.dp)])

    def row_blocks(self):
        return [
            (z * 2 + (self.y ^ y_other)) * 2 + c
            for z in range(self.depth)
            for c in range(2)
            for y_other in range(2)
        ]

    def block(self, r, y_other, c_other):
        z = (self.z - r) % self.depth
        return (z * 2 + (self.y ^ y_other)) * 2 + (self.c ^ c_other)


def ordered(at, mine, other, axis):
    first = jnp.where(at == 0, mine, other)
    second = jnp.where(at == 0, other, mine)
    return jnp.concatenate([first, second], axis=axis)


def pick(v, at, axis):
    return lax.dynamic_index_in_dim(v, at, axis, keepdims=False)


def add(a, b):
    return a.astype(full) + b.astype(full)


def group_cols(v, x):
    half = v.shape[1] // 2
    return lax.dynamic_slice_in_dim(v, x * half, half, 1)


def head_cols(v, y):
    keys = lax.dynamic_slice_in_dim(v, y * HEAD_SIZE, HEAD_SIZE, 1)
    values = lax.dynamic_slice_in_dim(v, (2 + y) * HEAD_SIZE, HEAD_SIZE, 1)
    return jnp.concatenate([keys, values], axis=1)


def join_heads(y, mine, other):
    first = jnp.where(y == 0, mine, other)
    second = jnp.where(y == 0, other, mine)
    return jnp.concatenate(
        [
            first[:, :HEAD_SIZE],
            second[:, :HEAD_SIZE],
            first[:, HEAD_SIZE:],
            second[:, HEAD_SIZE:],
        ],
        axis=1,
    )


class WeightBlock:
    def __init__(self, here, weight):
        self.here = here
        self.rows, cols = weight.shape
        half = cols // 2
        if not here.manual:
            held = lax.all_gather(weight, "dp", axis=0, tiled=True)
            self.from_y = lax.dynamic_slice_in_dim(held, here.y * half, half, 1)
            return
        mine = lax.dynamic_slice_in_dim(weight, here.y * half, half, 1)
        sent = lax.dynamic_slice_in_dim(weight, (1 - here.y) * half, half, 1)
        self.from_y = here.over_y(sent)
        self.block = jnp.concatenate([mine, self.from_y], axis=0)

    def result(self, *wait):
        here = self.here
        if not here.manual:
            return jnp.zeros((1,), jnp.int32), [self.from_y]
        held = lax.all_gather(
            after(self.block, *wait), "dp", axis=0, tiled=True, axis_index_groups=here.y_groups
        )
        offsets = [row * self.rows for row in here.row_blocks()]
        return jnp.stack(offsets).astype(jnp.int32), [held]


class GatherKv:
    def __init__(self, here, weight):
        self.here = here
        self.rows = weight.shape[0] // 2
        if here.manual:
            mine = lax.dynamic_slice_in_dim(weight, here.x * self.rows, self.rows, 0)
            self.first = [here.shift(mine, r) for r in (1, 3, 2)]
            self.held = jnp.concatenate([mine] + [self.first[k] for k in (0, 2, 1)], axis=0)
        else:
            self.held = lax.all_gather(weight, "dp", axis=0, tiled=True)
            self.first = [self.held]

    def over_y(self, *wait):
        if self.here.manual:
            from_y = self.here.over_y(after(self.held, *wait))
            self.near = jnp.concatenate([self.held, from_y], axis=0)
            return from_y
        return self.held

    def over_x(self, *wait):
        if self.here.manual:
            self.far = self.here.over_x(after(self.near, *wait))
            return self.far
        return self.held

    def result(self, *wait):
        here = self.here
        if not here.manual:
            return jnp.zeros((1,), jnp.int32), [self.held]
        pieces = [self.near, self.far]
        pieces += [here.over_core(self.near), here.over_core(after(self.far, *wait))]
        offsets = [
            here.block(r, y, c) * 2 * self.rows + (here.x ^ x) * self.rows
            for c in range(2)
            for x in range(2)
            for y in range(2)
            for r in range(4)
        ]
        return jnp.stack(offsets).astype(jnp.int32), pieces


def scatter_rows_of_y(here, act, heads):
    cols = heads.shape[1]
    features = act.shape[1]
    if here.manual:
        blocks = here.row_blocks()[::2]
        part = weight_grad(act, heads, jnp.stack(blocks).astype(jnp.int32))
    else:
        part = weight_grad(act, heads, jnp.arange(features // BLOCK, dtype=jnp.int32))
        part = pick(part.reshape(here.depth, 2, 2, -1, cols), here.y, 1)
    part = part.reshape(features // 2, cols)
    total = lax.psum_scatter(
        part, "dp", scatter_dimension=0, tiled=True, axis_index_groups=here.y_groups
    )
    return part, total.astype(full)


def scatter_weight(here, act, heads):
    cols = heads.shape[1]
    features = act.shape[1]
    if here.manual:
        part = weight_grad(act, heads, jnp.stack(here.row_blocks()).astype(jnp.int32))
    else:
        part = weight_grad(act, heads, jnp.arange(features // BLOCK, dtype=jnp.int32))
        part = part.reshape(here.depth, 2, 2, -1, cols)
        part = jnp.stack([pick(part, here.y, 1), pick(part, 1 - here.y, 1)], axis=2)
    part = part.reshape(features, cols)
    total = lax.psum_scatter(
        part, "dp", scatter_dimension=0, tiled=True, axis_index_groups=here.y_groups
    )

    def result(*wait):
        own, other = jnp.split(after(total, *wait), 2, axis=0)
        from_y = here.over_y(other)
        return ordered(here.y, own.astype(full), from_y.astype(full), 1), from_y

    return part, result


class ScatterKv:
    def __init__(self, here, ctx_n, d_kv, lat_n, d_kv_lat):
        self.here = here
        self.cols = d_kv.shape[1]
        self.args = (ctx_n, d_kv, lat_n, d_kv_lat)
        if not here.manual:
            every = jnp.arange(ctx_n.shape[1] // BLOCK, dtype=jnp.int32)
            part = kv_weight_grad_part(here.scalars, *self.args, every)
            part = ordered(here.x, part[0][:, None], part[1][:, None], 1)
            self.other_part = part.reshape(-1, self.cols)
            return
        self.other_part = self.part(d_kv, 1)
        self.received = here.over_core(self.other_part)

    def part(self, d_kv, c_other):
        here = self.here
        ctx_n, _, lat_n, d_kv_lat = self.args
        blocks = [here.block(r, y, c_other) for y in range(2) for r in range(here.depth)]
        blocks = jnp.stack(blocks).astype(jnp.int32)
        part = kv_weight_grad_part(here.scalars, ctx_n, d_kv, lat_n, d_kv_lat, blocks)
        return part.reshape(2, 2, here.depth, BLOCK // 2, self.cols)

    def own(self, *wait):
        self.own_part = self.other_part
        if self.here.manual:
            self.own_part = self.part(after(self.args[1], self.other_part, *wait), 0)

    def start(self, *wait):
        here = self.here
        if not here.manual:
            self.sent = self.first = self.last = [self.other_part]
            total = lax.psum_scatter(
                self.other_part, ("dp", "tensor"), scatter_dimension=0, tiled=True
            )
            self.total = total.astype(full)
            return
        mine, received = self.own_part, self.received
        half = self.cols // 2
        self.sent = [
            add(mine[:, 1, ..., :half], received[:, 1, ..., :half]).astype(low),
            add(mine[1, ..., half:], received[1, ..., half:]).astype(low),
        ]
        self.first = [
            here.over_y(after(self.sent[0], *wait)),
            here.over_x(after(self.sent[1], *wait)),
        ]
        self.halves = [
            add(mine[:, 0, ..., :half], received[:, 0, ..., :half]) + self.first[0],
            add(mine[0, ..., half:], received[0, ..., half:]) + self.first[1],
        ]

    def go_on(self, *wait):
        here = self.here
        if not here.manual:
            return
        a, b = self.halves
        self.last = [
            here.over_x(after(a[1].astype(low), *wait)),
            here.over_y(after(b[1].astype(low), *wait)),
        ]
        a, b = a[0] + self.last[0], b[0] + self.last[1]
        self.total = jnp.concatenate([a, b], axis=-1)

    def result(self, wait, *late):
        here, total = self.here, self.total
        if not here.manual:
            self.over_z = [total]
            return total
        held = [here.shift(after(total[r].astype(low), *wait), -r) for r in (1, 2, 3)]
        self.over_z = held
        return after(total[0], *late) + held[0] + held[1] + held[2]


class ScatterRows:
    def __init__(self, here, a_keep, a_sent, b_keep, b_sent, y_wait=(), x_wait=()):
        self.here = here
        self.keep = [a_keep, b_keep]
        self.first = [here.over_y(after(a_sent, *y_wait)), here.over_x(after(b_sent, *x_wait))]

    def prepare(self, *wait):
        here = self.here
        (a_keep, b_keep), (a, b) = self.keep, [after(v, *wait) for v in self.first]
        self.sent = [
            add(pick(a_keep, 1 - here.x, 0), pick(a, 1 - here.x, 0)).astype(low),
            add(b_keep[1], b[1]).astype(low),
        ]

    def finish(self, x_wait=(), y_wait=()):
        here = self.here
        self.last = [
            here.over_x(after(self.sent[0], *x_wait)),
            here.over_y(after(self.sent[1], *y_wait)),
        ]

    def result(self, *wait):
        here = self.here
        (a_keep, b_keep), (a, b) = self.keep, self.first
        a_last, b_last = [after(v, *wait) for v in self.last]
        a = add(pick(a_keep, here.x, 0), pick(a, here.x, 0)) + a_last
        b = add(b_keep[0], b[0]) + b_last
        return jnp.concatenate([a, b], axis=-1)


def gather_gains(here, part):
    if not here.manual:
        return part
    part = part.reshape(2, here.depth, 2, 2, 2, -1)
    part = pick(part, here.c, 3) + here.over_core(pick(part, 1 - here.c, 3))
    mine = [pick(part, (here.z - r) % here.depth, 1) for r in range(4)]
    return mine[0] + here.shift(mine[1], -1) + here.shift(mine[2], -2) + here.shift(mine[3], -3)


def scatter_gains(here, part):
    if not here.manual:
        devices = here.dp * 2
        part = part.reshape(2, devices, -1).swapaxes(0, 1)
        return lax.psum_scatter(part, ("dp", "tensor"), scatter_dimension=0)
    part = pick(part, here.x, 2) + here.over_x(pick(part, 1 - here.x, 2))
    return pick(part, here.y, 1) + here.over_y(pick(part, 1 - here.y, 1))


def norm_back(grad_rows, values, gain):
    scale_rows = lax.rsqrt(jnp.mean(values * values, axis=-1, keepdims=True) + norm_eps)
    unit_rows = values * scale_rows
    grad_unit = grad_rows * gain
    inner = jnp.mean(grad_unit * unit_rows, axis=-1, keepdims=True)
    return scale_rows * (grad_unit - unit_rows * inner)


def per_device(
    context, latents, lengths, ctx_gain, lat_gain, q_weight, key_value_weight, out_weight, out_grad
):
    here = Place()
    group_rows = latents.shape[0]
    my_rows = group_rows // 2
    features = context.shape[1]
    patch_rows = context.shape[0]

    kv = GatherKv(here, key_value_weight)
    lengths_y = here.over_y(lengths)
    q_block = WeightBlock(here, q_weight)
    out_block = WeightBlock(here, out_weight)
    full_q = q_block.result(*kv.first, lengths_y, out_block.from_y)
    first = [q_block.from_y, out_block.from_y, *kv.first]
    kv_from_y = kv.over_y(*first)
    grad_x = here.over_x(after(out_grad, *first))
    ctx_n, ctx_scales = norm_rows([after(context, *first)], ctx_gain)
    second = [kv_from_y, grad_x, ctx_n]
    kv_from_x = kv.over_x(*second)
    lat_other = here.over_y(after(latents, *second))
    full_kv = kv.result(lat_other)
    full_out = out_block.result(full_q[1][0], *full_kv[1][-2:], lat_other)
    both_lengths = jnp.concatenate([lengths, lengths_y], axis=0)
    ends = jnp.cumsum(both_lengths, axis=1)
    bounds = jnp.stack([(ends - both_lengths).reshape(-1), ends.reshape(-1)])

    kv_mine, kv_weight = rows_times_kv(ctx_n, full_kv)
    own_kv = head_cols(group_cols(kv_weight, here.x), here.y)
    kv_x = here.over_x(group_cols(kv_mine, 1 - here.x))
    grad_y_a = here.over_y(after(grad_x, lat_other, kv_from_x))
    lat_n, lat_scales = norm_rows([latents, after(lat_other, kv_mine, grad_y_a)], lat_gain)
    by_x = ordered(here.x, group_cols(kv_mine, here.x), kv_x, 0)
    kv_y = here.over_y(after(head_cols(by_x, 1 - here.y), lat_n, full_q[1][0]))
    kv_patch = jnp.stack([head_cols(by_x, here.y), kv_y])
    grad_y_b = here.over_y(after(out_grad, kv_y))

    kv_latent = jnp.dot(lat_n, own_kv, preferred_element_type=full).astype(low)
    queries = rows_times_weight(lat_n, full_q)

    mixed, lse = attend(bounds, queries, kv_patch, kv_latent)
    grad_all = jnp.stack([out_grad, grad_x, after(grad_y_b, mixed), after(grad_y_a, mixed)])
    grad_all = grad_all.reshape(2, 2, my_rows, features)
    grad_all = ordered(here.x, grad_all[:, :1], grad_all[:, 1:], 1)
    grad_all = grad_all.reshape(2 * group_rows, features)
    out_part, out_result = scatter_weight(here, grad_all, mixed)
    d_mixed = rows_times_weight(after(grad_all, out_part), full_out)
    d_queries, d_kv_patch, d_kv_latent = attend_back(
        bounds, queries, d_mixed, kv_patch, kv_latent, lse
    )
    d_group_y = here.over_y(d_kv_patch[1])
    branch_parts = heads_times_weight(here.scalars, after(mixed, d_queries), full_out)
    d_group = join_heads(here.y, d_kv_patch[0], d_group_y).reshape(2, patch_rows, -1)

    d_group_x = here.over_x(after(pick(d_group, 1 - here.x, 0), branch_parts[0]))
    d_kv_mine = ordered(here.x, pick(d_group, here.x, 0), d_group_x, 1)
    d_queries_y = here.over_y(after(d_queries, d_group_y, branch_parts[0]))
    lat_parts, lat_gain_part = lat_back(
        here.scalars, after(d_queries, d_group_y), full_q, d_kv_latent, own_kv,
        latents, lat_other, lat_scales,
    )
    kv_sum = ScatterKv(here, ctx_n, after(d_kv_mine, lat_parts[0]), lat_n, d_kv_latent)
    d_queries_y = jnp.concatenate([d_queries_y[group_rows:], d_queries_y[:group_rows]], axis=0)
    d_queries_all = ordered(here.y, d_queries, d_queries_y, 1)
    kv_sum.own()
    branch = ScatterRows(here, *branch_parts, [d_group_y], [d_group_y])
    q_part, q_weight_grad = scatter_rows_of_y(
        here, after(lat_n, kv_sum.own_part, *branch.first), d_queries_all
    )
    out_weight_grad, out_last = out_result(q_part)
    kv_sum.start(out_last)
    branch.prepare(*kv_sum.sent)
    branch.finish()
    context_grad, ctx_gain_part = ctx_back(
        after(d_kv_mine, *kv_sum.sent), kv_weight, context, ctx_scales, ctx_gain
    )
    gains = jnp.concatenate([after(ctx_gain_part, *kv_sum.first), lat_gain_part], axis=0)
    gains = gather_gains(here, gains)

    second = [*kv_sum.first, *branch.last, ctx_gain_part]
    lat_sum = ScatterRows(here, *lat_parts, second, second)
    kv_sum.go_on(*second)
    third = [*kv_sum.last, *lat_sum.first]
    kv_weight_grad = kv_sum.result(third, q_weight_grad)
    lat_sum.prepare()
    lat_sum.finish(third, third)
    gains = scatter_gains(here, after(gains, *third))
    lat_mine = lax.dynamic_slice_in_dim(latents, here.x * my_rows, my_rows, 0).astype(full)
    resampled = (lat_mine + branch.result()).astype(low)
    latents_grad = out_grad.astype(full) + norm_back(lat_sum.result(), lat_mine, lat_gain)
    return (
        resampled,
        context_grad,
        latents_grad,
        gains[0],
        gains[1],
        q_weight_grad,
        kv_weight_grad,
        out_weight_grad,
    )


def solution(mesh):
    in_specs = (
        P(("dp", "tensor"), None),
        P("dp", None),
        P("dp", None),
        P(),
        P(),
        P("dp", "tensor"),
        P("dp", None),
        P("dp", "tensor"),
        P(("dp", "tensor"), None),
    )
    out_specs = (
        P(("dp", "tensor"), None),
        P(("dp", "tensor"), None),
        P(("dp", "tensor"), None),
        P(("dp", "tensor")),
        P(("dp", "tensor")),
        P("dp", "tensor"),
        P(("dp", "tensor"), None),
        P("dp", "tensor"),
    )
    return jax.shard_map(
        per_device, mesh=mesh, in_specs=in_specs, out_specs=out_specs, check_vma=False
    )
```
